32 devices in a mesh: dp: 16 (over z, x, core), node: 2 (over y).
Axes of the slice: x: 2, y: 2, z: 4, core: 2. Of those that a mesh axis runs over, the one named last changes fastest.
Arguments:
- tokens: bfloat16 [384, 5120], P('node'), may hold values from -6 to 6
- cotangent: bfloat16 [384, 5120], P('node'), may hold values from -6 to 6
- gate_codes: bfloat16 [5120, 8192], P('node', 'dp'), may hold values from -4 to 4
- up_codes: bfloat16 [5120, 8192], P('node', 'dp'), may hold values from -4 to 4
- down_codes: bfloat16 [8192, 5120], P('dp', 'node'), may hold values from -4 to 4
- gate_scales: float32 [40, 8192], P(None, 'dp'), may hold values from 0.00559017 to 0.034938563
- up_scales: float32 [40, 8192], P(None, 'dp'), may hold values from 0.00559017 to 0.034938563
- down_scales: float32 [8192, 40], P('dp'), may hold values from 0.0044194176 to 0.027621359
Outputs:
- token_grad: bfloat16 [384, 5120], P('node', 'dp')
- gate_grad: bfloat16 [5120, 8192], P('node', 'dp')
- up_grad: bfloat16 [5120, 8192], P('node', 'dp')
- down_grad: bfloat16 [8192, 5120], P('dp', 'node')
The draws below stay inside these ranges and needn't reach their ends.
All inputs are finite; a program needn't handle non-finite values.
Results may differ from the reference program's by a relative error of at most 0.0077.
Values may be sent and summed in bfloat16 or wider, within the bound.
No kernel may reach another device: no remote copies, remote signals or barrier semaphores. Data moves between devices by JAX's collectives and lax.ppermute only.
A program may use at most 128 MiB of HBM per device.

```python
import math
import jax
import jax.numpy as jnp
from jax import lax

D = 5120
FF = 8192
QB = 128
TOK_DEV = 192
TOKENS = 384
N_NODE = 2


def with_spikes(result, key, source, target, blocks, factor):
    owner, partner = [(jnp.arange(result.shape[dim]) // (result.shape[dim] // blocks)).reshape([-1 if axis == dim else 1 for axis in range(result.ndim)]) for dim in (source, target)]
    chosen = jax.random.permutation(key, blocks)[partner]
    strong = (owner == chosen) | (owner == (partner + blocks // 2) % blocks)
    return jnp.where(strong, factor * result, result)


def level_of(rng, dims, pieces, low, largest):
    level = 1.0
    for position, blocks in pieces:
        heights = jax.random.uniform(jax.random.fold_in(jax.random.fold_in(rng, 6), position), (blocks,), jnp.float32, low / len(pieces), largest / len(pieces))
        level = level * jnp.repeat(jnp.exp(heights), dims[position] // blocks).reshape((-1,) + (1,) * (len(dims) - 1 - position))
    return level


def scatter_about(stream_key, shape, spread, most, split=(), kind=jnp.bfloat16):
    array = jax.random.normal(stream_key, shape, jnp.float32) * spread
    if len(split) > 0:
        array = level_of(stream_key, shape, split, -0.22, 0.18) * array
    return jnp.clip(array, min=-most, max=most).astype(kind)


def bell_draw_with(key, extent, deviation, bound, pieces, heavy, kind=jnp.bfloat16):
    values = deviation * jax.random.normal(key, extent, jnp.float32)
    if pieces:
        values = values * level_of(key, extent, pieces, -0.22, 0.18)
    return jnp.clip(with_spikes(values, jax.random.fold_in(key, 3), *heavy), -bound, bound).astype(kind)


def setup_inputs(seed: int = 0) -> dict:
    streams_of = jax.random.split(jax.random.key(seed), 9)
    return {
        "tokens": bell_draw_with(streams_of[0], (TOKENS, D), 1.0, 6.0, ((0, 2),), (0, 1, 2, 2.0)),
        "cotangent": bell_draw_with(streams_of[1], (TOKENS, D), 1.0, 6.0, ((0, 2),), (0, 1, 2, 2.0)),
        "gate_codes": bell_draw_with(streams_of[2], (D, FF), 1.0, 4.0, ((0, 2), (1, 16)), (1, 0, 16, 2.0)),
        "up_codes": bell_draw_with(streams_of[3], (D, FF), 1.0, 4.0, ((0, 2), (1, 16)), (1, 0, 16, 2.0)),
        "down_codes": scatter_about(streams_of[4], (FF, D), 1.0, 4.0, ((0, 16), (1, 2))),
        "gate_scales": jnp.clip(jnp.exp(math.log(0.034938563) - 1.8325814 * jax.random.uniform(streams_of[5], (D // QB, FF), jnp.float32) ** level_of(streams_of[5], (D // QB, FF), ((1, 16),), -0.2, 0.2)), 0.00559017, 0.034938563),
        "up_scales": jnp.clip(jnp.exp(math.log(0.034938563) - 1.8325814 * jax.random.uniform(streams_of[6], (D // QB, FF), jnp.float32) ** level_of(streams_of[6], (D // QB, FF), ((1, 16),), -0.2, 0.2)), 0.00559017, 0.034938563),
        "down_scales": jnp.clip(jnp.exp(math.log(0.027621359) - 1.8325814 * jax.random.uniform(streams_of[7], (FF, D // QB), jnp.float32) ** level_of(streams_of[7], (FF, D // QB), ((0, 16),), -0.2, 0.2)), 0.0044194176, 0.027621359),
    }


def scale_rows(codes, scales):
    blocks = codes.astype(jnp.float32).reshape(scales.shape[0], QB, codes.shape[1])
    return (blocks * scales[:, None, :]).reshape(codes.shape).astype(jnp.bfloat16)


def contract(left, right):
    return lax.dot_general(left, right, (((0,), (0,)), ((), ())), preferred_element_type=jnp.float32)


def against(left, right):
    return lax.dot_general(left, right, (((1,), (1,)), ((), ())), preferred_element_type=jnp.float32)


def reference(tokens, cotangent, gate_codes, up_codes, down_codes, gate_scales, up_scales, down_scales):
    w_gate = scale_rows(gate_codes, gate_scales)
    w_up = scale_rows(up_codes, up_scales)
    w_down_t = scale_rows(down_codes.T, down_scales.T)
    gate = jnp.dot(tokens, w_gate, preferred_element_type=jnp.float32)
    upper = jnp.dot(tokens, w_up, preferred_element_type=jnp.float32)
    sig = jax.nn.sigmoid(gate)
    silu_val = gate * sig
    act = (silu_val * upper).astype(jnp.bfloat16)
    d_act = jnp.dot(cotangent, w_down_t, preferred_element_type=jnp.float32)
    d_gate = (d_act * upper * sig * (1.0 + gate * (1.0 - sig))).astype(jnp.bfloat16)
    d_up = (d_act * silu_val).astype(jnp.bfloat16)
    token_grad = (against(d_gate, w_gate) + against(d_up, w_up)).astype(jnp.bfloat16)
    tok_groups = tokens.reshape(N_NODE, TOK_DEV, D)
    cot_groups = cotangent.reshape(N_NODE, TOK_DEV, D)
    act_groups = act.reshape(N_NODE, TOK_DEV, FF)
    dg_groups = d_gate.reshape(N_NODE, TOK_DEV, FF)
    du_groups = d_up.reshape(N_NODE, TOK_DEV, FF)
    zero = jnp.zeros((D, FF), jnp.float32)

    def node_step(carry, items):
        rows, grad_rows, act_rows, dg_rows, du_rows = items
        parts = (contract(rows, dg_rows), contract(rows, du_rows), contract(grad_rows, act_rows))
        return tuple(c + p.astype(jnp.bfloat16).astype(jnp.float32) for c, p in zip(carry, parts)), None

    totals, unused = lax.scan(node_step, (zero, zero, zero), (tok_groups, cot_groups, act_groups, dg_groups, du_groups))
    gate_grad = totals[0].astype(jnp.bfloat16)
    up_grad = totals[1].astype(jnp.bfloat16)
    down_grad = totals[2].T.astype(jnp.bfloat16)
    return token_grad, gate_grad, up_grad, down_grad
```

```python
import functools

import jax
import jax.numpy as jnp
from jax import lax
from jax.experimental import pallas as pl
from jax.experimental.pallas import tpu as pltpu
from jax.sharding import PartitionSpec as P

QB = 128
STEP = 640
SIDE_BIT = 2
IN_HBM = pl.BlockSpec(memory_space=pltpu.HBM)
IN_VMEM = pl.BlockSpec(memory_space=pltpu.VMEM)
IN_SMEM = pl.BlockSpec(memory_space=pltpu.SMEM)


def contract(left, right):
    return lax.dot_general(
        left, right, (((0,), (0,)), ((), ())), preferred_element_type=jnp.float32
    )


def against(left, right):
    return lax.dot_general(
        left, right, (((1,), (1,)), ((), ())), preferred_element_type=jnp.float32
    )


def flipped(size, mask):
    return [(i, i ^ mask) for i in range(size)]


def swap(value, axis, size, mask):
    return lax.ppermute(value, axis, flipped(size, mask))


def in_hbm(array):
    return pltpu.with_memory_space_constraint(array, pltpu.HBM)


def in_vmem(array):
    return pltpu.with_memory_space_constraint(array, pltpu.VMEM)


def cost(operations):
    return pl.CostEstimate(flops=operations, transcendentals=0, bytes_accessed=0)


def grant(mebibytes):
    return pltpu.CompilerParams(vmem_limit_bytes=mebibytes * 1024 * 1024)


def side_of(place):
    return (place >> SIDE_BIT) & 1


def fetch_kernel(mask, node, place, tokens, cot, target, sem):
    half, rows = target.shape
    start = pl.multiple_of(side_of(place[0]) * half, 16)
    column = pl.multiple_of((node[0] ^ mask) * rows, 128)
    part = (pl.ds(start, half), pl.ds(column, rows))

    @pl.when((place[0] & 1) == 0)
    def _():
        copy = pltpu.make_async_copy(tokens.at[part], target, sem)
        copy.start()
        copy.wait()

    @pl.when((place[0] & 1) == 1)
    def _():
        copy = pltpu.make_async_copy(cot.at[part], target, sem)
        copy.start()
        copy.wait()


def fetch(mask, node, place, tokens, cot, shape):
    return pl.pallas_call(
        functools.partial(fetch_kernel, mask),
        in_specs=[IN_SMEM, IN_SMEM, IN_HBM, IN_HBM],
        out_specs=IN_VMEM,
        out_shape=pltpu.VMEM(shape, tokens.dtype),
        scratch_shapes=[pltpu.SemaphoreType.DMA],
        compiler_params=grant(4),
        cost_estimate=cost(0),
        name="fetch",
    )(node, place, in_hbm(tokens), in_hbm(cot))


def prepare_kernel(
    node, tokens, cot, gate_codes, up_codes, down_codes, gate_scales, up_scales, down_scales,
    own_tokens, own_cot, w_in, w_down, total, short, gate_held, up_held, down_held, sems,
):
    rows, units = gate_codes.shape
    steps, per_step = rows // STEP, STEP // QB
    own = slice(0, tokens.shape[0])

    def copies(step):
        column = pl.multiple_of(node[0] * rows + step * STEP, 128)
        part = pl.ds(pl.multiple_of(step * STEP, 128), STEP)
        pairs = (
            (gate_codes.at[part, :], gate_held.at[part, :]),
            (up_codes.at[part, :], up_held.at[part, :]),
            (tokens.at[:, pl.ds(column, STEP)], own_tokens.at[own, part]),
            (down_codes.at[:, part], down_held.at[:, part]),
            (cot.at[:, pl.ds(column, STEP)], own_cot.at[own, part]),
        )
        return [pltpu.make_async_copy(a, b, sems.at[step, i]) for i, (a, b) in enumerate(pairs)]

    for step in range(steps):
        for copy in copies(step):
            copy.start()
    total[...] = jnp.zeros(total.shape, total.dtype)

    def one(step, carry):
        for copy in copies(step):
            copy.wait()
        first_scale = (node[0] * steps + step) * per_step
        for j in range(per_step):
            part = pl.ds(pl.multiple_of(step * STEP + j * QB, QB), QB)
            scale = pl.ds(first_scale + j, 1)
            w_in[part, :units] = (gate_held[part, :].astype(jnp.float32) * gate_scales[scale, :]).astype(w_in.dtype)
            w_in[part, units:] = (up_held[part, :].astype(jnp.float32) * up_scales[scale, :]).astype(w_in.dtype)
            w_down[:, part] = (
                down_held[:, part].astype(jnp.float32) * down_scales[step, :, j : j + 1]
            ).astype(w_down.dtype)
        part = pl.ds(pl.multiple_of(step * STEP, 128), STEP)
        total[:, : 2 * units] += jnp.dot(own_tokens[own, part], w_in[part, :], preferred_element_type=jnp.float32)
        total[:, 2 * units :] += against(own_cot[own, part], w_down[:, part])
        return carry

    lax.fori_loop(0, steps, one, 0)
    short[...] = total[...].astype(short.dtype)


def prepare(nodes, node, tokens, cot, gate_codes, up_codes, down_codes, gate_scales, up_scales, down_scales):
    rows, units = gate_codes.shape
    count = tokens.shape[0]
    steps, per_step = rows // STEP, STEP // QB
    scales = lax.dynamic_slice_in_dim(down_scales, node[0] * (rows // QB), rows // QB, 1)
    scales = scales.reshape(units, steps, per_step).transpose(1, 0, 2)
    codes = jnp.bfloat16
    return pl.pallas_call(
        prepare_kernel,
        in_specs=[IN_SMEM] + [IN_HBM] * 5 + [IN_VMEM] * 3,
        out_specs=[IN_VMEM] * 6,
        out_shape=[
            pltpu.VMEM((nodes * count, rows), codes),
            pltpu.VMEM((nodes * count, rows), codes),
            pltpu.VMEM((rows, 2 * units), codes),
            pltpu.VMEM((units, rows), codes),
            pltpu.VMEM((count, 3 * units), jnp.float32),
            pltpu.VMEM((count, 3 * units), codes),
        ],
        scratch_shapes=[
            pltpu.VMEM((rows, units), codes),
            pltpu.VMEM((rows, units), codes),
            pltpu.VMEM((units, rows), codes),
            pltpu.SemaphoreType.DMA((steps, 5)),
        ],
        compiler_params=grant(16),
        cost_estimate=cost(0),
        name="prepare",
    )(
        node, *(in_hbm(a) for a in (tokens, cot, gate_codes, up_codes, down_codes)),
        gate_scales, up_scales, scales,
    )


def reorder_kernel(blocks, place, source, target):
    rows = target.shape[0] // blocks
    bits = blocks.bit_length() - 1
    for i in range(blocks):
        block = 0
        for bit in range(bits):
            own = (place[0] >> bit) & 1
            block += (own if (i >> (bits - 1 - bit)) & 1 else 1 - own) << bit
        target[i * rows : (i + 1) * rows, :] = source[pl.ds(pl.multiple_of(block * rows, 16), rows), :]


def reorder(place, weights, blocks):
    return pl.pallas_call(
        functools.partial(reorder_kernel, blocks),
        in_specs=[IN_SMEM, IN_VMEM],
        out_specs=IN_VMEM,
        out_shape=pltpu.VMEM(weights.shape, weights.dtype),
        compiler_params=grant(4),
        cost_estimate=cost(0),
        name="reorder",
    )(place, in_vmem(weights))


def join_kernel(group, far, place, held, given, w_in, w_down, *refs):
    tokens, cot, total, short = refs[-4:]
    half, rows = held.shape
    units = w_down.shape[0]
    side = side_of(place[0])
    natural = (1 - side if far else side) * half
    mine = pl.ds(pl.multiple_of(2 * group * half + natural, 16), half)
    out = pl.ds(pl.multiple_of(natural, 16), half)

    @pl.when((place[0] & 1) == 0)
    def _():
        tokens[mine, :] = held[...]
        cot[mine, :] = given[...]

    @pl.when((place[0] & 1) == 1)
    def _():
        tokens[mine, :] = given[...]
        cot[mine, :] = held[...]

    for step in range(rows // STEP):
        part = slice(step * STEP, (step + 1) * STEP)
        inner = jnp.dot(tokens[mine, part], w_in[part, :], preferred_element_type=jnp.float32)
        outer = against(cot[mine, part], w_down[:, part])
        if step == 0:
            total[out, : 2 * units] = inner
            total[out, 2 * units :] = outer
        else:
            total[out, : 2 * units] += inner
            total[out, 2 * units :] += outer
    short[...] = total[out, :].astype(short.dtype)


def join(group, far, place, held, given, w_in, w_down, before):
    half, rows = held.shape
    units = w_down.shape[0]
    return pl.pallas_call(
        functools.partial(join_kernel, group, far),
        in_specs=[IN_SMEM] + [IN_VMEM] * (4 + len(before)),
        out_specs=[IN_VMEM] * 4,
        out_shape=[
            pltpu.VMEM(before[0].shape, jnp.bfloat16),
            pltpu.VMEM(before[1].shape, jnp.bfloat16),
            pltpu.VMEM((2 * half, 3 * units), jnp.float32),
            pltpu.VMEM((half, 3 * units), jnp.bfloat16),
        ],
        input_output_aliases={5 + i: i for i in range(len(before))},
        compiler_params=grant(8),
        cost_estimate=cost(0),
        name="join",
    )(place, *(in_vmem(a) for a in (held, given, w_in, w_down, *before)))


def activate_kernel(group, turns, count, place, weights, total, arrived, *refs):
    act, d_inner, *targets = refs[-6:]
    units, half, chunk = act.shape[1], count // 2, 32
    side = side_of(place[0])
    width = targets[0].shape[1]

    def rows(first, length):
        return pl.ds(pl.multiple_of(first, 16), length)

    for turn in turns:
        natural = (1 - side if turn else side) * half
        for start in range(0, half, chunk):
            def of(array):
                return rows((natural if array.shape[0] == count else 0) + start, chunk)

            sums = total[of(total), :] + arrived[of(arrived), :].astype(jnp.float32)
            gate, upper, d_act = sums[:, :units], sums[:, units : 2 * units], sums[:, 2 * units :]
            sig = jax.nn.sigmoid(gate)
            silu_val = gate * sig
            kept = rows(group * count + natural + start, chunk)
            act[kept, :] = (silu_val * upper).astype(act.dtype)
            d_inner[kept, :units] = (d_act * upper * sig * (1.0 + gate * (1.0 - sig))).astype(d_inner.dtype)
            d_inner[kept, units:] = (d_act * silu_val).astype(d_inner.dtype)
    if len(turns) == 2:
        mine, out = rows(group * count, count), rows(0, count)
    else:
        mine, out = rows(group * count + natural, half), rows(natural, half)
    for i, target in enumerate(targets):
        product = against(d_inner[mine, :], weights[i * width : (i + 1) * width, :])
        target[out, :] = product.astype(target.dtype)


def activate(group, groups, turns, place, total, arrived, weights, before):
    units = weights.shape[1] // 2
    count = arrived.shape[0] * (3 - len(turns))
    terms = count, weights.shape[0] // 4
    return pl.pallas_call(
        functools.partial(activate_kernel, group, turns, count),
        in_specs=[IN_SMEM] + [IN_VMEM] * (3 + len(before)),
        out_specs=[IN_VMEM] * 6,
        out_shape=[
            pltpu.VMEM((groups * count, units), jnp.bfloat16),
            pltpu.VMEM((groups * count, 2 * units), jnp.bfloat16),
            pltpu.VMEM(terms, jnp.bfloat16),
            pltpu.VMEM(terms, jnp.bfloat16),
            pltpu.VMEM(terms, jnp.float32),
            pltpu.VMEM(terms, jnp.float32),
        ],
        input_output_aliases={4 + i: i for i in range(len(before))},
        compiler_params=grant(12),
        cost_estimate=cost(0),
        name="activate",
    )(place, *(in_vmem(a) for a in (weights, total, arrived, *before)))


def grads_kernel(tokens, cot, act, d_inner, gate_grad, up_grad, down_grad, gate_held, up_held, down_held, sems):
    rows, units = gate_grad.shape
    copies = []

    def send(held, target, part, i):
        copies.append(pltpu.make_async_copy(held.at[part], target.at[part], sems.at[i]))
        copies[-1].start()

    steps = rows // STEP
    for step in range(steps):
        part = slice(step * STEP, (step + 1) * STEP)
        both = contract(tokens[:, part], d_inner[...])
        gate_held[part, :] = both[:, :units].astype(gate_held.dtype)
        send(gate_held, gate_grad, (part, slice(None)), step)
        up_held[part, :] = both[:, units:].astype(up_held.dtype)
        send(up_held, up_grad, (part, slice(None)), steps + step)
    for step in range(steps):
        part = slice(step * STEP, (step + 1) * STEP)
        down_held[:, part] = contract(act[...], cot[:, part]).astype(down_held.dtype)
        send(down_held, down_grad, (slice(None), part), 2 * steps + step)
    for copy in copies:
        copy.wait()


def weight_grads(tokens, cot, act, d_inner):
    rows, units = tokens.shape[1], act.shape[1]
    shapes = [(rows, units), (rows, units), (units, rows)]
    return pl.pallas_call(
        grads_kernel,
        in_specs=[IN_VMEM] * 4,
        out_specs=[IN_HBM] * 3,
        out_shape=[pltpu.HBM(shape, jnp.bfloat16) for shape in shapes],
        scratch_shapes=[pltpu.VMEM(shape, jnp.bfloat16) for shape in shapes]
        + [pltpu.SemaphoreType.DMA((3 * (rows // STEP),))],
        compiler_params=grant(20),
        cost_estimate=cost(6 * tokens.shape[0] * rows * units),
        name="weight_grads",
    )(*(in_vmem(a) for a in (tokens, cot, act, d_inner)))


def after(value, *earlier):
    return lax.optimization_barrier((value, earlier))[0]


def body(tokens, cotangent, gate_codes, up_codes, down_codes, gate_scales, up_scales, down_scales):
    nodes, width = lax.axis_size("node"), lax.axis_size("dp")
    node, place = lax.axis_index("node"), lax.axis_index("dp")
    node_ref, place_ref = node.reshape(1), place.reshape(1)
    rows, units = gate_codes.shape
    count = tokens.shape[0]
    owners = width // nodes
    bits = owners.bit_length() - 1

    side, half = side_of(place), count // 2

    def halves(array):
        return [lax.dynamic_slice_in_dim(array, s * half, half, 0) for s in (side, 1 - side)]

    fetched = [
        swap(fetch(k, node_ref, place_ref, tokens, cotangent, (half, rows)), "node", nodes, k)
        for k in range(1, nodes)
    ]
    all_tokens, all_cots, w_in, w_down, own_sums, own_short = prepare(
        nodes, node_ref, tokens, cotangent, gate_codes, up_codes, down_codes, gate_scales, up_scales, down_scales
    )
    fetched = after(fetched, own_short)
    w_relative = reorder(place_ref, w_in, owners)
    fetched = after(fetched, w_relative)

    sums, shorts = [own_sums], [None]
    for k, mine in enumerate(fetched, 1):
        given = swap(mine, "dp", width, 1)
        beside = swap(mine, "dp", width, 1 << SIDE_BIT)
        before, near_far = [all_tokens, all_cots], []
        for far, held in enumerate((mine, beside)):
            if far:
                given = swap(held, "dp", width, 1)
            *before, short = join(k, far, place_ref, held, given, w_in, w_down, before)
            near_far.append(short)
        all_tokens, all_cots, total = before
        sums.append(total)
        shorts.append(near_far)

    mask = 1
    if nodes > 2:
        while mask < nodes // 2:
            sent = [swap(s.astype(jnp.bfloat16), "node", nodes, mask) for s in sums]
            sums = [s + sent[k ^ mask].astype(jnp.float32) for k, s in enumerate(sums)]
            mask *= 2
        own_short = sums[0].astype(jnp.bfloat16)
        shorts = [halves(s.astype(jnp.bfloat16)) for s in sums]
    near_far = [swap(s, "node", nodes, mask) for s in shorts[mask]]
    arrived = [None]
    for k in range(1, nodes):
        short = own_short if k == mask else sums[k ^ mask].astype(jnp.bfloat16)
        arrived.append(swap(short, "node", nodes, mask))

    def pair(parts):
        got = [swap(part, "dp", width, 1).astype(jnp.float32) for part in parts[:2]]
        return (parts[2] + got[0]).astype(jnp.bfloat16), parts[3] + got[1]

    def cut(terms, got):
        edge = terms.shape[1] // 2
        sending = (terms[:, :edge] + got[:, :edge].astype(jnp.float32)).astype(jnp.bfloat16)
        return sending, terms[:, edge:] + got[:, edge:].astype(jnp.float32)

    blocks, before = [None] * nodes, []
    for k in reversed(range(1, nodes)):
        *before, a, b, c, d = activate(k, nodes, (0, 1), place_ref, sums[k], arrived[k], w_relative, before)
        x_sent, terms = pair((a, b, c, d))
        last = x_sent
        got = swap(x_sent, "dp", width, 2)
        for bit in range(2, bits):
            last, terms = cut(terms, got)
            got = swap(last, "dp", width, 1 << bit)
        blocks[k] = terms, got

    before = activate(0, nodes, (0,), place_ref, sums[0], near_far[0], w_relative, before)
    act, d_inner, *parts = activate(0, nodes, (1,), place_ref, sums[0], after(near_far[1], x_sent), w_relative, before)
    sending, terms = pair(parts)
    got = swap(sending, "dp", width, 2)
    for k in range(1, nodes):
        block = (blocks[k][0] + blocks[k][1].astype(jnp.float32)).astype(jnp.bfloat16)
        act, sending, block = lax.optimization_barrier((act, sending, block))
        blocks[k] = swap(block, "node", nodes, k).astype(jnp.float32)
    act, d_inner = after((act, d_inner), sending)
    gate_grad, up_grad, down_grad = weight_grads(all_tokens, all_cots, act, d_inner)
    got = after(got, gate_grad, up_grad, down_grad)
    for bit in range(2, bits):
        sending, terms = cut(terms, got)
        got = swap(sending, "dp", width, 1 << bit)
    blocks[0] = terms + got.astype(jnp.float32)
    high = place // owners

    def block_for(owner):
        chosen = blocks[0]
        for k in range(1, nodes):
            chosen = jnp.where((owner ^ node) == k, blocks[k], chosen)
        return chosen

    token_grad = block_for(high)
    for j in range(1, nodes):
        token_grad += swap(block_for(high ^ j).astype(jnp.bfloat16), "dp", width, j * owners).astype(jnp.float32)
    return token_grad.astype(jnp.bfloat16), gate_grad, up_grad, down_grad


def solution(mesh):
    return jax.shard_map(
        body,
        mesh=mesh,
        in_specs=(
            P("node", None),
            P("node", None),
            P("node", "dp"),
            P("node", "dp"),
            P("dp", "node"),
            P(None, "dp"),
            P(None, "dp"),
            P("dp", None),
        ),
        out_specs=(P("node", "dp"), P("node", "dp"), P("node", "dp"), P("dp", "node")),
        check_vma=False,
    )
```

```python
import functools

import jax
import jax.numpy as jnp
from jax import lax
from jax.experimental import pallas as pl
from jax.experimental.pallas import tpu as pltpu
from jax.sharding import PartitionSpec as P

QB = 128
STEP = 640
SIDE_BIT = 2
IN_HBM = pl.BlockSpec(memory_space=pltpu.HBM)
IN_VMEM = pl.BlockSpec(memory_space=pltpu.VMEM)
IN_SMEM = pl.BlockSpec(memory_space=pltpu.SMEM)


def contract(left, right):
    return lax.dot_general(
        left, right, (((0,), (0,)), ((), ())), preferred_element_type=jnp.float32
    )


def against(left, right):
    return lax.dot_general(
        left, right, (((1,), (1,)), ((), ())), preferred_element_type=jnp.float32
    )


def flipped(size, mask):
    return [(i, i ^ mask) for i in range(size)]


def swap(value, axis, size, mask):
    return lax.ppermute(value, axis, flipped(size, mask))


def in_hbm(array):
    return pltpu.with_memory_space_constraint(array, pltpu.HBM)


def in_vmem(array):
    return pltpu.with_memory_space_constraint(array, pltpu.VMEM)


def cost(operations):
    return pl.CostEstimate(flops=operations, transcendentals=0, bytes_accessed=0)


def grant(mebibytes):
    return pltpu.CompilerParams(vmem_limit_bytes=mebibytes * 1024 * 1024)


def side_of(place):
    return (place >> SIDE_BIT) & 1


def fetch_kernel(mask, node, place, tokens, cot, target, sem):
    half, rows = target.shape
    start = pl.multiple_of(side_of(place[0]) * half, 16)
    column = pl.multiple_of((node[0] ^ mask) * rows, 128)
    part = (pl.ds(start, half), pl.ds(column, rows))

    @pl.when((place[0] & 1) == 0)
    def _():
        copy = pltpu.make_async_copy(tokens.at[part], target, sem)
        copy.start()
        copy.wait()

    @pl.when((place[0] & 1) == 1)
    def _():
        copy = pltpu.make_async_copy(cot.at[part], target, sem)
        copy.start()
        copy.wait()


def fetch(mask, node, place, tokens, cot, shape):
    return pl.pallas_call(
        functools.partial(fetch_kernel, mask),
        in_specs=[IN_SMEM, IN_SMEM, IN_HBM, IN_HBM],
        out_specs=IN_VMEM,
        out_shape=pltpu.VMEM(shape, tokens.dtype),
        scratch_shapes=[pltpu.SemaphoreType.DMA],
        compiler_params=grant(4),
        cost_estimate=cost(0),
        name="fetch",
    )(node, place, in_hbm(tokens), in_hbm(cot))


def prepare_kernel(
    node, tokens, cot, gate_codes, up_codes, down_codes, gate_scales, up_scales, down_scales,
    own_tokens, own_cot, w_in, w_down, total, short, gate_held, up_held, down_held, sems,
):
    rows, units = gate_codes.shape
    steps, per_step = rows // STEP, STEP // QB
    own = slice(0, tokens.shape[0])

    def copies(step):
        column = pl.multiple_of(node[0] * rows + step * STEP, 128)
        part = pl.ds(pl.multiple_of(step * STEP, 128), STEP)
        pairs = (
            (gate_codes.at[part, :], gate_held.at[part, :]),
            (up_codes.at[part, :], up_held.at[part, :]),
            (tokens.at[:, pl.ds(column, STEP)], own_tokens.at[own, part]),
            (down_codes.at[:, part], down_held.at[:, part]),
            (cot.at[:, pl.ds(column, STEP)], own_cot.at[own, part]),
        )
        return [pltpu.make_async_copy(a, b, sems.at[step, i]) for i, (a, b) in enumerate(pairs)]

    for step in range(steps):
        for copy in copies(step):
            copy.start()
    total[...] = jnp.zeros(total.shape, total.dtype)

    def one(step, carry):
        for copy in copies(step):
            copy.wait()
        first_scale = (node[0] * steps + step) * per_step
        for j in range(per_step):
            part = pl.ds(pl.multiple_of(step * STEP + j * QB, QB), QB)
            scale = pl.ds(first_scale + j, 1)
            w_in[part, :units] = (gate_held[part, :].astype(jnp.float32) * gate_scales[scale, :]).astype(w_in.dtype)
            w_in[part, units:] = (up_held[part, :].astype(jnp.float32) * up_scales[scale, :]).astype(w_in.dtype)
            w_down[:, part] = (
                down_held[:, part].astype(jnp.float32) * down_scales[step, :, j : j + 1]
            ).astype(w_down.dtype)
        part = pl.ds(pl.multiple_of(step * STEP, 128), STEP)
        total[:, : 2 * units] += jnp.dot(own_tokens[own, part], w_in[part, :], preferred_element_type=jnp.float32)
        total[:, 2 * units :] += against(own_cot[own, part], w_down[:, part])
        return carry

    lax.fori_loop(0, steps, one, 0)
    short[...] = total[...].astype(short.dtype)


def prepare(nodes, node, tokens, cot, gate_codes, up_codes, down_codes, gate_scales, up_scales, down_scales):
    rows, units = gate_codes.shape
    count = tokens.shape[0]
    steps, per_step = rows // STEP, STEP // QB
    scales = lax.dynamic_slice_in_dim(down_scales, node[0] * (rows // QB), rows // QB, 1)
    scales = scales.reshape(units, steps, per_step).transpose(1, 0, 2)
    codes = jnp.bfloat16
    return pl.pallas_call(
        prepare_kernel,
        in_specs=[IN_SMEM] + [IN_HBM] * 5 + [IN_VMEM] * 3,
        out_specs=[IN_VMEM] * 6,
        out_shape=[
            pltpu.VMEM((nodes * count, rows), codes),
            pltpu.VMEM((nodes * count, rows), codes),
            pltpu.VMEM((rows, 2 * units), codes),
            pltpu.VMEM((units, rows), codes),
            pltpu.VMEM((count, 3 * units), jnp.float32),
            pltpu.VMEM((count, 3 * units), codes),
        ],
        scratch_shapes=[
            pltpu.VMEM((rows, units), codes),
            pltpu.VMEM((rows, units), codes),
            pltpu.VMEM((units, rows), codes),
            pltpu.SemaphoreType.DMA((steps, 5)),
        ],
        compiler_params=grant(16),
        cost_estimate=cost(0),
        name="prepare",
    )(
        node, *(in_hbm(a) for a in (tokens, cot, gate_codes, up_codes, down_codes)),
        gate_scales, up_scales, scales,
    )


def reorder_kernel(blocks, place, source, target):
    rows = target.shape[0] // blocks
    bits = blocks.bit_length() - 1
    for i in range(blocks):
        block = 0
        for bit in range(bits):
            own = (place[0] >> bit) & 1
            block += (own if (i >> (bits - 1 - bit)) & 1 else 1 - own) << bit
        target[i * rows : (i + 1) * rows, :] = source[pl.ds(pl.multiple_of(block * rows, 16), rows), :]


def reorder(place, weights, blocks):
    return pl.pallas_call(
        functools.partial(reorder_kernel, blocks),
        in_specs=[IN_SMEM, IN_VMEM],
        out_specs=IN_VMEM,
        out_shape=pltpu.VMEM(weights.shape, weights.dtype),
        compiler_params=grant(4),
        cost_estimate=cost(0),
        name="reorder",
    )(place, in_vmem(weights))


def join_kernel(group, far, place, held, given, w_in, w_down, *refs):
    tokens, cot, total, short = refs[-4:]
    half, rows = held.shape
    units = w_down.shape[0]
    side = side_of(place[0])
    natural = (1 - side if far else side) * half
    mine = pl.ds(pl.multiple_of(2 * group * half + natural, 16), half)
    out = pl.ds(pl.multiple_of(natural, 16), half)

    @pl.when((place[0] & 1) == 0)
    def _():
        tokens[mine, :] = held[...]
        cot[mine, :] = given[...]

    @pl.when((place[0] & 1) == 1)
    def _():
        tokens[mine, :] = given[...]
        cot[mine, :] = held[...]

    for step in range(rows // STEP):
        part = slice(step * STEP, (step + 1) * STEP)
        inner = jnp.dot(tokens[mine, part], w_in[part, :], preferred_element_type=jnp.float32)
        outer = against(cot[mine, part], w_down[:, part])
        if step == 0:
            total[out, : 2 * units] = inner
            total[out, 2 * units :] = outer
        else:
            total[out, : 2 * units] += inner
            total[out, 2 * units :] += outer
    short[...] = total[out, :].astype(short.dtype)


def join(group, far, place, held, given, w_in, w_down, before):
    half, rows = held.shape
    units = w_down.shape[0]
    return pl.pallas_call(
        functools.partial(join_kernel, group, far),
        in_specs=[IN_SMEM] + [IN_VMEM] * (4 + len(before)),
        out_specs=[IN_VMEM] * 4,
        out_shape=[
            pltpu.VMEM(before[0].shape, jnp.bfloat16),
            pltpu.VMEM(before[1].shape, jnp.bfloat16),
            pltpu.VMEM((2 * half, 3 * units), jnp.float32),
            pltpu.VMEM((half, 3 * units), jnp.bfloat16),
        ],
        input_output_aliases={5 + i: i for i in range(len(before))},
        compiler_params=grant(8),
        cost_estimate=cost(0),
        name="join",
    )(place, *(in_vmem(a) for a in (held, given, w_in, w_down, *before)))


def activate_kernel(group, turns, count, block, place, weights, total, arrived, *refs):
    pairs = weights.shape[0] // (2 * block)
    act, d_inner, *targets = refs[-2 - pairs :]
    units, half, chunk = act.shape[1], count // 2, 32
    side = side_of(place[0])

    def rows(first, length):
        return pl.ds(pl.multiple_of(first, 16), length)

    for turn in turns:
        natural = (1 - side if turn else side) * half
        for start in range(0, half, chunk):
            def of(array):
                return rows((natural if array.shape[0] == count else 0) + start, chunk)

            sums = total[of(total), :] + arrived[of(arrived), :].astype(jnp.float32)
            gate, upper, d_act = sums[:, :units], sums[:, units : 2 * units], sums[:, 2 * units :]
            sig = jax.nn.sigmoid(gate)
            silu_val = gate * sig
            kept = rows(group * count + natural + start, chunk)
            act[kept, :] = (silu_val * upper).astype(act.dtype)
            d_inner[kept, :units] = (d_act * upper * sig * (1.0 + gate * (1.0 - sig))).astype(d_inner.dtype)
            d_inner[kept, units:] = (d_act * silu_val).astype(d_inner.dtype)
    if len(turns) == 2:
        mine = rows(group * count, count)
    else:
        mine = rows(group * count + natural, half)

    def store(target, product, h):
        for i in (0, 1):
            lanes = slice((2 * i + h) * block, (2 * i + h + 1) * block)
            target[:, lanes] = product[:, i * block : (i + 1) * block].astype(target.dtype)

    for p, target in enumerate(targets):
        product = against(d_inner[mine, :], weights[2 * p * block : 2 * (p + 1) * block, :])
        if len(turns) == 2:
            store(target, product[:half], 0)
            store(target, product[half:], 1)
        else:
            for h in (0, 1):
                pl.when(natural == h * half)(functools.partial(store, target, product, h))


def activate(group, groups, turns, place, total, arrived, weights, blocks, before):
    units, pairs = weights.shape[1] // 2, blocks // 2
    block = weights.shape[0] // blocks
    count = arrived.shape[0] * (3 - len(turns))
    terms = count // 2, 4 * block
    return pl.pallas_call(
        functools.partial(activate_kernel, group, turns, count, block),
        in_specs=[IN_SMEM] + [IN_VMEM] * (3 + len(before)),
        out_specs=[IN_VMEM] * (2 + pairs),
        out_shape=[
            pltpu.VMEM((groups * count, units), jnp.bfloat16),
            pltpu.VMEM((groups * count, 2 * units), jnp.bfloat16),
        ]
        + [pltpu.VMEM(terms, jnp.bfloat16)] * (pairs // 2)
        + [pltpu.VMEM(terms, jnp.float32)] * (pairs // 2),
        input_output_aliases={4 + i: i for i in range(len(before))},
        compiler_params=grant(12),
        cost_estimate=cost(0),
        name="activate",
    )(place, *(in_vmem(a) for a in (weights, total, arrived, *before)))


def grads_kernel(first, by_rows, left, right, target, held, sems):
    wide = left if by_rows else right
    copies = []
    for step in range(wide.shape[1] // STEP):
        part = slice(step * STEP, (step + 1) * STEP)
        if by_rows:
            index = (part, slice(None))
            held[index] = contract(left[:, part], right[:, first : first + target.shape[1]]).astype(held.dtype)
        else:
            index = (slice(None), part)
            held[index] = contract(left[...], right[:, part]).astype(held.dtype)
        copies.append(pltpu.make_async_copy(held.at[index], target.at[index], sems.at[step]))
        copies[-1].start()
    for copy in copies:
        copy.wait()


def weight_grad(left, right, first, units, by_rows):
    rows = (left if by_rows else right).shape[1]
    shape = (rows, units) if by_rows else (units, rows)
    return pl.pallas_call(
        functools.partial(grads_kernel, first, by_rows),
        in_specs=[IN_VMEM] * 2,
        out_specs=IN_HBM,
        out_shape=pltpu.HBM(shape, jnp.bfloat16),
        scratch_shapes=[pltpu.VMEM(shape, jnp.bfloat16), pltpu.SemaphoreType.DMA((rows // STEP,))],
        compiler_params=grant(10),
        cost_estimate=cost(2 * left.shape[0] * rows * units),
        name="weight_grad",
    )(in_vmem(left), in_vmem(right))


def after(value, *earlier):
    return lax.optimization_barrier((value, earlier))[0]


def body(tokens, cotangent, gate_codes, up_codes, down_codes, gate_scales, up_scales, down_scales):
    nodes, width = lax.axis_size("node"), lax.axis_size("dp")
    node, place = lax.axis_index("node"), lax.axis_index("dp")
    node_ref, place_ref = node.reshape(1), place.reshape(1)
    rows, units = gate_codes.shape
    count = tokens.shape[0]
    owners = width // nodes
    bits = owners.bit_length() - 1
    block = rows // owners

    side, half = side_of(place), count // 2

    def halves(array):
        return [lax.dynamic_slice_in_dim(array, s * half, half, 0) for s in (side, 1 - side)]

    fetched = [
        swap(fetch(k, node_ref, place_ref, tokens, cotangent, (half, rows)), "node", nodes, k)
        for k in range(1, nodes)
    ]
    all_tokens, all_cots, w_in, w_down, own_sums, own_short = prepare(
        nodes, node_ref, tokens, cotangent, gate_codes, up_codes, down_codes, gate_scales, up_scales, down_scales
    )
    fetched = after(fetched, own_short)
    w_relative = reorder(place_ref, w_in, owners)
    fetched = after(fetched, w_relative)

    sums, shorts = [own_sums], [None]
    for k, mine in enumerate(fetched, 1):
        given = swap(mine, "dp", width, 1)
        beside = swap(mine, "dp", width, 1 << SIDE_BIT)
        before, near_far = [all_tokens, all_cots], []
        for far, held in enumerate((mine, beside)):
            if far:
                given = swap(held, "dp", width, 1)
            *before, short = join(k, far, place_ref, held, given, w_in, w_down, before)
            near_far.append(short)
        all_tokens, all_cots, total = before
        sums.append(total)
        shorts.append(near_far)

    mask = 1
    if nodes > 2:
        while mask < nodes // 2:
            sent = [swap(s.astype(jnp.bfloat16), "node", nodes, mask) for s in sums]
            sums = [s + sent[k ^ mask].astype(jnp.float32) for k, s in enumerate(sums)]
            mask *= 2
        own_short = sums[0].astype(jnp.bfloat16)
        shorts = [halves(s.astype(jnp.bfloat16)) for s in sums]
    near_far = [swap(s, "node", nodes, mask) for s in shorts[mask]]
    arrived = [None]
    for k in range(1, nodes):
        short = own_short if k == mask else sums[k ^ mask].astype(jnp.bfloat16)
        arrived.append(swap(short, "node", nodes, mask))

    peers = owners // 2

    def split(parts, *earlier):
        size = len(parts) // 2
        got = [swap(part, "dp", width, 1) for part in parts[:size]]
        if earlier:
            got = after(got, *earlier)
        sending = []
        for r in range(peers):
            lanes = slice(r % 2 * 2 * block, (r % 2 + 1) * 2 * block)
            both = parts[size + r // 2][:, lanes] + got[r // 2][:, lanes].astype(jnp.float32)
            if r < peers - 1:
                mask = sum(1 << bit for bit in range(1, bits) if (r >> (bits - 1 - bit)) & 1 == 0)
                sending.append((mask, both.astype(jnp.bfloat16)))
        return sending, both

    def exchange(sending):
        return [swap(value, "dp", width, mask) for mask, value in sending]

    def add(mine, got):
        for value in got:
            mine += value.astype(jnp.float32)
        return mine

    blocks, before, others = [None] * nodes, [], [None] * nodes
    for k in reversed(range(1, nodes)):
        act, d_inner, *others[k] = activate(
            k, nodes, (0, 1), place_ref, sums[k], arrived[k], w_relative, owners, before
        )
        before = [act, d_inner]
    before = activate(0, nodes, (0,), place_ref, sums[0], near_far[0], w_relative, owners, before)
    last = []
    for k in range(1, nodes):
        sending, mine = split(others[k], before)
        last.append([value for _, value in sending])
        blocks[k] = mine, exchange(sending)
    act, d_inner, *parts = activate(
        0, nodes, (1,), place_ref, sums[0], after(near_far[1], last), w_relative, owners, before
    )
    sending, mine = split(parts)
    got = exchange(sending)
    sent = [value for _, value in sending]
    for k in range(1, nodes):
        value = add(*blocks[k]).astype(jnp.bfloat16)
        act, sent, value = lax.optimization_barrier((act, sent, value))
        blocks[k] = swap(value, "node", nodes, k).astype(jnp.float32)
    down_grad = weight_grad(after(act, sent), all_cots, 0, units, False)
    blocks[0] = add(mine, after(got, down_grad))
    high = place // owners

    def block_for(owner):
        chosen = blocks[0]
        for k in range(1, nodes):
            chosen = jnp.where((owner ^ node) == k, blocks[k], chosen)
        return chosen

    sent = [block_for(high ^ j).astype(jnp.bfloat16) for j in range(1, nodes)]
    d_inner = after(d_inner, sent)
    gate_grad = weight_grad(all_tokens, d_inner, 0, units, True)
    up_grad = weight_grad(all_tokens, d_inner, units, units, True)
    token_grad = block_for(high)
    for j in range(1, nodes):
        arrived = after(swap(sent[j - 1], "dp", width, j * owners), gate_grad, up_grad)
        token_grad += arrived.astype(jnp.float32)
    token_grad = token_grad.astype(jnp.bfloat16)
    token_grad = jnp.concatenate([token_grad[:, :block], token_grad[:, block:]])
    return token_grad, gate_grad, up_grad, down_grad


def solution(mesh):
    return jax.shard_map(
        body,
        mesh=mesh,
        in_specs=(
            P("node", None),
            P("node", None),
            P("node", "dp"),
            P("node", "dp"),
            P("dp", "node"),
            P(None, "dp"),
            P(None, "dp"),
            P("dp", None),
        ),
        out_specs=(P("node", "dp"), P("node", "dp"), P("node", "dp"), P("dp", "node")),
        check_vma=False,
    )
```

```python
import functools

import jax
import jax.numpy as jnp
from jax import lax
from jax.experimental import pallas as pl
from jax.experimental.pallas import tpu as pltpu
from jax.sharding import PartitionSpec as P

QB = 128
STEP = 640
SIDE_BIT = 2
IN_HBM = pl.BlockSpec(memory_space=pltpu.HBM)
IN_VMEM = pl.BlockSpec(memory_space=pltpu.VMEM)
IN_SMEM = pl.BlockSpec(memory_space=pltpu.SMEM)


def contract(left, right):
    return lax.dot_general(
        left, right, (((0,), (0,)), ((), ())), preferred_element_type=jnp.float32
    )


def against(left, right):
    return lax.dot_general(
        left, right, (((1,), (1,)), ((), ())), preferred_element_type=jnp.float32
    )


def flipped(size, mask):
    return [(i, i ^ mask) for i in range(size)]


def swap(value, axis, size, mask):
    return lax.ppermute(value, axis, flipped(size, mask))


def in_hbm(array):
    return pltpu.with_memory_space_constraint(array, pltpu.HBM)


def in_vmem(array):
    return pltpu.with_memory_space_constraint(array, pltpu.VMEM)


def cost(operations):
    return pl.CostEstimate(flops=operations, transcendentals=0, bytes_accessed=0)


def grant(mebibytes):
    return pltpu.CompilerParams(vmem_limit_bytes=mebibytes * 1024 * 1024)


def side_of(place):
    return (place >> SIDE_BIT) & 1


def fetch_kernel(mask, node, place, tokens, cot, target, sem):
    half, rows = target.shape
    start = pl.multiple_of(side_of(place[0]) * half, 16)
    column = pl.multiple_of((node[0] ^ mask) * rows, 128)
    part = (pl.ds(start, half), pl.ds(column, rows))

    @pl.when((place[0] & 1) == 0)
    def _():
        copy = pltpu.make_async_copy(tokens.at[part], target, sem)
        copy.start()
        copy.wait()

    @pl.when((place[0] & 1) == 1)
    def _():
        copy = pltpu.make_async_copy(cot.at[part], target, sem)
        copy.start()
        copy.wait()


def fetch(mask, node, place, tokens, cot, shape):
    return pl.pallas_call(
        functools.partial(fetch_kernel, mask),
        in_specs=[IN_SMEM, IN_SMEM, IN_HBM, IN_HBM],
        out_specs=IN_VMEM,
        out_shape=pltpu.VMEM(shape, tokens.dtype),
        scratch_shapes=[pltpu.SemaphoreType.DMA],
        compiler_params=grant(2),
        cost_estimate=cost(0),
        name="fetch",
    )(node, place, in_hbm(tokens), in_hbm(cot))


def prepare_kernel(
    node, tokens, cot, gate_codes, up_codes, down_codes, gate_scales, up_scales, down_scales,
    all_tokens, all_cots, w_in, w_down, total, short, sems,
):
    rows, units = gate_codes.shape
    steps, per_step = rows // STEP, STEP // QB
    own = slice(0, tokens.shape[0])
    gate, up = slice(0, units), slice(units, 2 * units)

    def copies(step):
        column = pl.multiple_of(node[0] * rows + step * STEP, 128)
        part = pl.ds(pl.multiple_of(step * STEP, 128), STEP)
        pairs = (
            (gate_codes.at[part, :], w_in.at[part, gate]),
            (up_codes.at[part, :], w_in.at[part, up]),
            (tokens.at[:, pl.ds(column, STEP)], all_tokens.at[own, part]),
            (down_codes.at[:, part], w_down.at[:, part]),
            (cot.at[:, pl.ds(column, STEP)], all_cots.at[own, part]),
        )
        return [pltpu.make_async_copy(a, b, sems.at[step, i]) for i, (a, b) in enumerate(pairs)]

    for step in range(steps):
        for copy in copies(step):
            copy.start()
    total[...] = jnp.zeros(total.shape, total.dtype)

    def scale(weights, index, factor):
        weights[index] = (weights[index].astype(jnp.float32) * factor).astype(weights.dtype)

    def one(step, carry):
        for copy in copies(step):
            copy.wait()
        first_scale = (node[0] * steps + step) * per_step
        for j in range(per_step):
            part = pl.ds(pl.multiple_of(step * STEP + j * QB, QB), QB)
            row = pl.ds(first_scale + j, 1)
            scale(w_in, (part, gate), gate_scales[row, :])
            scale(w_in, (part, up), up_scales[row, :])
            scale(w_down, (slice(None), part), down_scales[step, :, j : j + 1])
        part = pl.ds(pl.multiple_of(step * STEP, 128), STEP)
        total[:, : 2 * units] += jnp.dot(all_tokens[own, part], w_in[part, :], preferred_element_type=jnp.float32)
        total[:, 2 * units :] += against(all_cots[own, part], w_down[:, part])
        return carry

    lax.fori_loop(0, steps, one, 0)
    short[...] = total[...].astype(short.dtype)


def prepare(nodes, node, tokens, cot, gate_codes, up_codes, down_codes, gate_scales, up_scales, down_scales):
    rows, units = gate_codes.shape
    count = tokens.shape[0]
    steps, per_step = rows // STEP, STEP // QB
    scales = lax.dynamic_slice_in_dim(down_scales, node[0] * (rows // QB), rows // QB, 1)
    scales = scales.reshape(units, steps, per_step).transpose(1, 0, 2)
    codes = jnp.bfloat16
    return pl.pallas_call(
        prepare_kernel,
        in_specs=[IN_SMEM] + [IN_HBM] * 5 + [IN_VMEM] * 3,
        out_specs=[IN_VMEM] * 6,
        out_shape=[
            pltpu.VMEM((nodes * count, rows), codes),
            pltpu.VMEM((nodes * count, rows), codes),
            pltpu.VMEM((rows, 2 * units), codes),
            pltpu.VMEM((units, rows), codes),
            pltpu.VMEM((count, 3 * units), jnp.float32),
            pltpu.VMEM((count, 3 * units), codes),
        ],
        scratch_shapes=[pltpu.SemaphoreType.DMA((steps, 5))],
        compiler_params=grant(4),
        cost_estimate=cost(0),
        name="prepare",
    )(
        node, *(in_hbm(a) for a in (tokens, cot, gate_codes, up_codes, down_codes)),
        gate_scales, up_scales, scales,
    )


def join_kernel(group, far, place, held, given, w_in, w_down, *refs):
    tokens, cot, total, short = refs[-4:]
    half, rows = held.shape
    units = w_down.shape[0]
    side = side_of(place[0])
    natural = (1 - side if far else side) * half
    mine = pl.ds(pl.multiple_of(2 * group * half + natural, 16), half)
    out = pl.ds(pl.multiple_of(natural, 16), half)

    @pl.when((place[0] & 1) == 0)
    def _():
        tokens[mine, :] = held[...]
        cot[mine, :] = given[...]

    @pl.when((place[0] & 1) == 1)
    def _():
        tokens[mine, :] = given[...]
        cot[mine, :] = held[...]

    for step in range(rows // STEP):
        part = slice(step * STEP, (step + 1) * STEP)
        inner = jnp.dot(tokens[mine, part], w_in[part, :], preferred_element_type=jnp.float32)
        outer = against(cot[mine, part], w_down[:, part])
        if step == 0:
            total[out, : 2 * units] = inner
            total[out, 2 * units :] = outer
        else:
            total[out, : 2 * units] += inner
            total[out, 2 * units :] += outer
    short[...] = total[out, :].astype(short.dtype)


def join(group, far, place, held, given, w_in, w_down, before):
    half, rows = held.shape
    units = w_down.shape[0]
    return pl.pallas_call(
        functools.partial(join_kernel, group, far),
        in_specs=[IN_SMEM] + [IN_VMEM] * (4 + len(before)),
        out_specs=[IN_VMEM] * 4,
        out_shape=[
            pltpu.VMEM(before[0].shape, jnp.bfloat16),
            pltpu.VMEM(before[1].shape, jnp.bfloat16),
            pltpu.VMEM((2 * half, 3 * units), jnp.float32),
            pltpu.VMEM((half, 3 * units), jnp.bfloat16),
        ],
        input_output_aliases={5 + i: i for i in range(len(before))},
        compiler_params=grant(6),
        cost_estimate=cost(0),
        name="join",
    )(place, *(in_vmem(a) for a in (held, given, w_in, w_down, *before)))


def activate_kernel(group, turns, count, blocks, place, weights, total, arrived, *refs):
    block = weights.shape[0] // blocks
    act, d_inner, *targets = refs[-2 - blocks // 2 :]
    units, half, chunk = act.shape[1], count // 2, 32
    side = side_of(place[0])

    def rows(first, length):
        return pl.ds(pl.multiple_of(first, 16), length)

    for turn in turns:
        natural = (1 - side if turn else side) * half
        for start in range(0, half, chunk):
            def of(array):
                return rows((natural if array.shape[0] == count else 0) + start, chunk)

            sums = total[of(total), :] + arrived[of(arrived), :].astype(jnp.float32)
            gate, upper, d_act = sums[:, :units], sums[:, units : 2 * units], sums[:, 2 * units :]
            sig = jax.nn.sigmoid(gate)
            silu_val = gate * sig
            kept = rows(group * count + natural + start, chunk)
            act[kept, :] = (silu_val * upper).astype(act.dtype)
            d_inner[kept, :units] = (d_act * upper * sig * (1.0 + gate * (1.0 - sig))).astype(d_inner.dtype)
            d_inner[kept, units:] = (d_act * silu_val).astype(d_inner.dtype)
    def block_rows(relative):
        bits = blocks.bit_length() - 1
        owner = 0
        for bit in range(bits):
            own = (place[0] >> bit) & 1
            owner += (own if (relative >> (bits - 1 - bit)) & 1 else 1 - own) << bit
        return weights[rows(owner * block, block), :]

    def store(h, mine):
        for p, target in enumerate(targets):
            pieces, places, width = [], [], 0
            for i in (0, 1):
                pad = ((2 * i + h) * block - width) % 128
                if pad:
                    pieces.append(weights[:pad, :])
                pieces.append(block_rows(2 * p + i))
                places.append(width + pad)
                width += pad + block
            product = against(mine, jnp.concatenate(pieces))
            for i in (0, 1):
                lanes = slice((2 * i + h) * block, (2 * i + h + 1) * block)
                target[:, lanes] = product[:, places[i] : places[i] + block].astype(target.dtype)

    for h in (0, 1):
        if len(turns) == 2:
            store(h, d_inner[rows(group * count + h * half, half), :])
        else:
            pl.when(natural == h * half)(lambda: store(h, d_inner[rows(group * count + h * half, half), :]))


def activate(group, groups, turns, place, total, arrived, weights, blocks, before):
    units, pairs = weights.shape[1] // 2, blocks // 2
    block = weights.shape[0] // blocks
    count = arrived.shape[0] * (3 - len(turns))
    terms = count // 2, 4 * block
    return pl.pallas_call(
        functools.partial(activate_kernel, group, turns, count, blocks),
        in_specs=[IN_SMEM] + [IN_VMEM] * (3 + len(before)),
        out_specs=[IN_VMEM] * (2 + pairs),
        out_shape=[
            pltpu.VMEM((groups * count, units), jnp.bfloat16),
            pltpu.VMEM((groups * count, 2 * units), jnp.bfloat16),
        ]
        + [pltpu.VMEM(terms, jnp.bfloat16)] * (pairs // 2)
        + [pltpu.VMEM(terms, jnp.float32)] * (pairs // 2),
        input_output_aliases={4 + i: i for i in range(len(before))},
        compiler_params=grant(8),
        cost_estimate=cost(0),
        name="activate",
    )(place, *(in_vmem(a) for a in (weights, total, arrived, *before)))


def grads_kernel(first, by_rows, left, right, target, held, sems):
    wide = left if by_rows else right
    copies = []
    for step in range(wide.shape[1] // STEP):
        part = slice(step * STEP, (step + 1) * STEP)
        if by_rows:
            index = (part, slice(None))
            held[index] = contract(left[:, part], right[:, first : first + target.shape[1]]).astype(held.dtype)
        else:
            index = (slice(None), part)
            held[index] = contract(left[...], right[:, part]).astype(held.dtype)
        copies.append(pltpu.make_async_copy(held.at[index], target.at[index], sems.at[step]))
        copies[-1].start()
    for copy in copies:
        copy.wait()


def weight_grad(left, right, first, units, by_rows):
    rows = (left if by_rows else right).shape[1]
    shape = (rows, units) if by_rows else (units, rows)
    return pl.pallas_call(
        functools.partial(grads_kernel, first, by_rows),
        in_specs=[IN_VMEM] * 2,
        out_specs=IN_HBM,
        out_shape=pltpu.HBM(shape, jnp.bfloat16),
        scratch_shapes=[pltpu.VMEM(shape, jnp.bfloat16), pltpu.SemaphoreType.DMA((rows // STEP,))],
        compiler_params=grant(6),
        cost_estimate=cost(2 * left.shape[0] * rows * units),
        name="weight_grad",
    )(in_vmem(left), in_vmem(right))


def after(value, *earlier):
    return lax.optimization_barrier((value, earlier))[0]


def body(tokens, cotangent, gate_codes, up_codes, down_codes, gate_scales, up_scales, down_scales):
    nodes, width = lax.axis_size("node"), lax.axis_size("dp")
    node, place = lax.axis_index("node"), lax.axis_index("dp")
    node_ref, place_ref = node.reshape(1), place.reshape(1)
    rows, units = gate_codes.shape
    count = tokens.shape[0]
    owners = width // nodes
    bits = owners.bit_length() - 1
    block = rows // owners

    side, half = side_of(place), count // 2

    def halves(array):
        return [lax.dynamic_slice_in_dim(array, s * half, half, 0) for s in (side, 1 - side)]

    fetched = [
        swap(fetch(k, node_ref, place_ref, tokens, cotangent, (half, rows)), "node", nodes, k)
        for k in range(1, nodes)
    ]
    all_tokens, all_cots, w_in, w_down, own_sums, own_short = prepare(
        nodes, node_ref, tokens, cotangent, gate_codes, up_codes, down_codes, gate_scales, up_scales, down_scales
    )
    fetched = after(fetched, own_short)

    sums, shorts = [own_sums], [None]
    for k, mine in enumerate(fetched, 1):
        given = swap(mine, "dp", width, 1)
        beside = swap(mine, "dp", width, 1 << SIDE_BIT)
        before, near_far = [all_tokens, all_cots], []
        for far, held in enumerate((mine, beside)):
            if far:
                given = swap(held, "dp", width, 1)
            *before, short = join(k, far, place_ref, held, given, w_in, w_down, before)
            near_far.append(short)
        all_tokens, all_cots, total = before
        sums.append(total)
        shorts.append(near_far)

    mask = 1
    if nodes > 2:
        while mask < nodes // 2:
            sent = [swap(s.astype(jnp.bfloat16), "node", nodes, mask) for s in sums]
            sums = [s + sent[k ^ mask].astype(jnp.float32) for k, s in enumerate(sums)]
            mask *= 2
        own_short = sums[0].astype(jnp.bfloat16)
        shorts = [halves(s.astype(jnp.bfloat16)) for s in sums]
    near_far = [swap(s, "node", nodes, mask) for s in shorts[mask]]
    arrived = [None]
    for k in range(1, nodes):
        short = own_short if k == mask else sums[k ^ mask].astype(jnp.bfloat16)
        arrived.append(swap(short, "node", nodes, mask))

    peers = owners // 2

    def split(parts, *earlier):
        size = len(parts) // 2
        got = [swap(part, "dp", width, 1) for part in parts[:size]]
        if earlier:
            got = after(got, *earlier)
        sending = []
        for r in range(peers):
            lanes = slice(r % 2 * 2 * block, (r % 2 + 1) * 2 * block)
            both = parts[size + r // 2][:, lanes] + got[r // 2][:, lanes].astype(jnp.float32)
            if r < peers - 1:
                mask = sum(1 << bit for bit in range(1, bits) if (r >> (bits - 1 - bit)) & 1 == 0)
                sending.append((mask, both.astype(jnp.bfloat16)))
        return sending, both

    def exchange(sending):
        return [swap(value, "dp", width, mask) for mask, value in sending]

    def add(mine, got):
        for value in got:
            mine += value.astype(jnp.float32)
        return mine

    blocks, before, others = [None] * nodes, [], [None] * nodes
    for k in reversed(range(1, nodes)):
        act, d_inner, *others[k] = activate(
            k, nodes, (0, 1), place_ref, sums[k], arrived[k], w_in, owners, before
        )
        before = [act, d_inner]
    before = activate(0, nodes, (0,), place_ref, sums[0], near_far[0], w_in, owners, before)
    last = []
    for k in range(1, nodes):
        sending, mine = split(others[k], before)
        last.append([value for _, value in sending])
        blocks[k] = mine, exchange(sending)
    act, d_inner, *parts = activate(
        0, nodes, (1,), place_ref, sums[0], after(near_far[1], last), w_in, owners, before
    )
    sending, mine = split(parts)
    got = exchange(sending)
    sent = [value for _, value in sending]
    for k in range(1, nodes):
        value = add(*blocks[k]).astype(jnp.bfloat16)
        act, sent, value = lax.optimization_barrier((act, sent, value))
        blocks[k] = swap(value, "node", nodes, k).astype(jnp.float32)
    down_grad = weight_grad(after(act, sent), all_cots, 0, units, False)
    blocks[0] = add(mine, after(got, down_grad))
    high = place // owners

    def block_for(owner):
        chosen = blocks[0]
        for k in range(1, nodes):
            chosen = jnp.where((owner ^ node) == k, blocks[k], chosen)
        return chosen

    sent = [block_for(high ^ j).astype(jnp.bfloat16) for j in range(1, nodes)]
    d_inner = after(d_inner, sent)
    gate_grad = weight_grad(all_tokens, d_inner, 0, units, True)
    up_grad = weight_grad(all_tokens, d_inner, units, units, True)
    token_grad = block_for(high)
    for j in range(1, nodes):
        arrived = after(swap(sent[j - 1], "dp", width, j * owners), gate_grad, up_grad)
        token_grad += arrived.astype(jnp.float32)
    token_grad = token_grad.astype(jnp.bfloat16)
    token_grad = jnp.concatenate([token_grad[:, :block], token_grad[:, block:]])
    return token_grad, gate_grad, up_grad, down_grad


def solution(mesh):
    return jax.shard_map(
        body,
        mesh=mesh,
        in_specs=(
            P("node", None),
            P("node", None),
            P("node", "dp"),
            P("node", "dp"),
            P("dp", "node"),
            P(None, "dp"),
            P(None, "dp"),
            P("dp", None),
        ),
        out_specs=(P("node", "dp"), P("node", "dp"), P("node", "dp"), P("dp", "node")),
        check_vma=False,
    )
```

```python
import functools

import jax
import jax.numpy as jnp
from jax import lax
from jax.experimental import pallas as pl
from jax.experimental.pallas import tpu as pltpu
from jax.sharding import PartitionSpec as P

QB = 128
STEP = 640
SIDE_BIT = 2
IN_HBM = pl.BlockSpec(memory_space=pltpu.HBM)
IN_VMEM = pl.BlockSpec(memory_space=pltpu.VMEM)
IN_SMEM = pl.BlockSpec(memory_space=pltpu.SMEM)


def contract(left, right):
    return lax.dot_general(
        left, right, (((0,), (0,)), ((), ())), preferred_element_type=jnp.float32
    )


def against(left, right):
    return lax.dot_general(
        left, right, (((1,), (1,)), ((), ())), preferred_element_type=jnp.float32
    )


def flipped(size, mask):
    return [(i, i ^ mask) for i in range(size)]


def swap(value, axis, size, mask):
    return lax.ppermute(value, axis, flipped(size, mask))


def in_hbm(array):
    return pltpu.with_memory_space_constraint(array, pltpu.HBM)


def in_vmem(array):
    return pltpu.with_memory_space_constraint(array, pltpu.VMEM)


def cost(operations):
    return pl.CostEstimate(flops=operations, transcendentals=0, bytes_accessed=0)


def grant(mebibytes):
    return pltpu.CompilerParams(vmem_limit_bytes=mebibytes * 1024 * 1024)


def side_of(place):
    return (place >> SIDE_BIT) & 1


def fetch_kernel(mask, node, place, tokens, cot, target, sem):
    half, rows = target.shape
    start = pl.multiple_of(side_of(place[0]) * half, 16)
    column = pl.multiple_of((node[0] ^ mask) * rows, 128)
    part = (pl.ds(start, half), pl.ds(column, rows))

    @pl.when((place[0] & 1) == 0)
    def _():
        copy = pltpu.make_async_copy(tokens.at[part], target, sem)
        copy.start()
        copy.wait()

    @pl.when((place[0] & 1) == 1)
    def _():
        copy = pltpu.make_async_copy(cot.at[part], target, sem)
        copy.start()
        copy.wait()


def fetch(mask, node, place, tokens, cot, shape):
    return pl.pallas_call(
        functools.partial(fetch_kernel, mask),
        in_specs=[IN_SMEM, IN_SMEM, IN_HBM, IN_HBM],
        out_specs=IN_VMEM,
        out_shape=pltpu.VMEM(shape, tokens.dtype),
        scratch_shapes=[pltpu.SemaphoreType.DMA],
        compiler_params=grant(2),
        cost_estimate=cost(0),
        name="fetch",
    )(node, place, in_hbm(tokens), in_hbm(cot))


def prepare_kernel(
    node, tokens, cot, gate_codes, up_codes, down_codes, gate_scales, up_scales, down_scales,
    all_tokens, all_cots, w_in, w_down, total, short, sems,
):
    rows, units = gate_codes.shape
    steps, per_step = rows // STEP, STEP // QB
    own = slice(0, tokens.shape[0])
    gate, up = slice(0, units), slice(units, 2 * units)

    def copies(step):
        column = pl.multiple_of(node[0] * rows + step * STEP, 128)
        part = pl.ds(pl.multiple_of(step * STEP, 128), STEP)
        pairs = (
            (gate_codes.at[part, :], w_in.at[part, gate]),
            (up_codes.at[part, :], w_in.at[part, up]),
            (tokens.at[:, pl.ds(column, STEP)], all_tokens.at[own, part]),
            (down_codes.at[:, part], w_down.at[:, part]),
            (cot.at[:, pl.ds(column, STEP)], all_cots.at[own, part]),
        )
        return [pltpu.make_async_copy(a, b, sems.at[step, i]) for i, (a, b) in enumerate(pairs)]

    for step in range(steps):
        for copy in copies(step):
            copy.start()
    total[...] = jnp.zeros(total.shape, total.dtype)

    def scale(weights, index, factor):
        weights[index] = (weights[index].astype(jnp.float32) * factor).astype(weights.dtype)

    def one(step, carry):
        for copy in copies(step):
            copy.wait()
        first_scale = (node[0] * steps + step) * per_step
        for j in range(per_step):
            part = pl.ds(pl.multiple_of(step * STEP + j * QB, QB), QB)
            row = pl.ds(first_scale + j, 1)
            scale(w_in, (part, gate), gate_scales[row, :])
            scale(w_in, (part, up), up_scales[row, :])
            scale(w_down, (slice(None), part), down_scales[step, :, j : j + 1])
        part = pl.ds(pl.multiple_of(step * STEP, 128), STEP)
        total[:, : 2 * units] += jnp.dot(all_tokens[own, part], w_in[part, :], preferred_element_type=jnp.float32)
        total[:, 2 * units :] += against(all_cots[own, part], w_down[:, part])
        return carry

    lax.fori_loop(0, steps, one, 0)
    short[...] = total[...].astype(short.dtype)


def prepare(nodes, node, tokens, cot, gate_codes, up_codes, down_codes, gate_scales, up_scales, down_scales):
    rows, units = gate_codes.shape
    count = tokens.shape[0]
    steps, per_step = rows // STEP, STEP // QB
    scales = lax.dynamic_slice_in_dim(down_scales, node[0] * (rows // QB), rows // QB, 1)
    scales = scales.reshape(units, steps, per_step).transpose(1, 0, 2)
    codes = jnp.bfloat16
    return pl.pallas_call(
        prepare_kernel,
        in_specs=[IN_SMEM] + [IN_HBM] * 5 + [IN_VMEM] * 3,
        out_specs=[IN_VMEM] * 6,
        out_shape=[
            pltpu.VMEM((nodes * count, rows), codes),
            pltpu.VMEM((nodes * count, rows), codes),
            pltpu.VMEM((rows, 2 * units), codes),
            pltpu.VMEM((units, rows), codes),
            pltpu.VMEM((count, 3 * units), jnp.float32),
            pltpu.VMEM((count, 3 * units), codes),
        ],
        scratch_shapes=[pltpu.SemaphoreType.DMA((steps, 5))],
        compiler_params=grant(4),
        cost_estimate=cost(0),
        name="prepare",
    )(
        node, *(in_hbm(a) for a in (tokens, cot, gate_codes, up_codes, down_codes)),
        gate_scales, up_scales, scales,
    )


def join_kernel(group, far, place, held, given, w_in, w_down, *refs):
    tokens, cot, total, short = refs[-4:]
    half, rows = held.shape
    units = w_down.shape[0]
    side = side_of(place[0])
    natural = (1 - side if far else side) * half
    mine = pl.ds(pl.multiple_of(2 * group * half + natural, 16), half)
    out = pl.ds(pl.multiple_of(natural, 16), half)

    @pl.when((place[0] & 1) == 0)
    def _():
        tokens[mine, :] = held[...]
        cot[mine, :] = given[...]

    @pl.when((place[0] & 1) == 1)
    def _():
        tokens[mine, :] = given[...]
        cot[mine, :] = held[...]

    for step in range(rows // STEP):
        part = slice(step * STEP, (step + 1) * STEP)
        inner = jnp.dot(tokens[mine, part], w_in[part, :], preferred_element_type=jnp.float32)
        outer = against(cot[mine, part], w_down[:, part])
        if step == 0:
            total[out, : 2 * units] = inner
            total[out, 2 * units :] = outer
        else:
            total[out, : 2 * units] += inner
            total[out, 2 * units :] += outer
    short[...] = total[out, :].astype(short.dtype)


def join(group, far, place, held, given, w_in, w_down, before):
    half, rows = held.shape
    units = w_down.shape[0]
    return pl.pallas_call(
        functools.partial(join_kernel, group, far),
        in_specs=[IN_SMEM] + [IN_VMEM] * (4 + len(before)),
        out_specs=[IN_VMEM] * 4,
        out_shape=[
            pltpu.VMEM(before[0].shape, jnp.bfloat16),
            pltpu.VMEM(before[1].shape, jnp.bfloat16),
            pltpu.VMEM((2 * half, 3 * units), jnp.float32),
            pltpu.VMEM((half, 3 * units), jnp.bfloat16),
        ],
        input_output_aliases={5 + i: i for i in range(len(before))},
        compiler_params=grant(6),
        cost_estimate=cost(0),
        name="join",
    )(place, *(in_vmem(a) for a in (held, given, w_in, w_down, *before)))


def activate_kernel(group, turns, count, blocks, place, weights, total, arrived, *refs):
    block = weights.shape[0] // blocks
    act, d_inner, *targets = refs[-2 - blocks // 2 :]
    units, half, chunk = act.shape[1], count // 2, 32
    side = side_of(place[0])

    def rows(first, length):
        return pl.ds(pl.multiple_of(first, 16), length)

    for turn in turns:
        natural = (1 - side if turn else side) * half
        for start in range(0, half, chunk):
            def of(array):
                return rows((natural if array.shape[0] == count else 0) + start, chunk)

            sums = total[of(total), :] + arrived[of(arrived), :].astype(jnp.float32)
            gate, upper, d_act = sums[:, :units], sums[:, units : 2 * units], sums[:, 2 * units :]
            sig = jax.nn.sigmoid(gate)
            silu_val = gate * sig
            kept = rows(group * count + natural + start, chunk)
            act[kept, :] = (silu_val * upper).astype(act.dtype)
            d_inner[kept, :units] = (d_act * upper * sig * (1.0 + gate * (1.0 - sig))).astype(d_inner.dtype)
            d_inner[kept, units:] = (d_act * silu_val).astype(d_inner.dtype)
    def block_rows(relative):
        bits = blocks.bit_length() - 1
        owner = 0
        for bit in range(bits):
            own = (place[0] >> bit) & 1
            owner += (own if (relative >> (bits - 1 - bit)) & 1 else 1 - own) << bit
        return weights[rows(owner * block, block), :]

    def store(h, mine):
        for p, target in enumerate(targets):
            pieces, places, width = [], [], 0
            for i in (0, 1):
                pad = ((2 * i + h) * block - width) % 128
                if pad:
                    pieces.append(weights[:pad, :])
                pieces.append(block_rows(2 * p + i))
                places.append(width + pad)
                width += pad + block
            product = against(mine, jnp.concatenate(pieces))
            for i in (0, 1):
                lanes = slice((2 * i + h) * block, (2 * i + h + 1) * block)
                target[:, lanes] = product[:, places[i] : places[i] + block].astype(target.dtype)

    for h in (0, 1):
        if len(turns) == 2:
            store(h, d_inner[rows(group * count + h * half, half), :])
        else:
            pl.when(natural == h * half)(lambda: store(h, d_inner[rows(group * count + h * half, half), :]))


def activate(group, groups, turns, place, total, arrived, weights, blocks, before):
    units, pairs = weights.shape[1] // 2, blocks // 2
    block = weights.shape[0] // blocks
    count = arrived.shape[0] * (3 - len(turns))
    terms = count // 2, 4 * block
    return pl.pallas_call(
        functools.partial(activate_kernel, group, turns, count, blocks),
        in_specs=[IN_SMEM] + [IN_VMEM] * (3 + len(before)),
        out_specs=[IN_VMEM] * (2 + pairs),
        out_shape=[
            pltpu.VMEM((groups * count, units), jnp.bfloat16),
            pltpu.VMEM((groups * count, 2 * units), jnp.bfloat16),
        ]
        + [pltpu.VMEM(terms, jnp.bfloat16)] * (pairs // 2)
        + [pltpu.VMEM(terms, jnp.float32)] * (pairs // 2),
        input_output_aliases={4 + i: i for i in range(len(before))},
        compiler_params=grant(8),
        cost_estimate=cost(0),
        name="activate",
    )(place, *(in_vmem(a) for a in (weights, total, arrived, *before)))


def grads_kernel(tokens, cot, act, d_inner, gate_grad, up_grad, down_grad, gate_held, up_held, down_held, sems):
    rows, units = gate_grad.shape
    copies = []

    def send(held, target, part, i):
        copies.append(pltpu.make_async_copy(held.at[part], target.at[part], sems.at[i]))
        copies[-1].start()

    steps = rows // STEP
    for step in range(steps):
        part = slice(step * STEP, (step + 1) * STEP)
        both = contract(tokens[:, part], d_inner[...])
        gate_held[part, :] = both[:, :units].astype(gate_held.dtype)
        send(gate_held, gate_grad, (part, slice(None)), step)
        up_held[part, :] = both[:, units:].astype(up_held.dtype)
        send(up_held, up_grad, (part, slice(None)), steps + step)
    for step in range(steps):
        part = slice(step * STEP, (step + 1) * STEP)
        down_held[:, part] = contract(act[...], cot[:, part]).astype(down_held.dtype)
        send(down_held, down_grad, (slice(None), part), 2 * steps + step)
    for copy in copies:
        copy.wait()


def weight_grads(tokens, cot, act, d_inner):
    rows, units = tokens.shape[1], act.shape[1]
    shapes = [(rows, units), (rows, units), (units, rows)]
    return pl.pallas_call(
        grads_kernel,
        in_specs=[IN_VMEM] * 4,
        out_specs=[IN_HBM] * 3,
        out_shape=[pltpu.HBM(shape, jnp.bfloat16) for shape in shapes],
        scratch_shapes=[pltpu.VMEM(shape, jnp.bfloat16) for shape in shapes]
        + [pltpu.SemaphoreType.DMA((3 * (rows // STEP),))],
        compiler_params=grant(20),
        cost_estimate=cost(6 * tokens.shape[0] * rows * units),
        name="weight_grads",
    )(*(in_vmem(a) for a in (tokens, cot, act, d_inner)))


def after(value, *earlier):
    return lax.optimization_barrier((value, earlier))[0]


def body(tokens, cotangent, gate_codes, up_codes, down_codes, gate_scales, up_scales, down_scales):
    nodes, width = lax.axis_size("node"), lax.axis_size("dp")
    node, place = lax.axis_index("node"), lax.axis_index("dp")
    node_ref, place_ref = node.reshape(1), place.reshape(1)
    rows, units = gate_codes.shape
    count = tokens.shape[0]
    owners = width // nodes
    bits = owners.bit_length() - 1
    block = rows // owners

    side, half = side_of(place), count // 2

    def halves(array):
        return [lax.dynamic_slice_in_dim(array, s * half, half, 0) for s in (side, 1 - side)]

    fetched = [
        swap(fetch(k, node_ref, place_ref, tokens, cotangent, (half, rows)), "node", nodes, k)
        for k in range(1, nodes)
    ]
    all_tokens, all_cots, w_in, w_down, own_sums, own_short = prepare(
        nodes, node_ref, tokens, cotangent, gate_codes, up_codes, down_codes, gate_scales, up_scales, down_scales
    )
    fetched = after(fetched, own_short)

    sums, shorts = [own_sums], [None]
    for k, mine in enumerate(fetched, 1):
        given = swap(mine, "dp", width, 1)
        beside = swap(mine, "dp", width, 1 << SIDE_BIT)
        before, near_far = [all_tokens, all_cots], []
        for far, held in enumerate((mine, beside)):
            if far:
                given = swap(held, "dp", width, 1)
            *before, short = join(k, far, place_ref, held, given, w_in, w_down, before)
            near_far.append(short)
        all_tokens, all_cots, total = before
        sums.append(total)
        shorts.append(near_far)

    mask = 1
    if nodes > 2:
        while mask < nodes // 2:
            sent = [swap(s.astype(jnp.bfloat16), "node", nodes, mask) for s in sums]
            sums = [s + sent[k ^ mask].astype(jnp.float32) for k, s in enumerate(sums)]
            mask *= 2
        own_short = sums[0].astype(jnp.bfloat16)
        shorts = [halves(s.astype(jnp.bfloat16)) for s in sums]
    near_far = [swap(s, "node", nodes, mask) for s in shorts[mask]]
    arrived = [None]
    for k in range(1, nodes):
        short = own_short if k == mask else sums[k ^ mask].astype(jnp.bfloat16)
        arrived.append(swap(short, "node", nodes, mask))

    peers = owners // 2

    def split(parts, *earlier):
        size = len(parts) // 2
        got = [swap(part, "dp", width, 1) for part in parts[:size]]
        if earlier:
            got = after(got, *earlier)
        sending = []
        for r in range(peers):
            lanes = slice(r % 2 * 2 * block, (r % 2 + 1) * 2 * block)
            both = parts[size + r // 2][:, lanes] + got[r // 2][:, lanes].astype(jnp.float32)
            if r < peers - 1:
                mask = sum(1 << bit for bit in range(1, bits) if (r >> (bits - 1 - bit)) & 1 == 0)
                sending.append((mask, both.astype(jnp.bfloat16)))
        return sending, both

    def exchange(sending):
        return [swap(value, "dp", width, mask) for mask, value in sending]

    def add(mine, got):
        for value in got:
            mine += value.astype(jnp.float32)
        return mine

    blocks, before, others = [None] * nodes, [], [None] * nodes
    for k in reversed(range(1, nodes)):
        act, d_inner, *others[k] = activate(
            k, nodes, (0, 1), place_ref, sums[k], arrived[k], w_in, owners, before
        )
        before = [act, d_inner]
    before = activate(0, nodes, (0,), place_ref, sums[0], near_far[0], w_in, owners, before)
    last = []
    for k in range(1, nodes):
        sending, mine = split(others[k], before)
        last.append([value for _, value in sending])
        blocks[k] = mine, exchange(sending)
    act, d_inner, *parts = activate(
        0, nodes, (1,), place_ref, sums[0], after(near_far[1], last), w_in, owners, before
    )
    sending, mine = split(parts)
    got = exchange(sending)
    sent = [value for _, value in sending]
    for k in range(1, nodes):
        value = add(*blocks[k]).astype(jnp.bfloat16)
        act, sent, value = lax.optimization_barrier((act, sent, value))
        blocks[k] = swap(value, "node", nodes, k).astype(jnp.float32)
    blocks[0] = add(mine, after(got, sent))
    high = place // owners

    def block_for(owner):
        chosen = blocks[0]
        for k in range(1, nodes):
            chosen = jnp.where((owner ^ node) == k, blocks[k], chosen)
        return chosen

    sent = [block_for(high ^ j).astype(jnp.bfloat16) for j in range(1, nodes)]
    act, d_inner = after((act, d_inner), sent)
    gate_grad, up_grad, down_grad = weight_grads(all_tokens, all_cots, act, d_inner)
    token_grad = block_for(high)
    for j in range(1, nodes):
        arrived = after(swap(sent[j - 1], "dp", width, j * owners), gate_grad)
        token_grad += arrived.astype(jnp.float32)
    token_grad = token_grad.astype(jnp.bfloat16)
    token_grad = jnp.concatenate([token_grad[:, :block], token_grad[:, block:]])
    return token_grad, gate_grad, up_grad, down_grad


def solution(mesh):
    return jax.shard_map(
        body,
        mesh=mesh,
        in_specs=(
            P("node", None),
            P("node", None),
            P("node", "dp"),
            P("node", "dp"),
            P("dp", "node"),
            P(None, "dp"),
            P(None, "dp"),
            P("dp", None),
        ),
        out_specs=(P("node", "dp"), P("node", "dp"), P("node", "dp"), P("dp", "node")),
        check_vma=False,
    )
```

```python
import functools

import jax
import jax.numpy as jnp
from jax import lax
from jax.experimental import pallas as pl
from jax.experimental.pallas import tpu as pltpu
from jax.sharding import PartitionSpec as P

QB = 128
STEP = 640
SIDE_BIT = 2
IN_HBM = pl.BlockSpec(memory_space=pltpu.HBM)
IN_VMEM = pl.BlockSpec(memory_space=pltpu.VMEM)
IN_SMEM = pl.BlockSpec(memory_space=pltpu.SMEM)


def contract(left, right):
    return lax.dot_general(
        left, right, (((0,), (0,)), ((), ())), preferred_element_type=jnp.float32
    )


def against(left, right):
    return lax.dot_general(
        left, right, (((1,), (1,)), ((), ())), preferred_element_type=jnp.float32
    )


def flipped(size, mask):
    return [(i, i ^ mask) for i in range(size)]


def swap(value, axis, size, mask):
    return lax.ppermute(value, axis, flipped(size, mask))


def in_hbm(array):
    return pltpu.with_memory_space_constraint(array, pltpu.HBM)


def in_vmem(array):
    return pltpu.with_memory_space_constraint(array, pltpu.VMEM)


def cost(operations):
    return pl.CostEstimate(flops=operations, transcendentals=0, bytes_accessed=0)


def grant(mebibytes):
    return pltpu.CompilerParams(vmem_limit_bytes=mebibytes * 1024 * 1024)


def side_of(place):
    return (place >> SIDE_BIT) & 1


def fetch_kernel(mask, node, place, tokens, cot, target, sem):
    half, rows = target.shape
    start = pl.multiple_of(side_of(place[0]) * half, 16)
    column = pl.multiple_of((node[0] ^ mask) * rows, 128)
    part = (pl.ds(start, half), pl.ds(column, rows))

    @pl.when((place[0] & 1) == 0)
    def _():
        copy = pltpu.make_async_copy(tokens.at[part], target, sem)
        copy.start()
        copy.wait()

    @pl.when((place[0] & 1) == 1)
    def _():
        copy = pltpu.make_async_copy(cot.at[part], target, sem)
        copy.start()
        copy.wait()


def fetch(mask, node, place, tokens, cot, shape):
    return pl.pallas_call(
        functools.partial(fetch_kernel, mask),
        in_specs=[IN_SMEM, IN_SMEM, IN_HBM, IN_HBM],
        out_specs=IN_VMEM,
        out_shape=pltpu.VMEM(shape, tokens.dtype),
        scratch_shapes=[pltpu.SemaphoreType.DMA],
        compiler_params=grant(10),
        cost_estimate=cost(0),
        name="fetch",
    )(node, place, in_hbm(tokens), in_hbm(cot))


def prepare_kernel(
    node, tokens, cot, gate_codes, up_codes, down_codes, gate_scales, up_scales, down_scales,
    all_tokens, all_cots, w_in, w_down, total, short, sems,
):
    rows, units = gate_codes.shape
    steps, per_step = rows // STEP, STEP // QB
    own = slice(0, tokens.shape[0])
    gate, up = slice(0, units), slice(units, 2 * units)

    def copies(step):
        column = pl.multiple_of(node[0] * rows + step * STEP, 128)
        part = pl.ds(pl.multiple_of(step * STEP, 128), STEP)
        pairs = (
            (gate_codes.at[part, :], w_in.at[part, gate]),
            (up_codes.at[part, :], w_in.at[part, up]),
            (tokens.at[:, pl.ds(column, STEP)], all_tokens.at[own, part]),
            (down_codes.at[:, part], w_down.at[:, part]),
            (cot.at[:, pl.ds(column, STEP)], all_cots.at[own, part]),
        )
        return [pltpu.make_async_copy(a, b, sems.at[step, i]) for i, (a, b) in enumerate(pairs)]

    for step in range(steps):
        for copy in copies(step):
            copy.start()
    total[...] = jnp.zeros(total.shape, total.dtype)

    def scale(weights, index, factor):
        weights[index] = (weights[index].astype(jnp.float32) * factor).astype(weights.dtype)

    def one(step, carry):
        for copy in copies(step):
            copy.wait()
        first_scale = (node[0] * steps + step) * per_step
        for j in range(per_step):
            part = pl.ds(pl.multiple_of(step * STEP + j * QB, QB), QB)
            row = pl.ds(first_scale + j, 1)
            scale(w_in, (part, gate), gate_scales[row, :])
            scale(w_in, (part, up), up_scales[row, :])
            scale(w_down, (slice(None), part), down_scales[step, :, j : j + 1])
        part = pl.ds(pl.multiple_of(step * STEP, 128), STEP)
        total[:, : 2 * units] += jnp.dot(all_tokens[own, part], w_in[part, :], preferred_element_type=jnp.float32)
        total[:, 2 * units :] += against(all_cots[own, part], w_down[:, part])
        return carry

    lax.fori_loop(0, steps, one, 0)
    short[...] = total[...].astype(short.dtype)


def prepare(nodes, node, tokens, cot, gate_codes, up_codes, down_codes, gate_scales, up_scales, down_scales):
    rows, units = gate_codes.shape
    count = tokens.shape[0]
    steps, per_step = rows // STEP, STEP // QB
    scales = lax.dynamic_slice_in_dim(down_scales, node[0] * (rows // QB), rows // QB, 1)
    scales = scales.reshape(units, steps, per_step).transpose(1, 0, 2)
    codes = jnp.bfloat16
    return pl.pallas_call(
        prepare_kernel,
        in_specs=[IN_SMEM] + [IN_HBM] * 5 + [IN_VMEM] * 3,
        out_specs=[IN_VMEM] * 6,
        out_shape=[
            pltpu.VMEM((nodes * count, rows), codes),
            pltpu.VMEM((nodes * count, rows), codes),
            pltpu.VMEM((rows, 2 * units), codes),
            pltpu.VMEM((units, rows), codes),
            pltpu.VMEM((count, 3 * units), jnp.float32),
            pltpu.VMEM((count, 3 * units), codes),
        ],
        scratch_shapes=[pltpu.SemaphoreType.DMA((steps, 5))],
        compiler_params=grant(10),
        cost_estimate=cost(0),
        name="prepare",
    )(
        node, *(in_hbm(a) for a in (tokens, cot, gate_codes, up_codes, down_codes)),
        gate_scales, up_scales, scales,
    )


def join_kernel(group, far, place, held, given, w_in, w_down, *refs):
    tokens, cot, total, short = refs[-4:]
    half, rows = held.shape
    units = w_down.shape[0]
    side = side_of(place[0])
    natural = (1 - side if far else side) * half
    mine = pl.ds(pl.multiple_of(2 * group * half + natural, 16), half)
    out = pl.ds(pl.multiple_of(natural, 16), half)

    @pl.when((place[0] & 1) == 0)
    def _():
        tokens[mine, :] = held[...]
        cot[mine, :] = given[...]

    @pl.when((place[0] & 1) == 1)
    def _():
        tokens[mine, :] = given[...]
        cot[mine, :] = held[...]

    for step in range(rows // STEP):
        part = slice(step * STEP, (step + 1) * STEP)
        inner = jnp.dot(tokens[mine, part], w_in[part, :], preferred_element_type=jnp.float32)
        outer = against(cot[mine, part], w_down[:, part])
        if step == 0:
            total[out, : 2 * units] = inner
            total[out, 2 * units :] = outer
        else:
            total[out, : 2 * units] += inner
            total[out, 2 * units :] += outer
    short[...] = total[out, :].astype(short.dtype)


def join(group, far, place, held, given, w_in, w_down, before):
    half, rows = held.shape
    units = w_down.shape[0]
    return pl.pallas_call(
        functools.partial(join_kernel, group, far),
        in_specs=[IN_SMEM] + [IN_VMEM] * (4 + len(before)),
        out_specs=[IN_VMEM] * 4,
        out_shape=[
            pltpu.VMEM(before[0].shape, jnp.bfloat16),
            pltpu.VMEM(before[1].shape, jnp.bfloat16),
            pltpu.VMEM((2 * half, 3 * units), jnp.float32),
            pltpu.VMEM((half, 3 * units), jnp.bfloat16),
        ],
        input_output_aliases={5 + i: i for i in range(len(before))},
        compiler_params=grant(10),
        cost_estimate=cost(0),
        name="join",
    )(place, *(in_vmem(a) for a in (held, given, w_in, w_down, *before)))


def activate_kernel(group, turns, count, blocks, place, weights, total, arrived, *refs):
    block = weights.shape[0] // blocks
    act, d_inner, *targets = refs[-2 - blocks // 2 :]
    units, half, chunk = act.shape[1], count // 2, 32
    side = side_of(place[0])

    def rows(first, length):
        return pl.ds(pl.multiple_of(first, 16), length)

    for turn in turns:
        natural = (1 - side if turn else side) * half
        for start in range(0, half, chunk):
            def of(array):
                return rows((natural if array.shape[0] == count else 0) + start, chunk)

            sums = total[of(total), :] + arrived[of(arrived), :].astype(jnp.float32)
            gate, upper, d_act = sums[:, :units], sums[:, units : 2 * units], sums[:, 2 * units :]
            sig = jax.nn.sigmoid(gate)
            silu_val = gate * sig
            kept = rows(group * count + natural + start, chunk)
            act[kept, :] = (silu_val * upper).astype(act.dtype)
            d_inner[kept, :units] = (d_act * upper * sig * (1.0 + gate * (1.0 - sig))).astype(d_inner.dtype)
            d_inner[kept, units:] = (d_act * silu_val).astype(d_inner.dtype)
    def block_rows(relative):
        bits = blocks.bit_length() - 1
        owner = 0
        for bit in range(bits):
            own = (place[0] >> bit) & 1
            owner += (own if (relative >> (bits - 1 - bit)) & 1 else 1 - own) << bit
        return weights[rows(owner * block, block), :]

    def store(h, mine):
        for p, target in enumerate(targets):
            pieces, places, width = [], [], 0
            for i in (0, 1):
                pad = ((2 * i + h) * block - width) % 128
                if pad:
                    pieces.append(weights[:pad, :])
                pieces.append(block_rows(2 * p + i))
                places.append(width + pad)
                width += pad + block
            product = against(mine, jnp.concatenate(pieces))
            for i in (0, 1):
                lanes = slice((2 * i + h) * block, (2 * i + h + 1) * block)
                target[:, lanes] = product[:, places[i] : places[i] + block].astype(target.dtype)

    for h in (0, 1):
        if len(turns) == 2:
            store(h, d_inner[rows(group * count + h * half, half), :])
        else:
            pl.when(natural == h * half)(lambda: store(h, d_inner[rows(group * count + h * half, half), :]))


def activate(group, groups, turns, place, total, arrived, weights, blocks, before):
    units, pairs = weights.shape[1] // 2, blocks // 2
    block = weights.shape[0] // blocks
    count = arrived.shape[0] * (3 - len(turns))
    terms = count // 2, 4 * block
    return pl.pallas_call(
        functools.partial(activate_kernel, group, turns, count, blocks),
        in_specs=[IN_SMEM] + [IN_VMEM] * (3 + len(before)),
        out_specs=[IN_VMEM] * (2 + pairs),
        out_shape=[
            pltpu.VMEM((groups * count, units), jnp.bfloat16),
            pltpu.VMEM((groups * count, 2 * units), jnp.bfloat16),
        ]
        + [pltpu.VMEM(terms, jnp.bfloat16)] * (pairs // 2)
        + [pltpu.VMEM(terms, jnp.float32)] * (pairs // 2),
        input_output_aliases={4 + i: i for i in range(len(before))},
        compiler_params=grant(10),
        cost_estimate=cost(0),
        name="activate",
    )(place, *(in_vmem(a) for a in (weights, total, arrived, *before)))


def grads_kernel(tokens, cot, act, d_inner, gate_grad, up_grad, down_grad, gate_held, up_held, down_held, sems):
    rows, units = gate_grad.shape
    copies = []

    def send(held, target, part, i):
        copies.append(pltpu.make_async_copy(held.at[part], target.at[part], sems.at[i]))
        copies[-1].start()

    steps = rows // STEP
    for step in range(steps):
        part = slice(step * STEP, (step + 1) * STEP)
        both = contract(tokens[:, part], d_inner[...])
        gate_held[part, :] = both[:, :units].astype(gate_held.dtype)
        send(gate_held, gate_grad, (part, slice(None)), step)
        up_held[part, :] = both[:, units:].astype(up_held.dtype)
        send(up_held, up_grad, (part, slice(None)), steps + step)
    for step in range(steps):
        part = slice(step * STEP, (step + 1) * STEP)
        down_held[:, part] = contract(act[...], cot[:, part]).astype(down_held.dtype)
        send(down_held, down_grad, (slice(None), part), 2 * steps + step)
    for copy in copies:
        copy.wait()


def weight_grads(tokens, cot, act, d_inner):
    rows, units = tokens.shape[1], act.shape[1]
    shapes = [(rows, units), (rows, units), (units, rows)]
    return pl.pallas_call(
        grads_kernel,
        in_specs=[IN_VMEM] * 4,
        out_specs=[IN_HBM] * 3,
        out_shape=[pltpu.HBM(shape, jnp.bfloat16) for shape in shapes],
        scratch_shapes=[pltpu.VMEM(shape, jnp.bfloat16) for shape in shapes]
        + [pltpu.SemaphoreType.DMA((3 * (rows // STEP),))],
        compiler_params=grant(10),
        cost_estimate=cost(6 * tokens.shape[0] * rows * units),
        name="weight_grads",
    )(*(in_vmem(a) for a in (tokens, cot, act, d_inner)))


def after(value, *earlier):
    return lax.optimization_barrier((value, earlier))[0]


def body(tokens, cotangent, gate_codes, up_codes, down_codes, gate_scales, up_scales, down_scales):
    nodes, width = lax.axis_size("node"), lax.axis_size("dp")
    node, place = lax.axis_index("node"), lax.axis_index("dp")
    node_ref, place_ref = node.reshape(1), place.reshape(1)
    rows, units = gate_codes.shape
    count = tokens.shape[0]
    owners = width // nodes
    bits = owners.bit_length() - 1
    block = rows // owners

    side, half = side_of(place), count // 2

    def halves(array):
        return [lax.dynamic_slice_in_dim(array, s * half, half, 0) for s in (side, 1 - side)]

    fetched = [
        swap(fetch(k, node_ref, place_ref, tokens, cotangent, (half, rows)), "node", nodes, k)
        for k in range(1, nodes)
    ]
    all_tokens, all_cots, w_in, w_down, own_sums, own_short = prepare(
        nodes, node_ref, tokens, cotangent, gate_codes, up_codes, down_codes, gate_scales, up_scales, down_scales
    )
    fetched = after(fetched, own_short)

    sums, shorts = [own_sums], [None]
    for k, mine in enumerate(fetched, 1):
        given = swap(mine, "dp", width, 1)
        beside = swap(mine, "dp", width, 1 << SIDE_BIT)
        before, near_far = [all_tokens, all_cots], []
        for far, held in enumerate((mine, beside)):
            if far:
                given = swap(held, "dp", width, 1)
            *before, short = join(k, far, place_ref, held, given, w_in, w_down, before)
            near_far.append(short)
        all_tokens, all_cots, total = before
        sums.append(total)
        shorts.append(near_far)

    mask = 1
    if nodes > 2:
        while mask < nodes // 2:
            sent = [swap(s.astype(jnp.bfloat16), "node", nodes, mask) for s in sums]
            sums = [s + sent[k ^ mask].astype(jnp.float32) for k, s in enumerate(sums)]
            mask *= 2
        own_short = sums[0].astype(jnp.bfloat16)
        shorts = [halves(s.astype(jnp.bfloat16)) for s in sums]
    near_far = [swap(s, "node", nodes, mask) for s in shorts[mask]]
    arrived = [None]
    for k in range(1, nodes):
        short = own_short if k == mask else sums[k ^ mask].astype(jnp.bfloat16)
        arrived.append(swap(short, "node", nodes, mask))

    peers = owners // 2

    def split(parts, *earlier):
        size = len(parts) // 2
        got = [swap(part, "dp", width, 1) for part in parts[:size]]
        if earlier:
            got = after(got, *earlier)
        sending = []
        for r in range(peers):
            lanes = slice(r % 2 * 2 * block, (r % 2 + 1) * 2 * block)
            both = parts[size + r // 2][:, lanes] + got[r // 2][:, lanes].astype(jnp.float32)
            if r < peers - 1:
                mask = sum(1 << bit for bit in range(1, bits) if (r >> (bits - 1 - bit)) & 1 == 0)
                sending.append((mask, both.astype(jnp.bfloat16)))
        return sending, both

    def exchange(sending):
        return [swap(value, "dp", width, mask) for mask, value in sending]

    def add(mine, got):
        for value in got:
            mine += value.astype(jnp.float32)
        return mine

    blocks, before, others = [None] * nodes, [], [None] * nodes
    for k in reversed(range(1, nodes)):
        act, d_inner, *others[k] = activate(
            k, nodes, (0, 1), place_ref, sums[k], arrived[k], w_in, owners, before
        )
        before = [act, d_inner]
    before = activate(0, nodes, (0,), place_ref, sums[0], near_far[0], w_in, owners, before)
    last = []
    for k in range(1, nodes):
        sending, mine = split(others[k], before)
        last.append([value for _, value in sending])
        blocks[k] = mine, exchange(sending)
    act, d_inner, *parts = activate(
        0, nodes, (1,), place_ref, sums[0], after(near_far[1], last), w_in, owners, before
    )
    sending, mine = split(parts)
    got = exchange(sending)
    sent = [value for _, value in sending]
    for k in range(1, nodes):
        value = add(*blocks[k]).astype(jnp.bfloat16)
        act, sent, value = lax.optimization_barrier((act, sent, value))
        blocks[k] = swap(value, "node", nodes, k).astype(jnp.float32)
    blocks[0] = add(mine, after(got, sent))
    high = place // owners

    def block_for(owner):
        chosen = blocks[0]
        for k in range(1, nodes):
            chosen = jnp.where((owner ^ node) == k, blocks[k], chosen)
        return chosen

    sent = [block_for(high ^ j).astype(jnp.bfloat16) for j in range(1, nodes)]
    act, d_inner = after((act, d_inner), sent)
    gate_grad, up_grad, down_grad = weight_grads(all_tokens, all_cots, act, d_inner)
    token_grad = block_for(high)
    for j in range(1, nodes):
        arrived = after(swap(sent[j - 1], "dp", width, j * owners), gate_grad)
        token_grad += arrived.astype(jnp.float32)
    token_grad = token_grad.astype(jnp.bfloat16)
    token_grad = jnp.concatenate([token_grad[:, :block], token_grad[:, block:]])
    return token_grad, gate_grad, up_grad, down_grad


def solution(mesh):
    return jax.shard_map(
        body,
        mesh=mesh,
        in_specs=(
            P("node", None),
            P("node", None),
            P("node", "dp"),
            P("node", "dp"),
            P("dp", "node"),
            P(None, "dp"),
            P(None, "dp"),
            P("dp", None),
        ),
        out_specs=(P("node", "dp"), P("node", "dp"), P("node", "dp"), P("dp", "node")),
        check_vma=False,
    )
```

```python
import functools

import jax
import jax.numpy as jnp
from jax import lax
from jax.experimental import pallas as pl
from jax.experimental.pallas import tpu as pltpu
from jax.sharding import PartitionSpec as P

QB = 128
STEP = 640
SIDE_BIT = 2
IN_HBM = pl.BlockSpec(memory_space=pltpu.HBM)
IN_VMEM = pl.BlockSpec(memory_space=pltpu.VMEM)
IN_SMEM = pl.BlockSpec(memory_space=pltpu.SMEM)


def contract(left, right):
    return lax.dot_general(
        left, right, (((0,), (0,)), ((), ())), preferred_element_type=jnp.float32
    )


def against(left, right):
    return lax.dot_general(
        left, right, (((1,), (1,)), ((), ())), preferred_element_type=jnp.float32
    )


def flipped(size, mask):
    return [(i, i ^ mask) for i in range(size)]


def swap(value, axis, size, mask):
    return lax.ppermute(value, axis, flipped(size, mask))


def in_hbm(array):
    return pltpu.with_memory_space_constraint(array, pltpu.HBM)


def in_vmem(array):
    return pltpu.with_memory_space_constraint(array, pltpu.VMEM)


def cost(operations):
    return pl.CostEstimate(flops=operations, transcendentals=0, bytes_accessed=0)


def grant(mebibytes):
    return pltpu.CompilerParams(vmem_limit_bytes=mebibytes * 1024 * 1024)


def side_of(place):
    return (place >> SIDE_BIT) & 1


def fetch_kernel(mask, node, place, tokens, cot, target, sem):
    half, rows = target.shape
    start = pl.multiple_of(side_of(place[0]) * half, 16)
    column = pl.multiple_of((node[0] ^ mask) * rows, 128)
    part = (pl.ds(start, half), pl.ds(column, rows))

    @pl.when((place[0] & 1) == 0)
    def _():
        copy = pltpu.make_async_copy(tokens.at[part], target, sem)
        copy.start()
        copy.wait()

    @pl.when((place[0] & 1) == 1)
    def _():
        copy = pltpu.make_async_copy(cot.at[part], target, sem)
        copy.start()
        copy.wait()


def fetch(mask, node, place, tokens, cot, shape):
    return pl.pallas_call(
        functools.partial(fetch_kernel, mask),
        in_specs=[IN_SMEM, IN_SMEM, IN_HBM, IN_HBM],
        out_specs=IN_VMEM,
        out_shape=pltpu.VMEM(shape, tokens.dtype),
        scratch_shapes=[pltpu.SemaphoreType.DMA],
        compiler_params=grant(10),
        cost_estimate=cost(0),
        name="fetch",
    )(node, place, in_hbm(tokens), in_hbm(cot))


def prepare_kernel(
    node, tokens, cot, gate_codes, up_codes, down_codes, gate_scales, up_scales, down_scales,
    all_tokens, all_cots, w_in, w_down, total, short, sems,
):
    rows, units = gate_codes.shape
    steps, per_step = rows // STEP, STEP // QB
    own = slice(0, tokens.shape[0])
    gate, up = slice(0, units), slice(units, 2 * units)

    def copies(step):
        column = pl.multiple_of(node[0] * rows + step * STEP, 128)
        part = pl.ds(pl.multiple_of(step * STEP, 128), STEP)
        pairs = (
            (gate_codes.at[part, :], w_in.at[part, gate]),
            (up_codes.at[part, :], w_in.at[part, up]),
            (tokens.at[:, pl.ds(column, STEP)], all_tokens.at[own, part]),
            (down_codes.at[:, part], w_down.at[:, part]),
            (cot.at[:, pl.ds(column, STEP)], all_cots.at[own, part]),
        )
        return [pltpu.make_async_copy(a, b, sems.at[step, i]) for i, (a, b) in enumerate(pairs)]

    for step in range(steps):
        for copy in copies(step):
            copy.start()
    total[...] = jnp.zeros(total.shape, total.dtype)

    def scale(weights, index, factor):
        weights[index] = (weights[index].astype(jnp.float32) * factor).astype(weights.dtype)

    def one(step, carry):
        for copy in copies(step):
            copy.wait()
        first_scale = (node[0] * steps + step) * per_step
        for j in range(per_step):
            part = pl.ds(pl.multiple_of(step * STEP + j * QB, QB), QB)
            row = pl.ds(first_scale + j, 1)
            scale(w_in, (part, gate), gate_scales[row, :])
            scale(w_in, (part, up), up_scales[row, :])
            scale(w_down, (slice(None), part), down_scales[step, :, j : j + 1])
        part = pl.ds(pl.multiple_of(step * STEP, 128), STEP)
        total[:, : 2 * units] += jnp.dot(all_tokens[own, part], w_in[part, :], preferred_element_type=jnp.float32)
        total[:, 2 * units :] += against(all_cots[own, part], w_down[:, part])
        return carry

    lax.fori_loop(0, steps, one, 0)
    short[...] = total[...].astype(short.dtype)


def prepare(nodes, node, tokens, cot, gate_codes, up_codes, down_codes, gate_scales, up_scales, down_scales):
    rows, units = gate_codes.shape
    count = tokens.shape[0]
    steps, per_step = rows // STEP, STEP // QB
    scales = lax.dynamic_slice_in_dim(down_scales, node[0] * (rows // QB), rows // QB, 1)
    scales = scales.reshape(units, steps, per_step).transpose(1, 0, 2)
    codes = jnp.bfloat16
    return pl.pallas_call(
        prepare_kernel,
        in_specs=[IN_SMEM] + [IN_HBM] * 5 + [IN_VMEM] * 3,
        out_specs=[IN_VMEM] * 6,
        out_shape=[
            pltpu.VMEM((nodes * count, rows), codes),
            pltpu.VMEM((nodes * count, rows), codes),
            pltpu.VMEM((rows, 2 * units), codes),
            pltpu.VMEM((units, rows), codes),
            pltpu.VMEM((count, 3 * units), jnp.float32),
            pltpu.VMEM((count, 3 * units), codes),
        ],
        scratch_shapes=[pltpu.SemaphoreType.DMA((steps, 5))],
        compiler_params=grant(10),
        cost_estimate=cost(0),
        name="prepare",
    )(
        node, *(in_hbm(a) for a in (tokens, cot, gate_codes, up_codes, down_codes)),
        gate_scales, up_scales, scales,
    )


def join_kernel(group, far, place, held, given, w_in, w_down, *refs):
    tokens, cot, total, short = refs[-4:]
    half, rows = held.shape
    units = w_down.shape[0]
    side = side_of(place[0])
    natural = (1 - side if far else side) * half
    mine = pl.ds(pl.multiple_of(2 * group * half + natural, 16), half)
    out = pl.ds(pl.multiple_of(natural, 16), half)

    @pl.when((place[0] & 1) == 0)
    def _():
        tokens[mine, :] = held[...]
        cot[mine, :] = given[...]

    @pl.when((place[0] & 1) == 1)
    def _():
        tokens[mine, :] = given[...]
        cot[mine, :] = held[...]

    for step in range(rows // STEP):
        part = slice(step * STEP, (step + 1) * STEP)
        inner = jnp.dot(tokens[mine, part], w_in[part, :], preferred_element_type=jnp.float32)
        outer = against(cot[mine, part], w_down[:, part])
        if step == 0:
            total[out, : 2 * units] = inner
            total[out, 2 * units :] = outer
        else:
            total[out, : 2 * units] += inner
            total[out, 2 * units :] += outer
    short[...] = total[out, :].astype(short.dtype)


def join(group, far, place, held, given, w_in, w_down, before):
    half, rows = held.shape
    units = w_down.shape[0]
    return pl.pallas_call(
        functools.partial(join_kernel, group, far),
        in_specs=[IN_SMEM] + [IN_VMEM] * (4 + len(before)),
        out_specs=[IN_VMEM] * 4,
        out_shape=[
            pltpu.VMEM(before[0].shape, jnp.bfloat16),
            pltpu.VMEM(before[1].shape, jnp.bfloat16),
            pltpu.VMEM((2 * half, 3 * units), jnp.float32),
            pltpu.VMEM((half, 3 * units), jnp.bfloat16),
        ],
        input_output_aliases={5 + i: i for i in range(len(before))},
        compiler_params=grant(10),
        cost_estimate=cost(0),
        name="join",
    )(place, *(in_vmem(a) for a in (held, given, w_in, w_down, *before)))


def activate_kernel(group, turns, count, blocks, place, weights, total, arrived, *refs):
    block = weights.shape[0] // blocks
    act, d_inner, *targets = refs[-2 - blocks // 2 :]
    units, half, chunk = act.shape[1], count // 2, 32
    side = side_of(place[0])

    def rows(first, length):
        return pl.ds(pl.multiple_of(first, 16), length)

    for turn in turns:
        natural = (1 - side if turn else side) * half
        for start in range(0, half, chunk):
            def of(array):
                return rows((natural if array.shape[0] == count else 0) + start, chunk)

            sums = total[of(total), :] + arrived[of(arrived), :].astype(jnp.float32)
            gate, upper, d_act = sums[:, :units], sums[:, units : 2 * units], sums[:, 2 * units :]
            sig = jax.nn.sigmoid(gate)
            silu_val = gate * sig
            kept = rows(group * count + natural + start, chunk)
            act[kept, :] = (silu_val * upper).astype(act.dtype)
            d_inner[kept, :units] = (d_act * upper * sig * (1.0 + gate * (1.0 - sig))).astype(d_inner.dtype)
            d_inner[kept, units:] = (d_act * silu_val).astype(d_inner.dtype)
    def block_rows(relative):
        bits = blocks.bit_length() - 1
        owner = 0
        for bit in range(bits):
            own = (place[0] >> bit) & 1
            owner += (own if (relative >> (bits - 1 - bit)) & 1 else 1 - own) << bit
        return weights[rows(owner * block, block), :]

    def store(h, mine):
        for p, target in enumerate(targets):
            pieces, places, width = [], [], 0
            for i in (0, 1):
                pad = ((2 * i + h) * block - width) % 128
                if pad:
                    pieces.append(weights[:pad, :])
                pieces.append(block_rows(2 * p + i))
                places.append(width + pad)
                width += pad + block
            product = against(mine, jnp.concatenate(pieces))
            for i in (0, 1):
                lanes = slice((2 * i + h) * block, (2 * i + h + 1) * block)
                target[:, lanes] = product[:, places[i] : places[i] + block].astype(target.dtype)

    for h in (0, 1):
        if len(turns) == 2:
            store(h, d_inner[rows(group * count + h * half, half), :])
        else:
            pl.when(natural == h * half)(lambda: store(h, d_inner[rows(group * count + h * half, half), :]))


def activate(group, groups, turns, place, total, arrived, weights, blocks, before):
    units, pairs = weights.shape[1] // 2, blocks // 2
    block = weights.shape[0] // blocks
    count = arrived.shape[0] * (3 - len(turns))
    terms = count // 2, 4 * block
    return pl.pallas_call(
        functools.partial(activate_kernel, group, turns, count, blocks),
        in_specs=[IN_SMEM] + [IN_VMEM] * (3 + len(before)),
        out_specs=[IN_VMEM] * (2 + pairs),
        out_shape=[
            pltpu.VMEM((groups * count, units), jnp.bfloat16),
            pltpu.VMEM((groups * count, 2 * units), jnp.bfloat16),
        ]
        + [pltpu.VMEM(terms, jnp.bfloat16)] * (pairs // 2)
        + [pltpu.VMEM(terms, jnp.float32)] * (pairs // 2),
        input_output_aliases={4 + i: i for i in range(len(before))},
        compiler_params=grant(10),
        cost_estimate=cost(0),
        name="activate",
    )(place, *(in_vmem(a) for a in (weights, total, arrived, *before)))


def grads_kernel(tokens, cot, act, d_inner, gate_grad, up_grad, down_grad, gate_held, up_held, down_held, sems):
    rows, units = gate_grad.shape
    copies = []

    def send(held, target, part, i):
        copies.append(pltpu.make_async_copy(held.at[part], target.at[part], sems.at[i]))
        copies[-1].start()

    steps = rows // STEP
    for step in range(steps):
        part = slice(step * STEP, (step + 1) * STEP)
        both = contract(tokens[:, part], d_inner[...])
        gate_held[part, :] = both[:, :units].astype(gate_held.dtype)
        send(gate_held, gate_grad, (part, slice(None)), step)
        up_held[part, :] = both[:, units:].astype(up_held.dtype)
        send(up_held, up_grad, (part, slice(None)), steps + step)
    for step in range(steps):
        part = slice(step * STEP, (step + 1) * STEP)
        down_held[:, part] = contract(act[...], cot[:, part]).astype(down_held.dtype)
        send(down_held, down_grad, (slice(None), part), 2 * steps + step)
    for copy in copies:
        copy.wait()


def weight_grads(tokens, cot, act, d_inner):
    rows, units = tokens.shape[1], act.shape[1]
    shapes = [(rows, units), (rows, units), (units, rows)]
    return pl.pallas_call(
        grads_kernel,
        in_specs=[IN_VMEM] * 4,
        out_specs=[IN_HBM] * 3,
        out_shape=[pltpu.HBM(shape, jnp.bfloat16) for shape in shapes],
        scratch_shapes=[pltpu.VMEM(shape, jnp.bfloat16) for shape in shapes]
        + [pltpu.SemaphoreType.DMA((3 * (rows // STEP),))],
        compiler_params=grant(10),
        cost_estimate=cost(6 * tokens.shape[0] * rows * units),
        name="weight_grads",
    )(*(in_vmem(a) for a in (tokens, cot, act, d_inner)))


def after(value, *earlier):
    return lax.optimization_barrier((value, earlier))[0]


def body(tokens, cotangent, gate_codes, up_codes, down_codes, gate_scales, up_scales, down_scales):
    nodes, width = lax.axis_size("node"), lax.axis_size("dp")
    node, place = lax.axis_index("node"), lax.axis_index("dp")
    node_ref, place_ref = node.reshape(1), place.reshape(1)
    rows, units = gate_codes.shape
    count = tokens.shape[0]
    owners = width // nodes
    bits = owners.bit_length() - 1
    block = rows // owners

    side, half = side_of(place), count // 2

    def halves(array):
        return [lax.dynamic_slice_in_dim(array, s * half, half, 0) for s in (side, 1 - side)]

    fetched = [
        swap(fetch(k, node_ref, place_ref, tokens, cotangent, (half, rows)), "node", nodes, k)
        for k in range(1, nodes)
    ]
    all_tokens, all_cots, w_in, w_down, own_sums, own_short = prepare(
        nodes, node_ref, tokens, cotangent, gate_codes, up_codes, down_codes, gate_scales, up_scales, down_scales
    )
    fetched = after(fetched, own_short)

    sums, shorts = [own_sums], [None]
    for k, mine in enumerate(fetched, 1):
        given = swap(mine, "dp", width, 1)
        beside = swap(mine, "dp", width, 1 << SIDE_BIT)
        before, near_far = [all_tokens, all_cots], []
        for far, held in enumerate((mine, beside)):
            if far:
                given = swap(held, "dp", width, 1)
            *before, short = join(k, far, place_ref, held, given, w_in, w_down, before)
            near_far.append(short)
        all_tokens, all_cots, total = before
        sums.append(total)
        shorts.append(near_far)

    mask = 1
    if nodes > 2:
        while mask < nodes // 2:
            sent = [swap(s.astype(jnp.bfloat16), "node", nodes, mask) for s in sums]
            sums = [s + sent[k ^ mask].astype(jnp.float32) for k, s in enumerate(sums)]
            mask *= 2
        own_short = sums[0].astype(jnp.bfloat16)
        shorts = [halves(s.astype(jnp.bfloat16)) for s in sums]
    near_far = [swap(s, "node", nodes, mask) for s in shorts[mask]]
    arrived = [None]
    for k in range(1, nodes):
        short = own_short if k == mask else sums[k ^ mask].astype(jnp.bfloat16)
        arrived.append(swap(short, "node", nodes, mask))

    peers = owners // 2

    def split(parts, *earlier):
        size = len(parts) // 2
        got = [swap(part, "dp", width, 1) for part in parts[:size]]
        if earlier:
            got = after(got, *earlier)
        sending = []
        for r in range(peers):
            lanes = slice(r % 2 * 2 * block, (r % 2 + 1) * 2 * block)
            both = parts[size + r // 2][:, lanes] + got[r // 2][:, lanes].astype(jnp.float32)
            if r < peers - 1:
                mask = sum(1 << bit for bit in range(1, bits) if (r >> (bits - 1 - bit)) & 1 == 0)
                sending.append((mask, both.astype(jnp.bfloat16)))
        return sending, both

    def exchange(sending):
        return [swap(value, "dp", width, mask) for mask, value in sending]

    def add(mine, got):
        for value in got:
            mine += value.astype(jnp.float32)
        return mine

    blocks, before, others = [None] * nodes, [], [None] * nodes
    for k in reversed(range(1, nodes)):
        act, d_inner, *others[k] = activate(
            k, nodes, (0, 1), place_ref, sums[k], arrived[k], w_in, owners, before
        )
        before = [act, d_inner]
    before = activate(0, nodes, (0,), place_ref, sums[0], near_far[0], w_in, owners, before)
    last = []
    for k in range(1, nodes):
        sending, mine = split(others[k], before)
        last.append([value for _, value in sending])
        blocks[k] = mine, exchange(sending)
    act, d_inner, *parts = activate(
        0, nodes, (1,), place_ref, sums[0], after(near_far[1], last), w_in, owners, before
    )
    sending, mine = split(parts)
    got = exchange(sending)
    sent = [value for _, value in sending]
    for k in range(1, nodes):
        value = add(*blocks[k]).astype(jnp.bfloat16)
        act, sent, value = lax.optimization_barrier((act, sent, value))
        blocks[k] = swap(value, "node", nodes, k).astype(jnp.float32)
    act, d_inner = after((act, d_inner), sent, value)
    gate_grad, up_grad, down_grad = weight_grads(all_tokens, all_cots, act, d_inner)
    blocks[0] = add(mine, after(got, gate_grad))
    high = place // owners

    def block_for(owner):
        chosen = blocks[0]
        for k in range(1, nodes):
            chosen = jnp.where((owner ^ node) == k, blocks[k], chosen)
        return chosen

    token_grad = block_for(high)
    for j in range(1, nodes):
        token_grad += swap(block_for(high ^ j).astype(jnp.bfloat16), "dp", width, j * owners).astype(jnp.float32)
    token_grad = token_grad.astype(jnp.bfloat16)
    token_grad = jnp.concatenate([token_grad[:, :block], token_grad[:, block:]])
    return token_grad, gate_grad, up_grad, down_grad


def solution(mesh):
    return jax.shard_map(
        body,
        mesh=mesh,
        in_specs=(
            P("node", None),
            P("node", None),
            P("node", "dp"),
            P("node", "dp"),
            P("dp", "node"),
            P(None, "dp"),
            P(None, "dp"),
            P("dp", None),
        ),
        out_specs=(P("node", "dp"), P("node", "dp"), P("node", "dp"), P("dp", "node")),
        check_vma=False,
    )
```

```python
import functools

import jax
import jax.numpy as jnp
from jax import lax
from jax.experimental import pallas as pl
from jax.experimental.pallas import tpu as pltpu
from jax.sharding import PartitionSpec as P

QB = 128
STEP = 640
SIDE_BIT = 2
IN_HBM = pl.BlockSpec(memory_space=pltpu.HBM)
IN_VMEM = pl.BlockSpec(memory_space=pltpu.VMEM)
IN_SMEM = pl.BlockSpec(memory_space=pltpu.SMEM)


def contract(left, right):
    return lax.dot_general(
        left, right, (((0,), (0,)), ((), ())), preferred_element_type=jnp.float32
    )


def against(left, right):
    return lax.dot_general(
        left, right, (((1,), (1,)), ((), ())), preferred_element_type=jnp.float32
    )


def flipped(size, mask):
    return [(i, i ^ mask) for i in range(size)]


def swap(value, axis, size, mask):
    return lax.ppermute(value, axis, flipped(size, mask))


def in_hbm(array):
    return pltpu.with_memory_space_constraint(array, pltpu.HBM)


def in_vmem(array):
    return pltpu.with_memory_space_constraint(array, pltpu.VMEM)


def cost(operations):
    return pl.CostEstimate(flops=operations, transcendentals=0, bytes_accessed=0)


def grant(mebibytes):
    return pltpu.CompilerParams(vmem_limit_bytes=mebibytes * 1024 * 1024)


def side_of(place):
    return (place >> SIDE_BIT) & 1


def fetch_kernel(mask, node, place, tokens, cot, target, sem):
    half, rows = target.shape
    start = pl.multiple_of(side_of(place[0]) * half, 16)
    column = pl.multiple_of((node[0] ^ mask) * rows, 128)
    part = (pl.ds(start, half), pl.ds(column, rows))

    @pl.when((place[0] & 1) == 0)
    def _():
        copy = pltpu.make_async_copy(tokens.at[part], target, sem)
        copy.start()
        copy.wait()

    @pl.when((place[0] & 1) == 1)
    def _():
        copy = pltpu.make_async_copy(cot.at[part], target, sem)
        copy.start()
        copy.wait()


def fetch(mask, node, place, tokens, cot, shape):
    return pl.pallas_call(
        functools.partial(fetch_kernel, mask),
        in_specs=[IN_SMEM, IN_SMEM, IN_HBM, IN_HBM],
        out_specs=IN_VMEM,
        out_shape=pltpu.VMEM(shape, tokens.dtype),
        scratch_shapes=[pltpu.SemaphoreType.DMA],
        compiler_params=grant(10),
        cost_estimate=cost(0),
        name="fetch",
    )(node, place, in_hbm(tokens), in_hbm(cot))


def prepare_kernel(
    node, tokens, cot, gate_codes, up_codes, down_codes, gate_scales, up_scales, down_scales,
    all_tokens, all_cots, w_in, w_down, total, short, sems,
):
    rows, units = gate_codes.shape
    steps, per_step = rows // STEP, STEP // QB
    own = slice(0, tokens.shape[0])
    gate, up = slice(0, units), slice(units, 2 * units)

    def copies(step):
        column = pl.multiple_of(node[0] * rows + step * STEP, 128)
        part = pl.ds(pl.multiple_of(step * STEP, 128), STEP)
        pairs = (
            (gate_codes.at[part, :], w_in.at[part, gate]),
            (up_codes.at[part, :], w_in.at[part, up]),
            (tokens.at[:, pl.ds(column, STEP)], all_tokens.at[own, part]),
            (down_codes.at[:, part], w_down.at[:, part]),
            (cot.at[:, pl.ds(column, STEP)], all_cots.at[own, part]),
        )
        return [pltpu.make_async_copy(a, b, sems.at[step, i]) for i, (a, b) in enumerate(pairs)]

    for step in range(steps):
        for copy in copies(step):
            copy.start()
    total[...] = jnp.zeros(total.shape, total.dtype)

    def scale(weights, index, factor):
        weights[index] = (weights[index].astype(jnp.float32) * factor).astype(weights.dtype)

    def one(step, carry):
        for copy in copies(step):
            copy.wait()
        first_scale = (node[0] * steps + step) * per_step
        for j in range(per_step):
            part = pl.ds(pl.multiple_of(step * STEP + j * QB, QB), QB)
            row = pl.ds(first_scale + j, 1)
            scale(w_in, (part, gate), gate_scales[row, :])
            scale(w_in, (part, up), up_scales[row, :])
            scale(w_down, (slice(None), part), down_scales[step, :, j : j + 1])
        part = pl.ds(pl.multiple_of(step * STEP, 128), STEP)
        total[:, : 2 * units] += jnp.dot(all_tokens[own, part], w_in[part, :], preferred_element_type=jnp.float32)
        total[:, 2 * units :] += against(all_cots[own, part], w_down[:, part])
        return carry

    lax.fori_loop(0, steps, one, 0)
    short[...] = total[...].astype(short.dtype)


def prepare(nodes, node, tokens, cot, gate_codes, up_codes, down_codes, gate_scales, up_scales, down_scales):
    rows, units = gate_codes.shape
    count = tokens.shape[0]
    steps, per_step = rows // STEP, STEP // QB
    scales = lax.dynamic_slice_in_dim(down_scales, node[0] * (rows // QB), rows // QB, 1)
    scales = scales.reshape(units, steps, per_step).transpose(1, 0, 2)
    codes = jnp.bfloat16
    return pl.pallas_call(
        prepare_kernel,
        in_specs=[IN_SMEM] + [IN_HBM] * 5 + [IN_VMEM] * 3,
        out_specs=[IN_VMEM] * 6,
        out_shape=[
            pltpu.VMEM((nodes * count, rows), codes),
            pltpu.VMEM((nodes * count, rows), codes),
            pltpu.VMEM((rows, 2 * units), codes),
            pltpu.VMEM((units, rows), codes),
            pltpu.VMEM((count, 3 * units), jnp.float32),
            pltpu.VMEM((count, 3 * units), codes),
        ],
        scratch_shapes=[pltpu.SemaphoreType.DMA((steps, 5))],
        compiler_params=grant(10),
        cost_estimate=cost(0),
        name="prepare",
    )(
        node, *(in_hbm(a) for a in (tokens, cot, gate_codes, up_codes, down_codes)),
        gate_scales, up_scales, scales,
    )


def join_kernel(group, far, place, held, given, w_in, w_down, *refs):
    tokens, cot, total, short = refs[-4:]
    half, rows = held.shape
    units = w_down.shape[0]
    side = side_of(place[0])
    natural = (1 - side if far else side) * half
    mine = pl.ds(pl.multiple_of(2 * group * half + natural, 16), half)
    out = pl.ds(pl.multiple_of(natural, 16), half)

    @pl.when((place[0] & 1) == 0)
    def _():
        tokens[mine, :] = held[...]
        cot[mine, :] = given[...]

    @pl.when((place[0] & 1) == 1)
    def _():
        tokens[mine, :] = given[...]
        cot[mine, :] = held[...]

    for step in range(rows // STEP):
        part = slice(step * STEP, (step + 1) * STEP)
        inner = jnp.dot(tokens[mine, part], w_in[part, :], preferred_element_type=jnp.float32)
        outer = against(cot[mine, part], w_down[:, part])
        if step == 0:
            total[out, : 2 * units] = inner
            total[out, 2 * units :] = outer
        else:
            total[out, : 2 * units] += inner
            total[out, 2 * units :] += outer
    short[...] = total[out, :].astype(short.dtype)


def join(group, far, place, held, given, w_in, w_down, before):
    half, rows = held.shape
    units = w_down.shape[0]
    return pl.pallas_call(
        functools.partial(join_kernel, group, far),
        in_specs=[IN_SMEM] + [IN_VMEM] * (4 + len(before)),
        out_specs=[IN_VMEM] * 4,
        out_shape=[
            pltpu.VMEM(before[0].shape, jnp.bfloat16),
            pltpu.VMEM(before[1].shape, jnp.bfloat16),
            pltpu.VMEM((2 * half, 3 * units), jnp.float32),
            pltpu.VMEM((half, 3 * units), jnp.bfloat16),
        ],
        input_output_aliases={5 + i: i for i in range(len(before))},
        compiler_params=grant(10),
        cost_estimate=cost(0),
        name="join",
    )(place, *(in_vmem(a) for a in (held, given, w_in, w_down, *before)))


def activate_kernel(group, turns, count, blocks, place, weights, total, arrived, *refs):
    block = weights.shape[0] // blocks
    act, d_inner, _, _, *targets = refs[-4 - blocks // 2 :]
    units, half, chunk = act.shape[1], count // 2, 32
    side = side_of(place[0])

    def rows(first, length):
        return pl.ds(pl.multiple_of(first, 16), length)

    for turn in turns:
        natural = (1 - side if turn else side) * half
        for start in range(0, half, chunk):
            def of(array):
                return rows((natural if array.shape[0] == count else 0) + start, chunk)

            sums = total[of(total), :] + arrived[of(arrived), :].astype(jnp.float32)
            gate, upper, d_act = sums[:, :units], sums[:, units : 2 * units], sums[:, 2 * units :]
            sig = jax.nn.sigmoid(gate)
            silu_val = gate * sig
            kept = rows(group * count + natural + start, chunk)
            act[kept, :] = (silu_val * upper).astype(act.dtype)
            d_inner[kept, :units] = (d_act * upper * sig * (1.0 + gate * (1.0 - sig))).astype(d_inner.dtype)
            d_inner[kept, units:] = (d_act * silu_val).astype(d_inner.dtype)
    def block_rows(relative):
        bits = blocks.bit_length() - 1
        owner = 0
        for bit in range(bits):
            own = (place[0] >> bit) & 1
            owner += (own if (relative >> (bits - 1 - bit)) & 1 else 1 - own) << bit
        return weights[rows(owner * block, block), :]

    def store(h, mine):
        for p, target in enumerate(targets):
            pieces, places, width = [], [], 0
            for i in (0, 1):
                pad = ((2 * i + h) * block - width) % 128
                if pad:
                    pieces.append(weights[:pad, :])
                pieces.append(block_rows(2 * p + i))
                places.append(width + pad)
                width += pad + block
            product = against(mine, jnp.concatenate(pieces))
            for i in (0, 1):
                lanes = slice((2 * i + h) * block, (2 * i + h + 1) * block)
                target[:, lanes] = product[:, places[i] : places[i] + block].astype(target.dtype)

    for h in (0, 1):
        if len(turns) == 2:
            store(h, d_inner[rows(group * count + h * half, half), :])
        else:
            pl.when(natural == h * half)(lambda: store(h, d_inner[rows(group * count + h * half, half), :]))


def activate(group, groups, turns, place, total, arrived, weights, blocks, before):
    units, pairs = weights.shape[1] // 2, blocks // 2
    block = weights.shape[0] // blocks
    count = arrived.shape[0] * (3 - len(turns))
    terms = count // 2, 4 * block
    return pl.pallas_call(
        functools.partial(activate_kernel, group, turns, count, blocks),
        in_specs=[IN_SMEM] + [IN_VMEM] * (3 + len(before)),
        out_specs=[IN_VMEM] * (4 + pairs),
        out_shape=[
            pltpu.VMEM((groups * count, units), jnp.bfloat16),
            pltpu.VMEM((groups * count, 2 * units), jnp.bfloat16),
        ]
        + [pltpu.VMEM(array.shape, array.dtype) for array in before[:4][-2:]]
        + [pltpu.VMEM(terms, jnp.bfloat16)] * (pairs // 2)
        + [pltpu.VMEM(terms, jnp.float32)] * (pairs // 2),
        input_output_aliases={4 + i: max(4 - len(before), 0) + i for i in range(len(before))},
        compiler_params=grant(10),
        cost_estimate=cost(0),
        name="activate",
    )(place, *(in_vmem(a) for a in (weights, total, arrived, *before)))


def grads_kernel(tokens, cot, act, d_inner, gate_grad, up_grad, down_grad, gate_held, up_held, down_held, sems):
    rows, units = gate_grad.shape
    copies = []

    def send(held, target, part, i):
        copies.append(pltpu.make_async_copy(held.at[part], target.at[part], sems.at[i]))
        copies[-1].start()

    steps = rows // STEP
    for step in range(steps):
        part = slice(step * STEP, (step + 1) * STEP)
        both = contract(tokens[:, part], d_inner[...])
        gate_held[part, :] = both[:, :units].astype(gate_held.dtype)
        send(gate_held, gate_grad, (part, slice(None)), step)
        up_held[part, :] = both[:, units:].astype(up_held.dtype)
        send(up_held, up_grad, (part, slice(None)), steps + step)
    for step in range(steps):
        part = slice(step * STEP, (step + 1) * STEP)
        down_held[:, part] = contract(act[...], cot[:, part]).astype(down_held.dtype)
        send(down_held, down_grad, (slice(None), part), 2 * steps + step)
    for copy in copies:
        copy.wait()


def weight_grads(tokens, cot, act, d_inner):
    rows, units = tokens.shape[1], act.shape[1]
    shapes = [(rows, units), (rows, units), (units, rows)]
    return pl.pallas_call(
        grads_kernel,
        in_specs=[IN_VMEM] * 4,
        out_specs=[IN_HBM] * 3,
        out_shape=[pltpu.HBM(shape, jnp.bfloat16) for shape in shapes],
        scratch_shapes=[pltpu.VMEM(shape, jnp.bfloat16) for shape in shapes]
        + [pltpu.SemaphoreType.DMA((3 * (rows // STEP),))],
        compiler_params=grant(10),
        cost_estimate=cost(0),
        name="weight_grads",
    )(*(in_vmem(a) for a in (tokens, cot, act, d_inner)))


def after(value, *earlier):
    return lax.optimization_barrier((value, earlier))[0]


def body(tokens, cotangent, gate_codes, up_codes, down_codes, gate_scales, up_scales, down_scales):
    nodes, width = lax.axis_size("node"), lax.axis_size("dp")
    node, place = lax.axis_index("node"), lax.axis_index("dp")
    node_ref, place_ref = node.reshape(1), place.reshape(1)
    rows, units = gate_codes.shape
    count = tokens.shape[0]
    owners = width // nodes
    bits = owners.bit_length() - 1
    block = rows // owners

    side, half = side_of(place), count // 2

    def halves(array):
        return [lax.dynamic_slice_in_dim(array, s * half, half, 0) for s in (side, 1 - side)]

    fetched = [
        swap(fetch(k, node_ref, place_ref, tokens, cotangent, (half, rows)), "node", nodes, k)
        for k in range(1, nodes)
    ]
    all_tokens, all_cots, w_in, w_down, own_sums, own_short = prepare(
        nodes, node_ref, tokens, cotangent, gate_codes, up_codes, down_codes, gate_scales, up_scales, down_scales
    )
    fetched = after(fetched, own_short)

    sums, shorts = [own_sums], [None]
    for k, mine in enumerate(fetched, 1):
        given = swap(mine, "dp", width, 1)
        beside = swap(mine, "dp", width, 1 << SIDE_BIT)
        before, near_far = [all_tokens, all_cots], []
        for far, held in enumerate((mine, beside)):
            if far:
                given = swap(held, "dp", width, 1)
            *before, short = join(k, far, place_ref, held, given, w_in, w_down, before)
            near_far.append(short)
        all_tokens, all_cots, total = before
        sums.append(total)
        shorts.append(near_far)

    mask = 1
    if nodes > 2:
        while mask < nodes // 2:
            sent = [swap(s.astype(jnp.bfloat16), "node", nodes, mask) for s in sums]
            sums = [s + sent[k ^ mask].astype(jnp.float32) for k, s in enumerate(sums)]
            mask *= 2
        own_short = sums[0].astype(jnp.bfloat16)
        shorts = [halves(s.astype(jnp.bfloat16)) for s in sums]
    near_far = [swap(s, "node", nodes, mask) for s in shorts[mask]]
    arrived = [None]
    for k in range(1, nodes):
        short = own_short if k == mask else sums[k ^ mask].astype(jnp.bfloat16)
        arrived.append(swap(short, "node", nodes, mask))

    peers = owners // 2

    def passed(results):
        return *results[:4], results[4:]

    def split(parts, *earlier):
        size = len(parts) // 2
        got = [swap(part, "dp", width, 1) for part in parts[:size]]
        if earlier:
            got = after(got, *earlier)
        sending = []
        for r in range(peers):
            lanes = slice(r % 2 * 2 * block, (r % 2 + 1) * 2 * block)
            both = parts[size + r // 2][:, lanes] + got[r // 2][:, lanes].astype(jnp.float32)
            if r < peers - 1:
                mask = sum(1 << bit for bit in range(1, bits) if (r >> (bits - 1 - bit)) & 1 == 0)
                sending.append((mask, both.astype(jnp.bfloat16)))
        return sending, both

    def exchange(sending):
        return [swap(value, "dp", width, mask) for mask, value in sending]

    def add(mine, got):
        for value in got:
            mine += value.astype(jnp.float32)
        return mine

    blocks, before, others = [None] * nodes, [all_tokens, all_cots], [None] * nodes
    for k in reversed(range(1, nodes)):
        *before, others[k] = passed(
            activate(k, nodes, (0, 1), place_ref, sums[k], arrived[k], w_in, owners, before)
        )
    *before, parts = passed(activate(0, nodes, (0,), place_ref, sums[0], near_far[0], w_in, owners, before))
    last = []
    for k in range(1, nodes):
        sending, mine = split(others[k], before[:2])
        last.append([value for _, value in sending])
        blocks[k] = mine, exchange(sending)
    act, d_inner, all_tokens, all_cots, parts = passed(
        activate(0, nodes, (1,), place_ref, sums[0], after(near_far[1], last), w_in, owners, [*before, *parts])
    )
    sending, mine = split(parts)
    sent, mine = lax.optimization_barrier(([value for _, value in sending], mine))
    got = exchange([(mask, value) for (mask, _), value in zip(sending, sent)])
    for k in range(1, nodes):
        value = add(*blocks[k]).astype(jnp.bfloat16)
        act, sent, value = lax.optimization_barrier((act, sent, value))
        blocks[k] = swap(value, "node", nodes, k).astype(jnp.float32)
    blocks[0] = add(mine, after(got, sent))
    high = place // owners

    def block_for(owner):
        chosen = blocks[0]
        for k in range(1, nodes):
            chosen = jnp.where((owner ^ node) == k, blocks[k], chosen)
        return chosen

    token_grad = block_for(high)
    sent = [block_for(high ^ j).astype(jnp.bfloat16) for j in range(1, nodes)]
    token_grad, sent = lax.optimization_barrier((token_grad, sent))
    act, d_inner = after((act, d_inner), sent)
    gate_grad, up_grad, down_grad = weight_grads(all_tokens, all_cots, act, d_inner)
    for j in range(1, nodes):
        arrived = after(swap(sent[j - 1], "dp", width, j * owners), gate_grad)
        token_grad += arrived.astype(jnp.float32)
    token_grad = token_grad.astype(jnp.bfloat16)
    token_grad = jnp.concatenate([token_grad[:, :block], token_grad[:, block:]])
    return token_grad, gate_grad, up_grad, down_grad


def solution(mesh):
    return jax.shard_map(
        body,
        mesh=mesh,
        in_specs=(
            P("node", None),
            P("node", None),
            P("node", "dp"),
            P("node", "dp"),
            P("dp", "node"),
            P(None, "dp"),
            P(None, "dp"),
            P("dp", None),
        ),
        out_specs=(P("node", "dp"), P("node", "dp"), P("node", "dp"), P("dp", "node")),
        check_vma=False,
    )
```

```python
import functools

import jax
import jax.numpy as jnp
from jax import lax
from jax.experimental import pallas as pl
from jax.experimental.pallas import tpu as pltpu
from jax.sharding import PartitionSpec as P

QB = 128
STEP = 640
SIDE_BIT = 2
IN_HBM = pl.BlockSpec(memory_space=pltpu.HBM)
IN_VMEM = pl.BlockSpec(memory_space=pltpu.VMEM)
IN_SMEM = pl.BlockSpec(memory_space=pltpu.SMEM)


def contract(left, right):
    return lax.dot_general(
        left, right, (((0,), (0,)), ((), ())), preferred_element_type=jnp.float32
    )


def against(left, right):
    return lax.dot_general(
        left, right, (((1,), (1,)), ((), ())), preferred_element_type=jnp.float32
    )


def flipped(size, mask):
    return [(i, i ^ mask) for i in range(size)]


def swap(value, axis, size, mask):
    return lax.ppermute(value, axis, flipped(size, mask))


def in_hbm(array):
    return pltpu.with_memory_space_constraint(array, pltpu.HBM)


def in_vmem(array):
    return pltpu.with_memory_space_constraint(array, pltpu.VMEM)


def cost(operations):
    return pl.CostEstimate(flops=operations, transcendentals=0, bytes_accessed=0)


def grant(mebibytes):
    return pltpu.CompilerParams(vmem_limit_bytes=mebibytes * 1024 * 1024)


def side_of(place):
    return (place >> SIDE_BIT) & 1


def fetch_kernel(mask, node, place, tokens, cot, target, sem):
    half, rows = target.shape
    start = pl.multiple_of(side_of(place[0]) * half, 16)
    column = pl.multiple_of((node[0] ^ mask) * rows, 128)
    part = (pl.ds(start, half), pl.ds(column, rows))

    @pl.when((place[0] & 1) == 0)
    def _():
        copy = pltpu.make_async_copy(tokens.at[part], target, sem)
        copy.start()
        copy.wait()

    @pl.when((place[0] & 1) == 1)
    def _():
        copy = pltpu.make_async_copy(cot.at[part], target, sem)
        copy.start()
        copy.wait()


def fetch(mask, node, place, tokens, cot, shape):
    return pl.pallas_call(
        functools.partial(fetch_kernel, mask),
        in_specs=[IN_SMEM, IN_SMEM, IN_HBM, IN_HBM],
        out_specs=IN_VMEM,
        out_shape=pltpu.VMEM(shape, tokens.dtype),
        scratch_shapes=[pltpu.SemaphoreType.DMA],
        compiler_params=grant(12),
        cost_estimate=cost(0),
        name="fetch",
    )(node, place, in_hbm(tokens), in_hbm(cot))


def prepare_kernel(
    node, tokens, cot, gate_codes, up_codes, down_codes, gate_scales, up_scales, down_scales,
    all_tokens, all_cots, w_in, w_down, total, short, sems,
):
    rows, units = gate_codes.shape
    steps, per_step = rows // STEP, STEP // QB
    own = slice(0, tokens.shape[0])
    gate, up = slice(0, units), slice(units, 2 * units)

    def copies(step):
        column = pl.multiple_of(node[0] * rows + step * STEP, 128)
        part = pl.ds(pl.multiple_of(step * STEP, 128), STEP)
        pairs = (
            (gate_codes.at[part, :], w_in.at[part, gate]),
            (up_codes.at[part, :], w_in.at[part, up]),
            (tokens.at[:, pl.ds(column, STEP)], all_tokens.at[own, part]),
            (down_codes.at[:, part], w_down.at[:, part]),
            (cot.at[:, pl.ds(column, STEP)], all_cots.at[own, part]),
        )
        return [pltpu.make_async_copy(a, b, sems.at[step, i]) for i, (a, b) in enumerate(pairs)]

    for step in range(steps):
        for copy in copies(step):
            copy.start()
    total[...] = jnp.zeros(total.shape, total.dtype)

    def scale(weights, index, factor):
        weights[index] = (weights[index].astype(jnp.float32) * factor).astype(weights.dtype)

    def one(step, carry):
        for copy in copies(step):
            copy.wait()
        first_scale = (node[0] * steps + step) * per_step
        for j in range(per_step):
            part = pl.ds(pl.multiple_of(step * STEP + j * QB, QB), QB)
            row = pl.ds(first_scale + j, 1)
            scale(w_in, (part, gate), gate_scales[row, :])
            scale(w_in, (part, up), up_scales[row, :])
            scale(w_down, (slice(None), part), down_scales[step, :, j : j + 1])
        part = pl.ds(pl.multiple_of(step * STEP, 128), STEP)
        total[:, : 2 * units] += jnp.dot(all_tokens[own, part], w_in[part, :], preferred_element_type=jnp.float32)
        total[:, 2 * units :] += against(all_cots[own, part], w_down[:, part])
        return carry

    lax.fori_loop(0, steps, one, 0)
    short[...] = total[...].astype(short.dtype)


def prepare(nodes, node, tokens, cot, gate_codes, up_codes, down_codes, gate_scales, up_scales, down_scales):
    rows, units = gate_codes.shape
    count = tokens.shape[0]
    steps, per_step = rows // STEP, STEP // QB
    scales = lax.dynamic_slice_in_dim(down_scales, node[0] * (rows // QB), rows // QB, 1)
    scales = scales.reshape(units, steps, per_step).transpose(1, 0, 2)
    codes = jnp.bfloat16
    return pl.pallas_call(
        prepare_kernel,
        in_specs=[IN_SMEM] + [IN_HBM] * 5 + [IN_VMEM] * 3,
        out_specs=[IN_VMEM] * 6,
        out_shape=[
            pltpu.VMEM((nodes * count, rows), codes),
            pltpu.VMEM((nodes * count, rows), codes),
            pltpu.VMEM((rows, 2 * units), codes),
            pltpu.VMEM((units, rows), codes),
            pltpu.VMEM((count, 3 * units), jnp.float32),
            pltpu.VMEM((count, 3 * units), codes),
        ],
        scratch_shapes=[pltpu.SemaphoreType.DMA((steps, 5))],
        compiler_params=grant(12),
        cost_estimate=cost(0),
        name="prepare",
    )(
        node, *(in_hbm(a) for a in (tokens, cot, gate_codes, up_codes, down_codes)),
        gate_scales, up_scales, scales,
    )


def join_kernel(group, far, place, held, given, w_in, w_down, *refs):
    tokens, cot, total, short = refs[-4:]
    half, rows = held.shape
    units = w_down.shape[0]
    side = side_of(place[0])
    natural = (1 - side if far else side) * half
    mine = pl.ds(pl.multiple_of(2 * group * half + natural, 16), half)
    out = pl.ds(pl.multiple_of(natural, 16), half)

    @pl.when((place[0] & 1) == 0)
    def _():
        tokens[mine, :] = held[...]
        cot[mine, :] = given[...]

    @pl.when((place[0] & 1) == 1)
    def _():
        tokens[mine, :] = given[...]
        cot[mine, :] = held[...]

    for step in range(rows // STEP):
        part = slice(step * STEP, (step + 1) * STEP)
        inner = jnp.dot(tokens[mine, part], w_in[part, :], preferred_element_type=jnp.float32)
        outer = against(cot[mine, part], w_down[:, part])
        if step == 0:
            total[out, : 2 * units] = inner
            total[out, 2 * units :] = outer
        else:
            total[out, : 2 * units] += inner
            total[out, 2 * units :] += outer
    short[...] = total[out, :].astype(short.dtype)


def join(group, far, place, held, given, w_in, w_down, before):
    half, rows = held.shape
    units = w_down.shape[0]
    return pl.pallas_call(
        functools.partial(join_kernel, group, far),
        in_specs=[IN_SMEM] + [IN_VMEM] * (4 + len(before)),
        out_specs=[IN_VMEM] * 4,
        out_shape=[
            pltpu.VMEM(before[0].shape, jnp.bfloat16),
            pltpu.VMEM(before[1].shape, jnp.bfloat16),
            pltpu.VMEM((2 * half, 3 * units), jnp.float32),
            pltpu.VMEM((half, 3 * units), jnp.bfloat16),
        ],
        input_output_aliases={5 + i: i for i in range(len(before))},
        compiler_params=grant(12),
        cost_estimate=cost(0),
        name="join",
    )(place, *(in_vmem(a) for a in (held, given, w_in, w_down, *before)))


def activate_kernel(group, turns, count, blocks, parked, place, weights, total, arrived, *refs):
    block = weights.shape[0] // blocks
    if parked:
        cots, sem = refs[-6 - blocks // 2], refs[-1]
        copy = pltpu.make_async_copy(cots, refs[-2], sem)
        copy.start()
        refs = refs[:-2]
    act, d_inner, _, *targets = refs[-3 - blocks // 2 :]
    units, half, chunk = act.shape[1], count // 2, 32
    side = side_of(place[0])

    def rows(first, length):
        return pl.ds(pl.multiple_of(first, 16), length)

    for turn in turns:
        natural = (1 - side if turn else side) * half
        for start in range(0, half, chunk):
            def of(array):
                return rows((natural if array.shape[0] == count else 0) + start, chunk)

            sums = total[of(total), :] + arrived[of(arrived), :].astype(jnp.float32)
            gate, upper, d_act = sums[:, :units], sums[:, units : 2 * units], sums[:, 2 * units :]
            sig = jax.nn.sigmoid(gate)
            silu_val = gate * sig
            kept = rows(group * count + natural + start, chunk)
            act[kept, :] = (silu_val * upper).astype(act.dtype)
            d_inner[kept, :units] = (d_act * upper * sig * (1.0 + gate * (1.0 - sig))).astype(d_inner.dtype)
            d_inner[kept, units:] = (d_act * silu_val).astype(d_inner.dtype)
    def block_rows(relative):
        bits = blocks.bit_length() - 1
        owner = 0
        for bit in range(bits):
            own = (place[0] >> bit) & 1
            owner += (own if (relative >> (bits - 1 - bit)) & 1 else 1 - own) << bit
        return weights[rows(owner * block, block), :]

    def store(h, mine):
        for p, target in enumerate(targets):
            pieces, places, width = [], [], 0
            for i in (0, 1):
                pad = ((2 * i + h) * block - width) % 128
                if pad:
                    pieces.append(weights[:pad, :])
                pieces.append(block_rows(2 * p + i))
                places.append(width + pad)
                width += pad + block
            product = against(mine, jnp.concatenate(pieces))
            for i in (0, 1):
                lanes = slice((2 * i + h) * block, (2 * i + h + 1) * block)
                target[:, lanes] = product[:, places[i] : places[i] + block].astype(target.dtype)

    if len(turns) == 2:
        for p, target in enumerate(targets):
            both = jnp.concatenate([block_rows(2 * p), block_rows(2 * p + 1)])
            product = against(d_inner[rows(group * count, count), :], both)
            for n in range(4):
                i, h = n // 2, n % 2
                value = product[h * half : (h + 1) * half, i * block : (i + 1) * block]
                target[:, n * block : (n + 1) * block] = value.astype(target.dtype)
    else:
        for h in (0, 1):
            pl.when(natural == h * half)(lambda: store(h, d_inner[rows(group * count + h * half, half), :]))
    if parked:
        copy.wait()


def activate(group, groups, turns, place, total, arrived, weights, blocks, before, park=()):
    units, pairs = weights.shape[1] // 2, blocks // 2
    block = weights.shape[0] // blocks
    count = arrived.shape[0] * (3 - len(turns))
    terms = count // 2, 4 * block
    return pl.pallas_call(
        functools.partial(activate_kernel, group, turns, count, blocks, len(park)),
        in_specs=[IN_SMEM] + [IN_VMEM] * (3 + len(before) + len(park)),
        out_specs=[IN_VMEM] * (3 + pairs) + [IN_HBM] * len(park),
        out_shape=[
            pltpu.VMEM((groups * count, units), jnp.bfloat16),
            pltpu.VMEM((groups * count, 2 * units), jnp.bfloat16),
            pltpu.VMEM((groups * count, weights.shape[0]), jnp.bfloat16),
        ]
        + [pltpu.VMEM(terms, jnp.bfloat16)] * (pairs // 2)
        + [pltpu.VMEM(terms, jnp.float32)] * (pairs // 2)
        + [pltpu.HBM(array.shape, array.dtype) for array in park],
        scratch_shapes=[pltpu.SemaphoreType.DMA] * len(park),
        input_output_aliases={4 + i: max(3 - len(before), 0) + i for i in range(len(before))},
        compiler_params=grant(12),
        cost_estimate=cost(0),
        name="activate",
    )(place, *(in_vmem(a) for a in (weights, total, arrived, *before, *park)))


def grads_kernel(
    tokens, cots, act, d_inner, gate_grad, up_grad, down_grad, gate_held, up_held, down_held, cot, sems, cot_sem
):
    arriving = pltpu.make_async_copy(cots, cot, cot_sem)
    arriving.start()
    rows, units = gate_grad.shape
    copies = []

    def send(held, target, part, i):
        copies.append(pltpu.make_async_copy(held.at[part], target.at[part], sems.at[i]))
        copies[-1].start()

    steps = rows // STEP
    for step in range(steps):
        part = slice(step * STEP, (step + 1) * STEP)
        both = contract(tokens[:, part], d_inner[...])
        gate_held[part, :] = both[:, :units].astype(gate_held.dtype)
        send(gate_held, gate_grad, (part, slice(None)), step)
        up_held[part, :] = both[:, units:].astype(up_held.dtype)
        send(up_held, up_grad, (part, slice(None)), steps + step)
    arriving.wait()
    for step in range(steps):
        part = slice(step * STEP, (step + 1) * STEP)
        down_held[:, part] = contract(act[...], cot[:, part]).astype(down_held.dtype)
        send(down_held, down_grad, (slice(None), part), 2 * steps + step)
    for copy in copies:
        copy.wait()


def weight_grads(tokens, cot, act, d_inner):
    rows, units = tokens.shape[1], act.shape[1]
    shapes = [(rows, units), (rows, units), (units, rows)]
    return pl.pallas_call(
        grads_kernel,
        in_specs=[IN_VMEM, IN_HBM, IN_VMEM, IN_VMEM],
        out_specs=[IN_HBM] * 3,
        out_shape=[pltpu.HBM(shape, jnp.bfloat16) for shape in shapes],
        scratch_shapes=[pltpu.VMEM(shape, jnp.bfloat16) for shape in shapes]
        + [
            pltpu.VMEM(cot.shape, cot.dtype),
            pltpu.SemaphoreType.DMA((3 * (rows // STEP),)),
            pltpu.SemaphoreType.DMA,
        ],
        compiler_params=grant(12),
        cost_estimate=cost(0),
        name="weight_grads",
    )(in_vmem(tokens), in_hbm(cot), in_vmem(act), in_vmem(d_inner))


def after(value, *earlier):
    return lax.optimization_barrier((value, earlier))[0]


def body(tokens, cotangent, gate_codes, up_codes, down_codes, gate_scales, up_scales, down_scales):
    nodes, width = lax.axis_size("node"), lax.axis_size("dp")
    node, place = lax.axis_index("node"), lax.axis_index("dp")
    node_ref, place_ref = node.reshape(1), place.reshape(1)
    rows, units = gate_codes.shape
    count = tokens.shape[0]
    owners = width // nodes
    bits = owners.bit_length() - 1
    block = rows // owners

    side, half = side_of(place), count // 2

    def halves(array):
        return [lax.dynamic_slice_in_dim(array, s * half, half, 0) for s in (side, 1 - side)]

    fetched = [
        swap(fetch(k, node_ref, place_ref, tokens, cotangent, (half, rows)), "node", nodes, k)
        for k in range(1, nodes)
    ]
    all_tokens, all_cots, w_in, w_down, own_sums, own_short = prepare(
        nodes, node_ref, tokens, cotangent, gate_codes, up_codes, down_codes, gate_scales, up_scales, down_scales
    )
    fetched = after(fetched, own_short)

    sums, shorts = [own_sums], [None]
    for k, mine in enumerate(fetched, 1):
        given = swap(mine, "dp", width, 1)
        beside = swap(mine, "dp", width, 1 << SIDE_BIT)
        before, near_far = [all_tokens, all_cots], []
        for far, held in enumerate((mine, beside)):
            if far:
                given = swap(held, "dp", width, 1)
            *before, short = join(k, far, place_ref, held, given, w_in, w_down, before)
            near_far.append(short)
        all_tokens, all_cots, total = before
        sums.append(total)
        shorts.append(near_far)

    mask = 1
    if nodes > 2:
        while mask < nodes // 2:
            sent = [swap(s.astype(jnp.bfloat16), "node", nodes, mask) for s in sums]
            sums = [s + sent[k ^ mask].astype(jnp.float32) for k, s in enumerate(sums)]
            mask *= 2
        own_short = sums[0].astype(jnp.bfloat16)
        shorts = [halves(s.astype(jnp.bfloat16)) for s in sums]
    near_far = [swap(s, "node", nodes, mask) for s in shorts[mask]]
    arrived = [None]
    for k in range(1, nodes):
        short = own_short if k == mask else sums[k ^ mask].astype(jnp.bfloat16)
        arrived.append(swap(short, "node", nodes, mask))

    peers = owners // 2

    def passed(results):
        return *results[:3], results[3:]

    def split(parts, *earlier):
        size = len(parts) // 2
        got = [swap(part, "dp", width, 1) for part in parts[:size]]
        if earlier:
            got = after(got, *earlier)
        sending = []
        for r in range(peers):
            lanes = slice(r % 2 * 2 * block, (r % 2 + 1) * 2 * block)
            both = parts[size + r // 2][:, lanes] + got[r // 2][:, lanes].astype(jnp.float32)
            if r < peers - 1:
                mask = sum(1 << bit for bit in range(1, bits) if (r >> (bits - 1 - bit)) & 1 == 0)
                sending.append((mask, both.astype(jnp.bfloat16)))
        return sending, both

    def exchange(sending):
        return [swap(value, "dp", width, mask) for mask, value in sending]

    def add(mine, got):
        for value in got:
            mine += value.astype(jnp.float32)
        return mine

    blocks, before, others = [None] * nodes, [all_tokens], [None] * nodes
    for k in reversed(range(1, nodes)):
        park = [all_cots] if k == 1 else []
        *before, others[k] = passed(
            activate(k, nodes, (0, 1), place_ref, sums[k], arrived[k], w_in, owners, before, park)
        )
    *others[1], all_cots = others[1]
    *before, parts = passed(activate(0, nodes, (0,), place_ref, sums[0], near_far[0], w_in, owners, before))
    last = []
    for k in range(1, nodes):
        sending, mine = split(others[k], before[:2])
        last.append([value for _, value in sending])
        blocks[k] = mine, exchange(sending)
    act, d_inner, all_tokens, parts = passed(
        activate(0, nodes, (1,), place_ref, sums[0], after(near_far[1], last), w_in, owners, [*before, *parts])
    )
    sending, mine = split(parts)
    sent, mine = lax.optimization_barrier(([value for _, value in sending], mine))
    got = exchange([(mask, value) for (mask, _), value in zip(sending, sent)])
    for k in range(1, nodes):
        value = add(*blocks[k]).astype(jnp.bfloat16)
        act, sent, value = lax.optimization_barrier((act, sent, value))
        blocks[k] = swap(value, "node", nodes, k).astype(jnp.float32)
    act, d_inner = after((act, d_inner), sent, value)
    gate_grad, up_grad, down_grad = weight_grads(all_tokens, all_cots, act, d_inner)
    blocks[0] = add(mine, after(got, gate_grad))
    high = place // owners

    def block_for(owner):
        chosen = blocks[0]
        for k in range(1, nodes):
            chosen = jnp.where((owner ^ node) == k, blocks[k], chosen)
        return chosen

    token_grad = block_for(high)
    sent = [block_for(high ^ j).astype(jnp.bfloat16) for j in range(1, nodes)]
    token_grad, sent = lax.optimization_barrier((token_grad, sent))
    for j in range(1, nodes):
        arrived = swap(sent[j - 1], "dp", width, j * owners)
        token_grad += arrived.astype(jnp.float32)
    token_grad = token_grad.astype(jnp.bfloat16)
    token_grad = jnp.concatenate([token_grad[:, :block], token_grad[:, block:]])
    return token_grad, gate_grad, up_grad, down_grad


def solution(mesh):
    return jax.shard_map(
        body,
        mesh=mesh,
        in_specs=(
            P("node", None),
            P("node", None),
            P("node", "dp"),
            P("node", "dp"),
            P("dp", "node"),
            P(None, "dp"),
            P(None, "dp"),
            P("dp", None),
        ),
        out_specs=(P("node", "dp"), P("node", "dp"), P("node", "dp"), P("dp", "node")),
        check_vma=False,
    )
```

```python
import functools

import jax
import jax.numpy as jnp
from jax import lax
from jax.experimental import pallas as pl
from jax.experimental.pallas import tpu as pltpu
from jax.sharding import PartitionSpec as P

QB = 128
STEP = 640
SIDE_BIT = 2
IN_HBM = pl.BlockSpec(memory_space=pltpu.HBM)
IN_VMEM = pl.BlockSpec(memory_space=pltpu.VMEM)
IN_SMEM = pl.BlockSpec(memory_space=pltpu.SMEM)


def contract(left, right):
    return lax.dot_general(
        left, right, (((0,), (0,)), ((), ())), preferred_element_type=jnp.float32
    )


def against(left, right):
    return lax.dot_general(
        left, right, (((1,), (1,)), ((), ())), preferred_element_type=jnp.float32
    )


def flipped(size, mask):
    return [(i, i ^ mask) for i in range(size)]


def swap(value, axis, size, mask):
    return lax.ppermute(value, axis, flipped(size, mask))


def in_hbm(array):
    return pltpu.with_memory_space_constraint(array, pltpu.HBM)


def in_vmem(array):
    return pltpu.with_memory_space_constraint(array, pltpu.VMEM)


def cost(operations):
    return pl.CostEstimate(flops=operations, transcendentals=0, bytes_accessed=0)


def grant(mebibytes):
    return pltpu.CompilerParams(vmem_limit_bytes=mebibytes * 1024 * 1024)


def side_of(place):
    return (place >> SIDE_BIT) & 1


def fetch_kernel(mask, node, place, tokens, cot, target, sem):
    half, rows = target.shape
    start = pl.multiple_of(side_of(place[0]) * half, 16)
    column = pl.multiple_of((node[0] ^ mask) * rows, 128)
    part = (pl.ds(start, half), pl.ds(column, rows))

    @pl.when((place[0] & 1) == 0)
    def _():
        copy = pltpu.make_async_copy(tokens.at[part], target, sem)
        copy.start()
        copy.wait()

    @pl.when((place[0] & 1) == 1)
    def _():
        copy = pltpu.make_async_copy(cot.at[part], target, sem)
        copy.start()
        copy.wait()


def fetch(mask, node, place, tokens, cot, shape):
    return pl.pallas_call(
        functools.partial(fetch_kernel, mask),
        in_specs=[IN_SMEM, IN_SMEM, IN_HBM, IN_HBM],
        out_specs=IN_VMEM,
        out_shape=pltpu.VMEM(shape, tokens.dtype),
        scratch_shapes=[pltpu.SemaphoreType.DMA],
        compiler_params=grant(12),
        cost_estimate=cost(0),
        name="fetch",
    )(node, place, in_hbm(tokens), in_hbm(cot))


def prepare_kernel(
    node, tokens, cot, gate_codes, up_codes, down_codes, gate_scales, up_scales, down_scales,
    all_tokens, all_cots, w_in, w_down, total, short, sems,
):
    rows, units = gate_codes.shape
    steps, per_step = rows // STEP, STEP // QB
    own = slice(0, tokens.shape[0])
    gate, up = slice(0, units), slice(units, 2 * units)

    def copies(step):
        column = pl.multiple_of(node[0] * rows + step * STEP, 128)
        part = pl.ds(pl.multiple_of(step * STEP, 128), STEP)
        pairs = (
            (gate_codes.at[part, :], w_in.at[part, gate]),
            (up_codes.at[part, :], w_in.at[part, up]),
            (tokens.at[:, pl.ds(column, STEP)], all_tokens.at[own, part]),
            (down_codes.at[:, part], w_down.at[:, part]),
            (cot.at[:, pl.ds(column, STEP)], all_cots.at[own, part]),
        )
        return [pltpu.make_async_copy(a, b, sems.at[step, i]) for i, (a, b) in enumerate(pairs)]

    for step in range(steps):
        for copy in copies(step):
            copy.start()
    total[...] = jnp.zeros(total.shape, total.dtype)

    def scale(weights, index, factor):
        weights[index] = (weights[index].astype(jnp.float32) * factor).astype(weights.dtype)

    def one(step, carry):
        for copy in copies(step):
            copy.wait()
        first_scale = (node[0] * steps + step) * per_step
        for j in range(per_step):
            part = pl.ds(pl.multiple_of(step * STEP + j * QB, QB), QB)
            row = pl.ds(first_scale + j, 1)
            scale(w_in, (part, gate), gate_scales[row, :])
            scale(w_in, (part, up), up_scales[row, :])
            scale(w_down, (slice(None), part), down_scales[step, :, j : j + 1])
        part = pl.ds(pl.multiple_of(step * STEP, 128), STEP)
        total[:, : 2 * units] += jnp.dot(all_tokens[own, part], w_in[part, :], preferred_element_type=jnp.float32)
        total[:, 2 * units :] += against(all_cots[own, part], w_down[:, part])
        return carry

    lax.fori_loop(0, steps, one, 0)
    short[...] = total[...].astype(short.dtype)


def prepare(nodes, node, tokens, cot, gate_codes, up_codes, down_codes, gate_scales, up_scales, down_scales):
    rows, units = gate_codes.shape
    count = tokens.shape[0]
    steps, per_step = rows // STEP, STEP // QB
    scales = lax.dynamic_slice_in_dim(down_scales, node[0] * (rows // QB), rows // QB, 1)
    scales = scales.reshape(units, steps, per_step).transpose(1, 0, 2)
    codes = jnp.bfloat16
    return pl.pallas_call(
        prepare_kernel,
        in_specs=[IN_SMEM] + [IN_HBM] * 5 + [IN_VMEM] * 3,
        out_specs=[IN_VMEM] * 6,
        out_shape=[
            pltpu.VMEM((nodes * count, rows), codes),
            pltpu.VMEM((nodes * count, rows), codes),
            pltpu.VMEM((rows, 2 * units), codes),
            pltpu.VMEM((units, rows), codes),
            pltpu.VMEM((count, 3 * units), jnp.float32),
            pltpu.VMEM((count, 3 * units), codes),
        ],
        scratch_shapes=[pltpu.SemaphoreType.DMA((steps, 5))],
        compiler_params=grant(12),
        cost_estimate=cost(0),
        name="prepare",
    )(
        node, *(in_hbm(a) for a in (tokens, cot, gate_codes, up_codes, down_codes)),
        gate_scales, up_scales, scales,
    )


def join_kernel(group, far, place, held, given, w_in, w_down, *refs):
    tokens, cot, total, short = refs[-4:]
    half, rows = held.shape
    units = w_down.shape[0]
    side = side_of(place[0])
    natural = (1 - side if far else side) * half
    mine = pl.ds(pl.multiple_of(2 * group * half + natural, 16), half)
    out = pl.ds(pl.multiple_of(natural, 16), half)

    @pl.when((place[0] & 1) == 0)
    def _():
        tokens[mine, :] = held[...]
        cot[mine, :] = given[...]

    @pl.when((place[0] & 1) == 1)
    def _():
        tokens[mine, :] = given[...]
        cot[mine, :] = held[...]

    for step in range(rows // STEP):
        part = slice(step * STEP, (step + 1) * STEP)
        inner = jnp.dot(tokens[mine, part], w_in[part, :], preferred_element_type=jnp.float32)
        outer = against(cot[mine, part], w_down[:, part])
        if step == 0:
            total[out, : 2 * units] = inner
            total[out, 2 * units :] = outer
        else:
            total[out, : 2 * units] += inner
            total[out, 2 * units :] += outer
    short[...] = total[out, :].astype(short.dtype)


def join(group, far, place, held, given, w_in, w_down, before):
    half, rows = held.shape
    units = w_down.shape[0]
    return pl.pallas_call(
        functools.partial(join_kernel, group, far),
        in_specs=[IN_SMEM] + [IN_VMEM] * (4 + len(before)),
        out_specs=[IN_VMEM] * 4,
        out_shape=[
            pltpu.VMEM(before[0].shape, jnp.bfloat16),
            pltpu.VMEM(before[1].shape, jnp.bfloat16),
            pltpu.VMEM((2 * half, 3 * units), jnp.float32),
            pltpu.VMEM((half, 3 * units), jnp.bfloat16),
        ],
        input_output_aliases={5 + i: i for i in range(len(before))},
        compiler_params=grant(12),
        cost_estimate=cost(0),
        name="join",
    )(place, *(in_vmem(a) for a in (held, given, w_in, w_down, *before)))


def activate_kernel(group, turns, count, blocks, parked, place, weights, total, arrived, *refs):
    block = weights.shape[0] // blocks
    if parked:
        cots, sem = refs[-6 - blocks // 2], refs[-1]
        copy = pltpu.make_async_copy(cots, refs[-2], sem)
        copy.start()
        refs = refs[:-2]
    act, d_inner, _, *targets = refs[-3 - blocks // 2 :]
    units, half, chunk = act.shape[1], count // 2, 32
    side = side_of(place[0])

    def rows(first, length):
        return pl.ds(pl.multiple_of(first, 16), length)

    for turn in turns:
        natural = (1 - side if turn else side) * half
        for start in range(0, half, chunk):
            def of(array):
                return rows((natural if array.shape[0] == count else 0) + start, chunk)

            sums = total[of(total), :] + arrived[of(arrived), :].astype(jnp.float32)
            gate, upper, d_act = sums[:, :units], sums[:, units : 2 * units], sums[:, 2 * units :]
            sig = jax.nn.sigmoid(gate)
            silu_val = gate * sig
            kept = rows(group * count + natural + start, chunk)
            act[kept, :] = (silu_val * upper).astype(act.dtype)
            d_inner[kept, :units] = (d_act * upper * sig * (1.0 + gate * (1.0 - sig))).astype(d_inner.dtype)
            d_inner[kept, units:] = (d_act * silu_val).astype(d_inner.dtype)
    def block_rows(relative):
        bits = blocks.bit_length() - 1
        owner = 0
        for bit in range(bits):
            own = (place[0] >> bit) & 1
            owner += (own if (relative >> (bits - 1 - bit)) & 1 else 1 - own) << bit
        return weights[rows(owner * block, block), :]

    def store(h, mine):
        for p, target in enumerate(targets):
            pieces, places, width = [], [], 0
            for i in (0, 1):
                pad = ((2 * i + h) * block - width) % 128
                if pad:
                    pieces.append(weights[:pad, :])
                pieces.append(block_rows(2 * p + i))
                places.append(width + pad)
                width += pad + block
            product = against(mine, jnp.concatenate(pieces))
            for i in (0, 1):
                lanes = slice((2 * i + h) * block, (2 * i + h + 1) * block)
                target[:, lanes] = product[:, places[i] : places[i] + block].astype(target.dtype)

    if len(turns) == 2:
        for p, target in enumerate(targets):
            both = jnp.concatenate([block_rows(2 * p), block_rows(2 * p + 1)])
            product = against(d_inner[rows(group * count, count), :], both)
            for n in range(4):
                i, h = n // 2, n % 2
                value = product[h * half : (h + 1) * half, i * block : (i + 1) * block]
                target[:, n * block : (n + 1) * block] = value.astype(target.dtype)
    else:
        for h in (0, 1):
            pl.when(natural == h * half)(lambda: store(h, d_inner[rows(group * count + h * half, half), :]))
    if parked:
        copy.wait()


def activate(group, groups, turns, place, total, arrived, weights, blocks, before, park=()):
    units, pairs = weights.shape[1] // 2, blocks // 2
    block = weights.shape[0] // blocks
    count = arrived.shape[0] * (3 - len(turns))
    terms = count // 2, 4 * block
    return pl.pallas_call(
        functools.partial(activate_kernel, group, turns, count, blocks, len(park)),
        in_specs=[IN_SMEM] + [IN_VMEM] * (3 + len(before) + len(park)),
        out_specs=[IN_VMEM] * (3 + pairs) + [IN_HBM] * len(park),
        out_shape=[
            pltpu.VMEM((groups * count, units), jnp.bfloat16),
            pltpu.VMEM((groups * count, 2 * units), jnp.bfloat16),
            pltpu.VMEM((groups * count, weights.shape[0]), jnp.bfloat16),
        ]
        + [pltpu.VMEM(terms, jnp.bfloat16)] * (pairs // 2)
        + [pltpu.VMEM(terms, jnp.float32)] * (pairs // 2)
        + [pltpu.HBM(array.shape, array.dtype) for array in park],
        scratch_shapes=[pltpu.SemaphoreType.DMA] * len(park),
        input_output_aliases={4 + i: max(3 - len(before), 0) + i for i in range(len(before))},
        compiler_params=grant(12),
        cost_estimate=cost(0),
        name="activate",
    )(place, *(in_vmem(a) for a in (weights, total, arrived, *before, *park)))


def inner_grads_kernel(tokens, d_inner, gate_grad, up_grad, gate_held, up_held, sems):
    rows, units = gate_grad.shape
    steps = rows // STEP
    copies = []
    for step in range(steps):
        part = slice(step * STEP, (step + 1) * STEP)
        both = contract(tokens[:, part], d_inner[...])
        gate_held[part, :] = both[:, :units].astype(gate_held.dtype)
        up_held[part, :] = both[:, units:].astype(up_held.dtype)
        for i, (held, target) in enumerate(((gate_held, gate_grad), (up_held, up_grad))):
            copies.append(pltpu.make_async_copy(held.at[part, :], target.at[part, :], sems.at[2 * step + i]))
            copies[-1].start()
    for copy in copies:
        copy.wait()


def inner_grads(tokens, d_inner):
    rows, units = tokens.shape[1], d_inner.shape[1] // 2
    return pl.pallas_call(
        inner_grads_kernel,
        in_specs=[IN_VMEM] * 2,
        out_specs=[IN_HBM] * 2,
        out_shape=[pltpu.HBM((rows, units), jnp.bfloat16)] * 2,
        scratch_shapes=[pltpu.VMEM((rows, units), jnp.bfloat16)] * 2
        + [pltpu.SemaphoreType.DMA((2 * (rows // STEP),))],
        compiler_params=grant(12),
        cost_estimate=cost(0),
        name="inner_grads",
    )(in_vmem(tokens), in_vmem(d_inner))


def down_grads_kernel(cots, act, down_grad, cot, held, in_sems, out_sems):
    steps = cots.shape[1] // STEP
    parts = [slice(step * STEP, (step + 1) * STEP) for step in range(steps)]
    arriving = [
        pltpu.make_async_copy(cots.at[:, part], cot.at[:, part], in_sems.at[step]) for step, part in enumerate(parts)
    ]
    leaving = [
        pltpu.make_async_copy(held.at[:, part], down_grad.at[:, part], out_sems.at[step])
        for step, part in enumerate(parts)
    ]
    for copy in arriving:
        copy.start()
    for step, part in enumerate(parts):
        arriving[step].wait()
        held[:, part] = contract(act[...], cot[:, part]).astype(held.dtype)
        leaving[step].start()
    for copy in leaving:
        copy.wait()


def down_grads(cots, act):
    shape = act.shape[1], cots.shape[1]
    sems = pltpu.SemaphoreType.DMA((shape[1] // STEP,))
    return pl.pallas_call(
        down_grads_kernel,
        in_specs=[IN_HBM, IN_VMEM],
        out_specs=IN_HBM,
        out_shape=pltpu.HBM(shape, jnp.bfloat16),
        scratch_shapes=[pltpu.VMEM(cots.shape, cots.dtype), pltpu.VMEM(shape, jnp.bfloat16), sems, sems],
        compiler_params=grant(12),
        cost_estimate=cost(0),
        name="down_grads",
    )(in_hbm(cots), in_vmem(act))


def after(value, *earlier):
    return lax.optimization_barrier((value, earlier))[0]


def body(tokens, cotangent, gate_codes, up_codes, down_codes, gate_scales, up_scales, down_scales):
    nodes, width = lax.axis_size("node"), lax.axis_size("dp")
    node, place = lax.axis_index("node"), lax.axis_index("dp")
    node_ref, place_ref = node.reshape(1), place.reshape(1)
    rows, units = gate_codes.shape
    count = tokens.shape[0]
    owners = width // nodes
    bits = owners.bit_length() - 1
    block = rows // owners

    side, half = side_of(place), count // 2

    def halves(array):
        return [lax.dynamic_slice_in_dim(array, s * half, half, 0) for s in (side, 1 - side)]

    fetched = [
        swap(fetch(k, node_ref, place_ref, tokens, cotangent, (half, rows)), "node", nodes, k)
        for k in range(1, nodes)
    ]
    all_tokens, all_cots, w_in, w_down, own_sums, own_short = prepare(
        nodes, node_ref, tokens, cotangent, gate_codes, up_codes, down_codes, gate_scales, up_scales, down_scales
    )
    fetched = after(fetched, own_short)

    sums, shorts = [own_sums], [None]
    for k, mine in enumerate(fetched, 1):
        given = swap(mine, "dp", width, 1)
        beside = swap(mine, "dp", width, 1 << SIDE_BIT)
        before, near_far = [all_tokens, all_cots], []
        for far, held in enumerate((mine, beside)):
            if far:
                given = swap(held, "dp", width, 1)
            *before, short = join(k, far, place_ref, held, given, w_in, w_down, before)
            near_far.append(short)
        all_tokens, all_cots, total = before
        sums.append(total)
        shorts.append(near_far)

    mask = 1
    if nodes > 2:
        while mask < nodes // 2:
            sent = [swap(s.astype(jnp.bfloat16), "node", nodes, mask) for s in sums]
            sums = [s + sent[k ^ mask].astype(jnp.float32) for k, s in enumerate(sums)]
            mask *= 2
        own_short = sums[0].astype(jnp.bfloat16)
        shorts = [halves(s.astype(jnp.bfloat16)) for s in sums]
    near_far = [swap(s, "node", nodes, mask) for s in shorts[mask]]
    arrived = [None]
    for k in range(1, nodes):
        short = own_short if k == mask else sums[k ^ mask].astype(jnp.bfloat16)
        arrived.append(swap(short, "node", nodes, mask))

    peers = owners // 2

    def passed(results):
        return *results[:3], results[3:]

    def split(parts, *earlier):
        size = len(parts) // 2
        got = [swap(part, "dp", width, 1) for part in parts[:size]]
        if earlier:
            got = after(got, *earlier)
        sending = []
        for r in range(peers):
            lanes = slice(r % 2 * 2 * block, (r % 2 + 1) * 2 * block)
            both = parts[size + r // 2][:, lanes] + got[r // 2][:, lanes].astype(jnp.float32)
            if r < peers - 1:
                mask = sum(1 << bit for bit in range(1, bits) if (r >> (bits - 1 - bit)) & 1 == 0)
                sending.append((mask, both.astype(jnp.bfloat16)))
        return sending, both

    def exchange(sending):
        return [swap(value, "dp", width, mask) for mask, value in sending]

    def add(mine, got):
        for value in got:
            mine += value.astype(jnp.float32)
        return mine

    blocks, before, others = [None] * nodes, [all_tokens], [None] * nodes
    for k in reversed(range(1, nodes)):
        park = [all_cots] if k == 1 else []
        *before, others[k] = passed(
            activate(k, nodes, (0, 1), place_ref, sums[k], arrived[k], w_in, owners, before, park)
        )
    *others[1], all_cots = others[1]
    *before, parts = passed(activate(0, nodes, (0,), place_ref, sums[0], near_far[0], w_in, owners, before))
    last = []
    for k in range(1, nodes):
        sending, mine = split(others[k], before[:2])
        last.append([value for _, value in sending])
        blocks[k] = mine, exchange(sending)
    act, d_inner, all_tokens, parts = passed(
        activate(0, nodes, (1,), place_ref, sums[0], after(near_far[1], last), w_in, owners, [*before, *parts])
    )
    sending, mine = split(parts)
    sent, mine = lax.optimization_barrier(([value for _, value in sending], mine))
    got = exchange([(mask, value) for (mask, _), value in zip(sending, sent)])
    for k in range(1, nodes):
        value = add(*blocks[k]).astype(jnp.bfloat16)
        act, sent, value = lax.optimization_barrier((act, sent, value))
        blocks[k] = swap(value, "node", nodes, k).astype(jnp.float32)
    gate_grad, up_grad = inner_grads(all_tokens, after(d_inner, sent, value))
    blocks[0] = add(mine, after(got, gate_grad))
    high = place // owners

    def block_for(owner):
        chosen = blocks[0]
        for k in range(1, nodes):
            chosen = jnp.where((owner ^ node) == k, blocks[k], chosen)
        return chosen

    token_grad = block_for(high)
    sent = [block_for(high ^ j).astype(jnp.bfloat16) for j in range(1, nodes)]
    token_grad, sent = lax.optimization_barrier((token_grad, sent))
    down_grad = down_grads(all_cots, after(act, sent))
    for j in range(1, nodes):
        arrived = after(swap(sent[j - 1], "dp", width, j * owners), down_grad)
        token_grad += arrived.astype(jnp.float32)
    token_grad = token_grad.astype(jnp.bfloat16)
    token_grad = jnp.concatenate([token_grad[:, :block], token_grad[:, block:]])
    return token_grad, gate_grad, up_grad, down_grad


def solution(mesh):
    return jax.shard_map(
        body,
        mesh=mesh,
        in_specs=(
            P("node", None),
            P("node", None),
            P("node", "dp"),
            P("node", "dp"),
            P("dp", "node"),
            P(None, "dp"),
            P(None, "dp"),
            P("dp", None),
        ),
        out_specs=(P("node", "dp"), P("node", "dp"), P("node", "dp"), P("dp", "node")),
        check_vma=False,
    )
```

```python
import functools

import jax
import jax.numpy as jnp
from jax import lax
from jax.experimental import pallas as pl
from jax.experimental.pallas import tpu as pltpu
from jax.sharding import PartitionSpec as P

QB = 128
STEP = 640
SIDE_BIT = 2
IN_HBM = pl.BlockSpec(memory_space=pltpu.HBM)
IN_VMEM = pl.BlockSpec(memory_space=pltpu.VMEM)
IN_SMEM = pl.BlockSpec(memory_space=pltpu.SMEM)


def contract(left, right):
    return lax.dot_general(
        left, right, (((0,), (0,)), ((), ())), preferred_element_type=jnp.float32
    )


def against(left, right):
    return lax.dot_general(
        left, right, (((1,), (1,)), ((), ())), preferred_element_type=jnp.float32
    )


def flipped(size, mask):
    return [(i, i ^ mask) for i in range(size)]


def swap(value, axis, size, mask):
    return lax.ppermute(value, axis, flipped(size, mask))


def in_hbm(array):
    return pltpu.with_memory_space_constraint(array, pltpu.HBM)


def in_vmem(array):
    return pltpu.with_memory_space_constraint(array, pltpu.VMEM)


def cost(operations):
    return pl.CostEstimate(flops=operations, transcendentals=0, bytes_accessed=0)


def grant(mebibytes):
    return pltpu.CompilerParams(vmem_limit_bytes=mebibytes * 1024 * 1024)


def side_of(place):
    return (place >> SIDE_BIT) & 1


def fetch_kernel(mask, node, place, tokens, cot, target, sem):
    half, rows = target.shape
    start = pl.multiple_of(side_of(place[0]) * half, 16)
    column = pl.multiple_of((node[0] ^ mask) * rows, 128)
    part = (pl.ds(start, half), pl.ds(column, rows))

    @pl.when((place[0] & 1) == 0)
    def _():
        copy = pltpu.make_async_copy(tokens.at[part], target, sem)
        copy.start()
        copy.wait()

    @pl.when((place[0] & 1) == 1)
    def _():
        copy = pltpu.make_async_copy(cot.at[part], target, sem)
        copy.start()
        copy.wait()


def fetch(mask, node, place, tokens, cot, shape):
    return pl.pallas_call(
        functools.partial(fetch_kernel, mask),
        in_specs=[IN_SMEM, IN_SMEM, IN_HBM, IN_HBM],
        out_specs=IN_VMEM,
        out_shape=pltpu.VMEM(shape, tokens.dtype),
        scratch_shapes=[pltpu.SemaphoreType.DMA],
        compiler_params=grant(12),
        cost_estimate=cost(0),
        name="fetch",
    )(node, place, in_hbm(tokens), in_hbm(cot))


def prepare_kernel(
    node, tokens, cot, gate_codes, up_codes, down_codes, gate_scales, up_scales, down_scales,
    all_tokens, all_cots, w_in, w_down, total, short, sems,
):
    rows, units = gate_codes.shape
    steps, per_step = rows // STEP, STEP // QB
    own = slice(0, tokens.shape[0])
    gate, up = slice(0, units), slice(units, 2 * units)

    def copies(step):
        column = pl.multiple_of(node[0] * rows + step * STEP, 128)
        part = pl.ds(pl.multiple_of(step * STEP, 128), STEP)
        pairs = (
            (gate_codes.at[part, :], w_in.at[part, gate]),
            (up_codes.at[part, :], w_in.at[part, up]),
            (tokens.at[:, pl.ds(column, STEP)], all_tokens.at[own, part]),
            (down_codes.at[:, part], w_down.at[:, part]),
            (cot.at[:, pl.ds(column, STEP)], all_cots.at[own, part]),
        )
        return [pltpu.make_async_copy(a, b, sems.at[step, i]) for i, (a, b) in enumerate(pairs)]

    for step in range(steps):
        for copy in copies(step):
            copy.start()
    total[...] = jnp.zeros(total.shape, total.dtype)

    def scale(weights, index, factor):
        weights[index] = (weights[index].astype(jnp.float32) * factor).astype(weights.dtype)

    def one(step, carry):
        for copy in copies(step):
            copy.wait()
        first_scale = (node[0] * steps + step) * per_step
        for j in range(per_step):
            part = pl.ds(pl.multiple_of(step * STEP + j * QB, QB), QB)
            row = pl.ds(first_scale + j, 1)
            scale(w_in, (part, gate), gate_scales[row, :])
            scale(w_in, (part, up), up_scales[row, :])
            scale(w_down, (slice(None), part), down_scales[step, :, j : j + 1])
        part = pl.ds(pl.multiple_of(step * STEP, 128), STEP)
        total[:, : 2 * units] += jnp.dot(all_tokens[own, part], w_in[part, :], preferred_element_type=jnp.float32)
        total[:, 2 * units :] += against(all_cots[own, part], w_down[:, part])
        return carry

    lax.fori_loop(0, steps, one, 0)
    short[...] = total[...].astype(short.dtype)


def prepare(nodes, node, tokens, cot, gate_codes, up_codes, down_codes, gate_scales, up_scales, down_scales):
    rows, units = gate_codes.shape
    count = tokens.shape[0]
    steps, per_step = rows // STEP, STEP // QB
    scales = lax.dynamic_slice_in_dim(down_scales, node[0] * (rows // QB), rows // QB, 1)
    scales = scales.reshape(units, steps, per_step).transpose(1, 0, 2)
    codes = jnp.bfloat16
    return pl.pallas_call(
        prepare_kernel,
        in_specs=[IN_SMEM] + [IN_HBM] * 5 + [IN_VMEM] * 3,
        out_specs=[IN_VMEM] * 6,
        out_shape=[
            pltpu.VMEM((nodes * count, rows), codes),
            pltpu.VMEM((nodes * count, rows), codes),
            pltpu.VMEM((rows, 2 * units), codes),
            pltpu.VMEM((units, rows), codes),
            pltpu.VMEM((count, 3 * units), jnp.float32),
            pltpu.VMEM((count, 3 * units), codes),
        ],
        scratch_shapes=[pltpu.SemaphoreType.DMA((steps, 5))],
        compiler_params=grant(12),
        cost_estimate=cost(0),
        name="prepare",
    )(
        node, *(in_hbm(a) for a in (tokens, cot, gate_codes, up_codes, down_codes)),
        gate_scales, up_scales, scales,
    )


def join_kernel(group, far, place, held, given, w_in, w_down, *refs):
    tokens, cot, total, short = refs[-4:]
    half, rows = held.shape
    units = w_down.shape[0]
    side = side_of(place[0])
    natural = (1 - side if far else side) * half
    mine = pl.ds(pl.multiple_of(2 * group * half + natural, 16), half)
    out = pl.ds(pl.multiple_of(natural, 16), half)

    @pl.when((place[0] & 1) == 0)
    def _():
        tokens[mine, :] = held[...]
        cot[mine, :] = given[...]

    @pl.when((place[0] & 1) == 1)
    def _():
        tokens[mine, :] = given[...]
        cot[mine, :] = held[...]

    for step in range(rows // STEP):
        part = slice(step * STEP, (step + 1) * STEP)
        inner = jnp.dot(tokens[mine, part], w_in[part, :], preferred_element_type=jnp.float32)
        outer = against(cot[mine, part], w_down[:, part])
        if step == 0:
            total[out, : 2 * units] = inner
            total[out, 2 * units :] = outer
        else:
            total[out, : 2 * units] += inner
            total[out, 2 * units :] += outer
    short[...] = total[out, :].astype(short.dtype)


def join(group, far, place, held, given, w_in, w_down, before):
    half, rows = held.shape
    units = w_down.shape[0]
    return pl.pallas_call(
        functools.partial(join_kernel, group, far),
        in_specs=[IN_SMEM] + [IN_VMEM] * (4 + len(before)),
        out_specs=[IN_VMEM] * 4,
        out_shape=[
            pltpu.VMEM(before[0].shape, jnp.bfloat16),
            pltpu.VMEM(before[1].shape, jnp.bfloat16),
            pltpu.VMEM((2 * half, 3 * units), jnp.float32),
            pltpu.VMEM((half, 3 * units), jnp.bfloat16),
        ],
        input_output_aliases={5 + i: i for i in range(len(before))},
        compiler_params=grant(12),
        cost_estimate=cost(0),
        name="join",
    )(place, *(in_vmem(a) for a in (held, given, w_in, w_down, *before)))


def activate_kernel(group, turns, count, blocks, parked, place, weights, total, arrived, *refs):
    block = weights.shape[0] // blocks
    if parked:
        cots, sem = refs[-6 - blocks // 2], refs[-1]
        copy = pltpu.make_async_copy(cots, refs[-2], sem)
        copy.start()
        refs = refs[:-2]
    act, d_inner, _, *targets = refs[-3 - blocks // 2 :]
    units, half, chunk = act.shape[1], count // 2, 32
    side = side_of(place[0])

    def rows(first, length):
        return pl.ds(pl.multiple_of(first, 16), length)

    for turn in turns:
        natural = (1 - side if turn else side) * half
        for start in range(0, half, chunk):
            def of(array):
                return rows((natural if array.shape[0] == count else 0) + start, chunk)

            sums = total[of(total), :] + arrived[of(arrived), :].astype(jnp.float32)
            gate, upper, d_act = sums[:, :units], sums[:, units : 2 * units], sums[:, 2 * units :]
            sig = jax.nn.sigmoid(gate)
            silu_val = gate * sig
            kept = rows(group * count + natural + start, chunk)
            act[kept, :] = (silu_val * upper).astype(act.dtype)
            d_inner[kept, :units] = (d_act * upper * sig * (1.0 + gate * (1.0 - sig))).astype(d_inner.dtype)
            d_inner[kept, units:] = (d_act * silu_val).astype(d_inner.dtype)
    def block_rows(relative):
        bits = blocks.bit_length() - 1
        owner = 0
        for bit in range(bits):
            own = (place[0] >> bit) & 1
            owner += (own if (relative >> (bits - 1 - bit)) & 1 else 1 - own) << bit
        return weights[rows(owner * block, block), :]

    def store(h, mine):
        for p, target in enumerate(targets):
            pieces, places, width = [], [], 0
            for i in (0, 1):
                pad = ((2 * i + h) * block - width) % 128
                if pad:
                    pieces.append(weights[:pad, :])
                pieces.append(block_rows(2 * p + i))
                places.append(width + pad)
                width += pad + block
            product = against(mine, jnp.concatenate(pieces))
            for i in (0, 1):
                lanes = slice((2 * i + h) * block, (2 * i + h + 1) * block)
                target[:, lanes] = product[:, places[i] : places[i] + block].astype(target.dtype)

    if len(turns) == 2:
        for p, target in enumerate(targets):
            both = jnp.concatenate([block_rows(2 * p), block_rows(2 * p + 1)])
            product = against(d_inner[rows(group * count, count), :], both)
            for n in range(4):
                i, h = n // 2, n % 2
                value = product[h * half : (h + 1) * half, i * block : (i + 1) * block]
                target[:, n * block : (n + 1) * block] = value.astype(target.dtype)
    else:
        for h in (0, 1):
            pl.when(natural == h * half)(lambda: store(h, d_inner[rows(group * count + h * half, half), :]))
    if parked:
        copy.wait()


def activate(group, groups, turns, place, total, arrived, weights, blocks, before, park=()):
    units, pairs = weights.shape[1] // 2, blocks // 2
    block = weights.shape[0] // blocks
    count = arrived.shape[0] * (3 - len(turns))
    terms = count // 2, 4 * block
    return pl.pallas_call(
        functools.partial(activate_kernel, group, turns, count, blocks, len(park)),
        in_specs=[IN_SMEM] + [IN_VMEM] * (3 + len(before) + len(park)),
        out_specs=[IN_VMEM] * (3 + pairs) + [IN_HBM] * len(park),
        out_shape=[
            pltpu.VMEM((groups * count, units), jnp.bfloat16),
            pltpu.VMEM((groups * count, 2 * units), jnp.bfloat16),
            pltpu.VMEM((groups * count, weights.shape[0]), jnp.bfloat16),
        ]
        + [pltpu.VMEM(terms, jnp.bfloat16)] * (pairs // 2)
        + [pltpu.VMEM(terms, jnp.float32)] * (pairs // 2)
        + [pltpu.HBM(array.shape, array.dtype) for array in park],
        scratch_shapes=[pltpu.SemaphoreType.DMA] * len(park),
        input_output_aliases={4 + i: max(3 - len(before), 0) + i for i in range(len(before))},
        compiler_params=grant(12),
        cost_estimate=cost(0),
        name="activate",
    )(place, *(in_vmem(a) for a in (weights, total, arrived, *before, *park)))


def inner_grads_kernel(tokens, d_inner, gate_grad, up_grad, gate_held, up_held, sems):
    rows, units = gate_grad.shape
    steps = rows // STEP
    copies = []
    for step in range(steps):
        part = slice(step * STEP, (step + 1) * STEP)
        both = contract(tokens[:, part], d_inner[...])
        gate_held[part, :] = both[:, :units].astype(gate_held.dtype)
        up_held[part, :] = both[:, units:].astype(up_held.dtype)
        for i, (held, target) in enumerate(((gate_held, gate_grad), (up_held, up_grad))):
            copies.append(pltpu.make_async_copy(held.at[part, :], target.at[part, :], sems.at[2 * step + i]))
            copies[-1].start()
    for copy in copies:
        copy.wait()


def inner_grads(tokens, d_inner):
    rows, units = tokens.shape[1], d_inner.shape[1] // 2
    return pl.pallas_call(
        inner_grads_kernel,
        in_specs=[IN_VMEM] * 2,
        out_specs=[IN_HBM] * 2,
        out_shape=[pltpu.HBM((rows, units), jnp.bfloat16)] * 2,
        scratch_shapes=[pltpu.VMEM((rows, units), jnp.bfloat16)] * 2
        + [pltpu.SemaphoreType.DMA((2 * (rows // STEP),))],
        compiler_params=grant(12),
        cost_estimate=cost(0),
        name="inner_grads",
    )(in_vmem(tokens), in_vmem(d_inner))


def down_grads_kernel(cots, act, down_grad, cot, held, in_sems, out_sems):
    steps = cots.shape[1] // STEP
    parts = [slice(step * STEP, (step + 1) * STEP) for step in range(steps)]
    arriving = [
        pltpu.make_async_copy(cots.at[:, part], cot.at[:, part], in_sems.at[step]) for step, part in enumerate(parts)
    ]
    leaving = [
        pltpu.make_async_copy(held.at[:, part], down_grad.at[:, part], out_sems.at[step])
        for step, part in enumerate(parts)
    ]
    for copy in arriving:
        copy.start()
    for step, part in enumerate(parts):
        arriving[step].wait()
        held[:, part] = contract(act[...], cot[:, part]).astype(held.dtype)
        leaving[step].start()
    for copy in leaving:
        copy.wait()


def down_grads(cots, act):
    shape = act.shape[1], cots.shape[1]
    sems = pltpu.SemaphoreType.DMA((shape[1] // STEP,))
    return pl.pallas_call(
        down_grads_kernel,
        in_specs=[IN_HBM, IN_VMEM],
        out_specs=IN_HBM,
        out_shape=pltpu.HBM(shape, jnp.bfloat16),
        scratch_shapes=[pltpu.VMEM(cots.shape, cots.dtype), pltpu.VMEM(shape, jnp.bfloat16), sems, sems],
        compiler_params=grant(12),
        cost_estimate=cost(0),
        name="down_grads",
    )(in_hbm(cots), in_vmem(act))


def after(value, *earlier):
    return lax.optimization_barrier((value, earlier))[0]


def body(tokens, cotangent, gate_codes, up_codes, down_codes, gate_scales, up_scales, down_scales):
    nodes, width = lax.axis_size("node"), lax.axis_size("dp")
    node, place = lax.axis_index("node"), lax.axis_index("dp")
    node_ref, place_ref = node.reshape(1), place.reshape(1)
    rows, units = gate_codes.shape
    count = tokens.shape[0]
    owners = width // nodes
    bits = owners.bit_length() - 1
    block = rows // owners

    side, half = side_of(place), count // 2

    def halves(array):
        return [lax.dynamic_slice_in_dim(array, s * half, half, 0) for s in (side, 1 - side)]

    fetched = [
        swap(fetch(k, node_ref, place_ref, tokens, cotangent, (half, rows)), "node", nodes, k)
        for k in range(1, nodes)
    ]
    all_tokens, all_cots, w_in, w_down, own_sums, own_short = prepare(
        nodes, node_ref, tokens, cotangent, gate_codes, up_codes, down_codes, gate_scales, up_scales, down_scales
    )
    fetched = after(fetched, own_short)

    sums, shorts = [own_sums], [None]
    for k, mine in enumerate(fetched, 1):
        given = swap(mine, "dp", width, 1)
        beside = swap(mine, "dp", width, 1 << SIDE_BIT)
        before, near_far = [all_tokens, all_cots], []
        for far, held in enumerate((mine, beside)):
            if far:
                held = after(held, near_far)
                given = swap(held, "dp", width, 1)
            *before, short = join(k, far, place_ref, held, given, w_in, w_down, before)
            near_far.append(short)
        all_tokens, all_cots, total = before
        sums.append(total)
        shorts.append(near_far)

    mask = 1
    if nodes > 2:
        while mask < nodes // 2:
            sent = [swap(s.astype(jnp.bfloat16), "node", nodes, mask) for s in sums]
            sums = [s + sent[k ^ mask].astype(jnp.float32) for k, s in enumerate(sums)]
            mask *= 2
        own_short = sums[0].astype(jnp.bfloat16)
        shorts = [halves(s.astype(jnp.bfloat16)) for s in sums]
    near_far = [swap(s, "node", nodes, mask) for s in shorts[mask]]
    arrived = [None]
    for k in range(1, nodes):
        short = own_short if k == mask else sums[k ^ mask].astype(jnp.bfloat16)
        arrived.append(swap(short, "node", nodes, mask))

    peers = owners // 2

    def passed(results):
        return *results[:3], results[3:]

    def split(parts, *earlier):
        size = len(parts) // 2
        got = [swap(part, "dp", width, 1) for part in parts[:size]]
        if earlier:
            got = after(got, *earlier)
        sending = []
        for r in range(peers):
            lanes = slice(r % 2 * 2 * block, (r % 2 + 1) * 2 * block)
            both = parts[size + r // 2][:, lanes] + got[r // 2][:, lanes].astype(jnp.float32)
            if r < peers - 1:
                mask = sum(1 << bit for bit in range(1, bits) if (r >> (bits - 1 - bit)) & 1 == 0)
                sending.append((mask, both.astype(jnp.bfloat16)))
        return sending, both

    def exchange(sending):
        return [swap(value, "dp", width, mask) for mask, value in sending]

    def add(mine, got):
        for value in got:
            mine += value.astype(jnp.float32)
        return mine

    blocks, before, others = [None] * nodes, [all_tokens], [None] * nodes
    for k in reversed(range(1, nodes)):
        park = [all_cots] if k == 1 else []
        *before, others[k] = passed(
            activate(k, nodes, (0, 1), place_ref, sums[k], arrived[k], w_in, owners, before, park)
        )
    *others[1], all_cots = others[1]
    *before, parts = passed(activate(0, nodes, (0,), place_ref, sums[0], near_far[0], w_in, owners, before))
    last = []
    for k in range(1, nodes):
        sending, mine = split(others[k], before[:2])
        last.append([value for _, value in sending])
        blocks[k] = mine, exchange(sending)
    act, d_inner, all_tokens, parts = passed(
        activate(0, nodes, (1,), place_ref, sums[0], after(near_far[1], last), w_in, owners, [*before, *parts])
    )
    sending, mine = split(parts)
    sent, mine = lax.optimization_barrier(([value for _, value in sending], mine))
    got = exchange([(mask, value) for (mask, _), value in zip(sending, sent)])
    for k in range(1, nodes):
        value = add(*blocks[k]).astype(jnp.bfloat16)
        act, sent, value = lax.optimization_barrier((act, sent, value))
        blocks[k] = swap(value, "node", nodes, k).astype(jnp.float32)
    gate_grad, up_grad = inner_grads(all_tokens, after(d_inner, sent, value))
    blocks[0] = add(mine, after(got, gate_grad))
    high = place // owners

    def block_for(owner):
        chosen = blocks[0]
        for k in range(1, nodes):
            chosen = jnp.where((owner ^ node) == k, blocks[k], chosen)
        return chosen

    token_grad = block_for(high)
    sent = [block_for(high ^ j).astype(jnp.bfloat16) for j in range(1, nodes)]
    token_grad, sent = lax.optimization_barrier((token_grad, sent))
    down_grad = down_grads(all_cots, after(act, sent))
    for j in range(1, nodes):
        arrived = after(swap(sent[j - 1], "dp", width, j * owners), down_grad)
        token_grad += arrived.astype(jnp.float32)
    token_grad = token_grad.astype(jnp.bfloat16)
    token_grad = jnp.concatenate([token_grad[:, :block], token_grad[:, block:]])
    return token_grad, gate_grad, up_grad, down_grad


def solution(mesh):
    return jax.shard_map(
        body,
        mesh=mesh,
        in_specs=(
            P("node", None),
            P("node", None),
            P("node", "dp"),
            P("node", "dp"),
            P("dp", "node"),
            P(None, "dp"),
            P(None, "dp"),
            P("dp", None),
        ),
        out_specs=(P("node", "dp"), P("node", "dp"), P("node", "dp"), P("dp", "node")),
        check_vma=False,
    )
```

```python
import functools

import jax
import jax.numpy as jnp
from jax import lax
from jax.experimental import pallas as pl
from jax.experimental.pallas import tpu as pltpu
from jax.sharding import PartitionSpec as P

QB = 128
STEP = 640
SIDE_BIT = 2
IN_HBM = pl.BlockSpec(memory_space=pltpu.HBM)
IN_VMEM = pl.BlockSpec(memory_space=pltpu.VMEM)
IN_SMEM = pl.BlockSpec(memory_space=pltpu.SMEM)


def contract(left, right):
    return lax.dot_general(
        left, right, (((0,), (0,)), ((), ())), preferred_element_type=jnp.float32
    )


def against(left, right):
    return lax.dot_general(
        left, right, (((1,), (1,)), ((), ())), preferred_element_type=jnp.float32
    )


def flipped(size, mask):
    return [(i, i ^ mask) for i in range(size)]


def swap(value, axis, size, mask):
    return lax.ppermute(value, axis, flipped(size, mask))


def in_hbm(array):
    return pltpu.with_memory_space_constraint(array, pltpu.HBM)


def in_vmem(array):
    return pltpu.with_memory_space_constraint(array, pltpu.VMEM)


def cost(operations):
    return pl.CostEstimate(flops=operations, transcendentals=0, bytes_accessed=0)


def grant(mebibytes):
    return pltpu.CompilerParams(vmem_limit_bytes=mebibytes * 1024 * 1024)


def side_of(place):
    return (place >> SIDE_BIT) & 1


def fetch_kernel(mask, node, place, tokens, cot, target, sem):
    half, rows = target.shape
    start = pl.multiple_of(side_of(place[0]) * half, 16)
    column = pl.multiple_of((node[0] ^ mask) * rows, 128)
    part = (pl.ds(start, half), pl.ds(column, rows))

    @pl.when((place[0] & 1) == 0)
    def _():
        copy = pltpu.make_async_copy(tokens.at[part], target, sem)
        copy.start()
        copy.wait()

    @pl.when((place[0] & 1) == 1)
    def _():
        copy = pltpu.make_async_copy(cot.at[part], target, sem)
        copy.start()
        copy.wait()


def fetch(mask, node, place, tokens, cot, shape):
    return pl.pallas_call(
        functools.partial(fetch_kernel, mask),
        in_specs=[IN_SMEM, IN_SMEM, IN_HBM, IN_HBM],
        out_specs=IN_VMEM,
        out_shape=pltpu.VMEM(shape, tokens.dtype),
        scratch_shapes=[pltpu.SemaphoreType.DMA],
        compiler_params=grant(12),
        cost_estimate=cost(0),
        name="fetch",
    )(node, place, in_hbm(tokens), in_hbm(cot))


def prepare_kernel(
    node, tokens, cot, gate_codes, up_codes, down_codes, gate_scales, up_scales, down_scales,
    all_tokens, all_cots, w_in, w_down, total, short, sems,
):
    rows, units = gate_codes.shape
    steps, per_step = rows // STEP, STEP // QB
    own = slice(0, tokens.shape[0])
    gate, up = slice(0, units), slice(units, 2 * units)

    def copies(step):
        column = pl.multiple_of(node[0] * rows + step * STEP, 128)
        part = pl.ds(pl.multiple_of(step * STEP, 128), STEP)
        pairs = (
            (gate_codes.at[part, :], w_in.at[part, gate]),
            (up_codes.at[part, :], w_in.at[part, up]),
            (tokens.at[:, pl.ds(column, STEP)], all_tokens.at[own, part]),
            (down_codes.at[:, part], w_down.at[:, part]),
            (cot.at[:, pl.ds(column, STEP)], all_cots.at[own, part]),
        )
        return [pltpu.make_async_copy(a, b, sems.at[step, i]) for i, (a, b) in enumerate(pairs)]

    for step in range(steps):
        for copy in copies(step):
            copy.start()
    total[...] = jnp.zeros(total.shape, total.dtype)

    def scale(weights, index, factor):
        weights[index] = (weights[index].astype(jnp.float32) * factor).astype(weights.dtype)

    def one(step, carry):
        for copy in copies(step):
            copy.wait()
        first_scale = (node[0] * steps + step) * per_step
        for j in range(per_step):
            part = pl.ds(pl.multiple_of(step * STEP + j * QB, QB), QB)
            row = pl.ds(first_scale + j, 1)
            scale(w_in, (part, gate), gate_scales[row, :])
            scale(w_in, (part, up), up_scales[row, :])
            scale(w_down, (slice(None), part), down_scales[step, :, j : j + 1])
        part = pl.ds(pl.multiple_of(step * STEP, 128), STEP)
        total[:, : 2 * units] += jnp.dot(all_tokens[own, part], w_in[part, :], preferred_element_type=jnp.float32)
        total[:, 2 * units :] += against(all_cots[own, part], w_down[:, part])
        return carry

    lax.fori_loop(0, steps, one, 0)
    short[...] = total[...].astype(short.dtype)


def prepare(nodes, node, tokens, cot, gate_codes, up_codes, down_codes, gate_scales, up_scales, down_scales):
    rows, units = gate_codes.shape
    count = tokens.shape[0]
    steps, per_step = rows // STEP, STEP // QB
    scales = lax.dynamic_slice_in_dim(down_scales, node[0] * (rows // QB), rows // QB, 1)
    scales = scales.reshape(units, steps, per_step).transpose(1, 0, 2)
    codes = jnp.bfloat16
    return pl.pallas_call(
        prepare_kernel,
        in_specs=[IN_SMEM] + [IN_HBM] * 5 + [IN_VMEM] * 3,
        out_specs=[IN_VMEM] * 6,
        out_shape=[
            pltpu.VMEM((nodes * count, rows), codes),
            pltpu.VMEM((nodes * count, rows), codes),
            pltpu.VMEM((rows, 2 * units), codes),
            pltpu.VMEM((units, rows), codes),
            pltpu.VMEM((count, 3 * units), jnp.float32),
            pltpu.VMEM((count, 3 * units), codes),
        ],
        scratch_shapes=[pltpu.SemaphoreType.DMA((steps, 5))],
        compiler_params=grant(12),
        cost_estimate=cost(0),
        name="prepare",
    )(
        node, *(in_hbm(a) for a in (tokens, cot, gate_codes, up_codes, down_codes)),
        gate_scales, up_scales, scales,
    )


def join_kernel(group, far, place, held, given, w_in, w_down, *refs):
    tokens, cot, total, short = refs[-4:]
    half, rows = held.shape
    units = w_down.shape[0]
    side = side_of(place[0])
    natural = (1 - side if far else side) * half
    mine = pl.ds(pl.multiple_of(2 * group * half + natural, 16), half)
    out = pl.ds(pl.multiple_of(natural, 16), half)

    @pl.when((place[0] & 1) == 0)
    def _():
        tokens[mine, :] = held[...]
        cot[mine, :] = given[...]

    @pl.when((place[0] & 1) == 1)
    def _():
        tokens[mine, :] = given[...]
        cot[mine, :] = held[...]

    for step in range(rows // STEP):
        part = slice(step * STEP, (step + 1) * STEP)
        inner = jnp.dot(tokens[mine, part], w_in[part, :], preferred_element_type=jnp.float32)
        outer = against(cot[mine, part], w_down[:, part])
        if step == 0:
            total[out, : 2 * units] = inner
            total[out, 2 * units :] = outer
        else:
            total[out, : 2 * units] += inner
            total[out, 2 * units :] += outer
    short[...] = total[out, :].astype(short.dtype)


def join(group, far, place, held, given, w_in, w_down, before):
    half, rows = held.shape
    units = w_down.shape[0]
    return pl.pallas_call(
        functools.partial(join_kernel, group, far),
        in_specs=[IN_SMEM] + [IN_VMEM] * (4 + len(before)),
        out_specs=[IN_VMEM] * 4,
        out_shape=[
            pltpu.VMEM(before[0].shape, jnp.bfloat16),
            pltpu.VMEM(before[1].shape, jnp.bfloat16),
            pltpu.VMEM((2 * half, 3 * units), jnp.float32),
            pltpu.VMEM((half, 3 * units), jnp.bfloat16),
        ],
        input_output_aliases={5 + i: i for i in range(len(before))},
        compiler_params=grant(12),
        cost_estimate=cost(0),
        name="join",
    )(place, *(in_vmem(a) for a in (held, given, w_in, w_down, *before)))


def activate_kernel(group, turns, count, blocks, parked, place, weights, total, arrived, *refs):
    block = weights.shape[0] // blocks
    if parked:
        cots, sem = refs[-6 - blocks // 2], refs[-1]
        copy = pltpu.make_async_copy(cots, refs[-2], sem)
        copy.start()
        refs = refs[:-2]
    act, d_inner, _, *targets = refs[-3 - blocks // 2 :]
    units, half, chunk = act.shape[1], count // 2, 32
    side = side_of(place[0])

    def rows(first, length):
        return pl.ds(pl.multiple_of(first, 16), length)

    for turn in turns:
        natural = (1 - side if turn else side) * half
        for start in range(0, half, chunk):
            def of(array):
                return rows((natural if array.shape[0] == count else 0) + start, chunk)

            sums = total[of(total), :] + arrived[of(arrived), :].astype(jnp.float32)
            gate, upper, d_act = sums[:, :units], sums[:, units : 2 * units], sums[:, 2 * units :]
            sig = jax.nn.sigmoid(gate)
            silu_val = gate * sig
            kept = rows(group * count + natural + start, chunk)
            act[kept, :] = (silu_val * upper).astype(act.dtype)
            d_inner[kept, :units] = (d_act * upper * sig * (1.0 + gate * (1.0 - sig))).astype(d_inner.dtype)
            d_inner[kept, units:] = (d_act * silu_val).astype(d_inner.dtype)
    def block_rows(relative):
        bits = blocks.bit_length() - 1
        owner = 0
        for bit in range(bits):
            own = (place[0] >> bit) & 1
            owner += (own if (relative >> (bits - 1 - bit)) & 1 else 1 - own) << bit
        return weights[rows(owner * block, block), :]

    def store(h, mine):
        for p, target in enumerate(targets):
            pieces, places, width = [], [], 0
            for i in (0, 1):
                pad = ((2 * i + h) * block - width) % 128
                if pad:
                    pieces.append(weights[:pad, :])
                pieces.append(block_rows(2 * p + i))
                places.append(width + pad)
                width += pad + block
            product = against(mine, jnp.concatenate(pieces))
            for i in (0, 1):
                lanes = slice((2 * i + h) * block, (2 * i + h + 1) * block)
                target[:, lanes] = product[:, places[i] : places[i] + block].astype(target.dtype)

    if len(turns) == 2:
        for p, target in enumerate(targets):
            both = jnp.concatenate([block_rows(2 * p), block_rows(2 * p + 1)])
            product = against(d_inner[rows(group * count, count), :], both)
            for n in range(4):
                i, h = n // 2, n % 2
                value = product[h * half : (h + 1) * half, i * block : (i + 1) * block]
                target[:, n * block : (n + 1) * block] = value.astype(target.dtype)
    else:
        for h in (0, 1):
            pl.when(natural == h * half)(lambda: store(h, d_inner[rows(group * count + h * half, half), :]))
    if parked:
        copy.wait()


def activate(group, groups, turns, place, total, arrived, weights, blocks, before, park=()):
    units, pairs = weights.shape[1] // 2, blocks // 2
    block = weights.shape[0] // blocks
    count = arrived.shape[0] * (3 - len(turns))
    terms = count // 2, 4 * block
    return pl.pallas_call(
        functools.partial(activate_kernel, group, turns, count, blocks, len(park)),
        in_specs=[IN_SMEM] + [IN_VMEM] * (3 + len(before) + len(park)),
        out_specs=[IN_VMEM] * (3 + pairs) + [IN_HBM] * len(park),
        out_shape=[
            pltpu.VMEM((groups * count, units), jnp.bfloat16),
            pltpu.VMEM((groups * count, 2 * units), jnp.bfloat16),
            pltpu.VMEM((groups * count, weights.shape[0]), jnp.bfloat16),
        ]
        + [pltpu.VMEM(terms, jnp.bfloat16)] * (pairs // 2)
        + [pltpu.VMEM(terms, jnp.float32)] * (pairs // 2)
        + [pltpu.HBM(array.shape, array.dtype) for array in park],
        scratch_shapes=[pltpu.SemaphoreType.DMA] * len(park),
        input_output_aliases={4 + i: max(3 - len(before), 0) + i for i in range(len(before))},
        compiler_params=grant(12),
        cost_estimate=cost(0),
        name="activate",
    )(place, *(in_vmem(a) for a in (weights, total, arrived, *before, *park)))


def inner_grads_kernel(tokens, d_inner, gate_grad, up_grad, gate_held, up_held, sems):
    rows, units = gate_grad.shape
    steps = rows // STEP
    copies = []
    for step in range(steps):
        part = slice(step * STEP, (step + 1) * STEP)
        both = contract(tokens[:, part], d_inner[...])
        gate_held[part, :] = both[:, :units].astype(gate_held.dtype)
        up_held[part, :] = both[:, units:].astype(up_held.dtype)
        for i, (held, target) in enumerate(((gate_held, gate_grad), (up_held, up_grad))):
            copies.append(pltpu.make_async_copy(held.at[part, :], target.at[part, :], sems.at[2 * step + i]))
            copies[-1].start()
    for copy in copies:
        copy.wait()


def inner_grads(tokens, d_inner):
    rows, units = tokens.shape[1], d_inner.shape[1] // 2
    return pl.pallas_call(
        inner_grads_kernel,
        in_specs=[IN_VMEM] * 2,
        out_specs=[IN_HBM] * 2,
        out_shape=[pltpu.HBM((rows, units), jnp.bfloat16)] * 2,
        scratch_shapes=[pltpu.VMEM((rows, units), jnp.bfloat16)] * 2
        + [pltpu.SemaphoreType.DMA((2 * (rows // STEP),))],
        compiler_params=grant(12),
        cost_estimate=cost(0),
        name="inner_grads",
    )(in_vmem(tokens), in_vmem(d_inner))


def down_grads_kernel(cots, act, down_grad, cot, held, in_sems, out_sems):
    steps = cots.shape[1] // STEP
    parts = [slice(step * STEP, (step + 1) * STEP) for step in range(steps)]
    arriving = [
        pltpu.make_async_copy(cots.at[:, part], cot.at[:, part], in_sems.at[step]) for step, part in enumerate(parts)
    ]
    leaving = [
        pltpu.make_async_copy(held.at[:, part], down_grad.at[:, part], out_sems.at[step])
        for step, part in enumerate(parts)
    ]
    for copy in arriving:
        copy.start()
    for step, part in enumerate(parts):
        arriving[step].wait()
        held[:, part] = contract(act[...], cot[:, part]).astype(held.dtype)
        leaving[step].start()
    for copy in leaving:
        copy.wait()


def down_grads(cots, act):
    shape = act.shape[1], cots.shape[1]
    sems = pltpu.SemaphoreType.DMA((shape[1] // STEP,))
    return pl.pallas_call(
        down_grads_kernel,
        in_specs=[IN_HBM, IN_VMEM],
        out_specs=IN_HBM,
        out_shape=pltpu.HBM(shape, jnp.bfloat16),
        scratch_shapes=[pltpu.VMEM(cots.shape, cots.dtype), pltpu.VMEM(shape, jnp.bfloat16), sems, sems],
        compiler_params=grant(12),
        cost_estimate=cost(0),
        name="down_grads",
    )(in_hbm(cots), in_vmem(act))


def after(value, *earlier):
    return lax.optimization_barrier((value, earlier))[0]


def body(tokens, cotangent, gate_codes, up_codes, down_codes, gate_scales, up_scales, down_scales):
    nodes, width = lax.axis_size("node"), lax.axis_size("dp")
    node, place = lax.axis_index("node"), lax.axis_index("dp")
    node_ref, place_ref = node.reshape(1), place.reshape(1)
    rows, units = gate_codes.shape
    count = tokens.shape[0]
    owners = width // nodes
    bits = owners.bit_length() - 1
    block = rows // owners

    side, half = side_of(place), count // 2

    def halves(array):
        return [lax.dynamic_slice_in_dim(array, s * half, half, 0) for s in (side, 1 - side)]

    fetched = [
        swap(fetch(k, node_ref, place_ref, tokens, cotangent, (half, rows)), "node", nodes, k)
        for k in range(1, nodes)
    ]
    all_tokens, all_cots, w_in, w_down, own_sums, own_short = prepare(
        nodes, node_ref, tokens, cotangent, gate_codes, up_codes, down_codes, gate_scales, up_scales, down_scales
    )
    fetched = after(fetched, own_short)

    sums, shorts = [own_sums], [None]
    for k, mine in enumerate(fetched, 1):
        given = swap(mine, "dp", width, 1)
        beside = swap(mine, "dp", width, 1 << SIDE_BIT)
        before, near_far = [all_tokens, all_cots], []
        for far, held in enumerate((mine, beside)):
            if far:
                held = after(held, near_far)
                given = swap(held, "dp", width, 1)
            *before, short = join(k, far, place_ref, held, given, w_in, w_down, before)
            near_far.append(short)
        all_tokens, all_cots, total = before
        sums.append(total)
        shorts.append(near_far)

    mask = 1
    if nodes > 2:
        while mask < nodes // 2:
            sent = [swap(s.astype(jnp.bfloat16), "node", nodes, mask) for s in sums]
            sums = [s + sent[k ^ mask].astype(jnp.float32) for k, s in enumerate(sums)]
            mask *= 2
        own_short = sums[0].astype(jnp.bfloat16)
        shorts = [halves(s.astype(jnp.bfloat16)) for s in sums]
    near_far = [swap(s, "node", nodes, mask) for s in shorts[mask]]
    arrived = [None]
    for k in range(1, nodes):
        short = own_short if k == mask else sums[k ^ mask].astype(jnp.bfloat16)
        arrived.append(swap(short, "node", nodes, mask))

    peers = owners // 2

    def passed(results):
        return *results[:3], results[3:]

    def split(parts, *earlier):
        size = len(parts) // 2
        got = [swap(part, "dp", width, 1) for part in parts[:size]]
        if earlier:
            got = after(got, *earlier)
        sending = []
        for r in range(peers):
            lanes = slice(r % 2 * 2 * block, (r % 2 + 1) * 2 * block)
            both = parts[size + r // 2][:, lanes] + got[r // 2][:, lanes].astype(jnp.float32)
            if r < peers - 1:
                mask = sum(1 << bit for bit in range(1, bits) if (r >> (bits - 1 - bit)) & 1 == 0)
                sending.append((mask, both.astype(jnp.bfloat16)))
        return sending, both

    def exchange(sending):
        return [swap(value, "dp", width, mask) for mask, value in sending]

    def add(mine, got):
        for value in got:
            mine += value.astype(jnp.float32)
        return mine

    blocks, before, others = [None] * nodes, [all_tokens], [None] * nodes
    for k in reversed(range(1, nodes)):
        park = [all_cots] if k == 1 else []
        *before, others[k] = passed(
            activate(k, nodes, (0, 1), place_ref, sums[k], arrived[k], w_in, owners, before, park)
        )
    *others[1], all_cots = others[1]
    *before, parts = passed(activate(0, nodes, (0,), place_ref, sums[0], near_far[0], w_in, owners, before))
    last = []
    for k in range(1, nodes):
        sending, mine = split(others[k], near_far[0])
        last.append([value for _, value in sending])
        blocks[k] = mine, exchange(sending)
    act, d_inner, all_tokens, parts = passed(
        activate(0, nodes, (1,), place_ref, sums[0], after(near_far[1], last), w_in, owners, [*before, *parts])
    )
    sending, mine = split(parts)
    sent, mine = lax.optimization_barrier(([value for _, value in sending], mine))
    got = exchange([(mask, value) for (mask, _), value in zip(sending, sent)])
    for k in range(1, nodes):
        value = add(*blocks[k]).astype(jnp.bfloat16)
        act, sent, value = lax.optimization_barrier((act, sent, value))
        blocks[k] = swap(value, "node", nodes, k).astype(jnp.float32)
    gate_grad, up_grad = inner_grads(all_tokens, after(d_inner, sent, value))
    blocks[0] = add(mine, after(got, gate_grad))
    high = place // owners

    def block_for(owner):
        chosen = blocks[0]
        for k in range(1, nodes):
            chosen = jnp.where((owner ^ node) == k, blocks[k], chosen)
        return chosen

    token_grad = block_for(high)
    sent = [block_for(high ^ j).astype(jnp.bfloat16) for j in range(1, nodes)]
    token_grad, sent = lax.optimization_barrier((token_grad, sent))
    down_grad = down_grads(all_cots, after(act, sent))
    for j in range(1, nodes):
        arrived = after(swap(sent[j - 1], "dp", width, j * owners), down_grad)
        token_grad += arrived.astype(jnp.float32)
    token_grad = token_grad.astype(jnp.bfloat16)
    token_grad = jnp.concatenate([token_grad[:, :block], token_grad[:, block:]])
    return token_grad, gate_grad, up_grad, down_grad


def solution(mesh):
    return jax.shard_map(
        body,
        mesh=mesh,
        in_specs=(
            P("node", None),
            P("node", None),
            P("node", "dp"),
            P("node", "dp"),
            P("dp", "node"),
            P(None, "dp"),
            P(None, "dp"),
            P("dp", None),
        ),
        out_specs=(P("node", "dp"), P("node", "dp"), P("node", "dp"), P("dp", "node")),
        check_vma=False,
    )
```
